32 devices in a mesh: irrep: 4 (over y, x), edge: 8 (over z, core).
Axes of the slice: x: 2, y: 2, z: 4, core: 2. Of those that a mesh axis runs over, the one named last changes fastest.
Arguments:
- edge_vec: float32 [3, 16384], P(None, ('irrep', 'edge')), may hold values from -4.8 to 4.8, as said below
- edge_live: int32 [16384], P(('irrep', 'edge')), may hold values from 0 to 1, as said below
- source: int32 [16384], P(('irrep', 'edge')), may hold values from 0 to 511
- target: int32 [16384], P(('irrep', 'edge')), may hold values from 0 to 511
- species: int32 [512], replicated, may hold values from 0 to 3
- force_label: float32 [3, 512], P(None, ('irrep', 'edge')), may hold values from -6 to 6
- force_mask: int32 [512], P(('irrep', 'edge')), may hold values 0 or 1
- block_owner: int32 [256], replicated, may hold values from 0 to 255, each once
- pair_in_weight: float32 [16, 1024], replicated, may hold values from -1.5 to 1.5
- pair_in_first: float32 [16, 1024], replicated, may hold values from -0.00061035156 to 0.00061035156
- pair_in_second: float32 [16, 1024], replicated, may hold values from 1e-08 to 4e-08
- pair_out_weight: float32 [1024, 1024], replicated, may hold values from -0.1875 to 0.1875
- pair_out_first: float32 [1024, 1024], replicated, may hold values from -0.00061035156 to 0.00061035156
- pair_out_second: float32 [1024, 1024], replicated, may hold values from 1e-08 to 4e-08
- env_weight: float32 [2, 64, 1024], replicated, may hold values from -0.1875 to 0.1875
- env_first: float32 [2, 64, 1024], replicated, may hold values from -0.00061035156 to 0.00061035156
- env_second: float32 [2, 64, 1024], replicated, may hold values from 1e-08 to 4e-08
- scalar_weight: float32 [2, 64, 1024], replicated, may hold values from -0.75 to 0.75
- scalar_first: float32 [2, 64, 1024], replicated, may hold values from -0.00061035156 to 0.00061035156
- scalar_second: float32 [2, 64, 1024], replicated, may hold values from 1e-08 to 4e-08
- mix_weight: float32 [1, 3, 64, 64], replicated, may hold values from -0.75 to 0.75
- mix_first: float32 [1, 3, 64, 64], replicated, may hold values from -0.00061035156 to 0.00061035156
- mix_second: float32 [1, 3, 64, 64], replicated, may hold values from 1e-08 to 4e-08
- energy_head: float32 [1028], replicated, may hold values from -1 to 2, as said below
- head_first: float32 [1028], replicated, may hold values from -0.00061035156 to 0.00061035156
- head_second: float32 [1028], replicated, may hold values from 1e-08 to 4e-08
- soap_weight: float32 [256, 128, 128], P(('irrep', 'edge')), may hold values from -0.1875 to 0.1875
- soap_first: float32 [256, 128, 128], P(('irrep', 'edge')), may hold values from -0.00061035156 to 0.00061035156
- soap_second: float32 [256, 128, 128], P(('irrep', 'edge')), may hold values from 1e-08 to 4e-08
- soap_left: float32 [256, 128, 128], P(('irrep', 'edge')), may hold values from -1 to 1, as said below
- soap_right: float32 [256, 128, 128], P(('irrep', 'edge')), may hold values from -1 to 1, as said below
- soap_lstat: float32 [256, 128, 128], P(('irrep', 'edge')), may hold values from -1 to 1, as said below
- soap_rstat: float32 [256, 128, 128], P(('irrep', 'edge')), may hold values from -1 to 1, as said below
- soap_average: float32 [256, 128, 128], P(('irrep', 'edge')), may hold values from -0.1875 to 0.1875
Outputs:
- loss_sum: float32 [], replicated
- label_count: float32 [], replicated
- new_pair_in_weight: float32 [16, 1024], replicated
- new_pair_in_first: float32 [16, 1024], replicated
- new_pair_in_second: float32 [16, 1024], replicated
- new_pair_out_weight: float32 [1024, 1024], replicated
- new_pair_out_first: float32 [1024, 1024], replicated
- new_pair_out_second: float32 [1024, 1024], replicated
- new_env_weight: float32 [2, 64, 1024], replicated
- new_env_first: float32 [2, 64, 1024], replicated
- new_env_second: float32 [2, 64, 1024], replicated
- new_scalar_weight: float32 [2, 64, 1024], replicated
- new_scalar_first: float32 [2, 64, 1024], replicated
- new_scalar_second: float32 [2, 64, 1024], replicated
- new_mix_weight: float32 [1, 3, 64, 64], replicated
- new_mix_first: float32 [1, 3, 64, 64], replicated
- new_mix_second: float32 [1, 3, 64, 64], replicated
- new_energy_head: float32 [1028], replicated
- new_head_first: float32 [1028], replicated
- new_head_second: float32 [1028], replicated
- new_soap_weight: float32 [256, 128, 128], P(('irrep', 'edge'))
- new_soap_first: float32 [256, 128, 128], P(('irrep', 'edge'))
- new_soap_second: float32 [256, 128, 128], P(('irrep', 'edge'))
- new_soap_left: float32 [256, 128, 128], P(('irrep', 'edge'))
- new_soap_right: float32 [256, 128, 128], P(('irrep', 'edge'))
- new_soap_lstat: float32 [256, 128, 128], P(('irrep', 'edge'))
- new_soap_rstat: float32 [256, 128, 128], P(('irrep', 'edge'))
- new_soap_average: float32 [256, 128, 128], P(('irrep', 'edge'))
The draws below stay inside these ranges and needn't reach their ends.
Inputs may be any that keep to these rules, and one draw needn't show every extreme that they name: `edge_vec`: every edge vector has length between 1 and 4.8. `edge_live`: in the 512 slots of each device the used ones come first, at least half are used, and some device uses all. `energy_head`: the first 1024 entries are readout weights, the last 4 are positive species scales. `soap_left`: each block is an orthogonal matrix. `soap_right`: each block is an orthogonal matrix. `soap_lstat`: each block is symmetric with a positive dominant diagonal. `soap_rstat`: each block is symmetric with a positive dominant diagonal.
All inputs are finite; a program needn't handle non-finite values. No bound on the sum of `force_mask` on one device may be relied on, other than what follows from the above.
Results may differ from the reference program's by a relative error of at most 0.0003.
Values sent between devices are 32-bit elements; how exact they have to be, the bound alone decides.
No kernel may reach another device: no remote copies, remote signals or barrier semaphores. Data moves between devices by JAX's collectives and lax.ppermute only.
A program may use at most 448 MiB of HBM per device.

```python
import math
import jax
import jax.numpy as jnp
import numpy as np
from jax import lax

D = 1024
C = 64
NB = 8
SPECIES = 4
LAYERS = 2
BS = 128
NS_STEPS = 4
ADAM_STEP = 10
EB = 512
EDGES = 16384
ATOMS = 512
NMAT = 4
NBLK = 256


def draw_edge_vec(key, part):
    key = jax.random.fold_in(key, 101)
    dir_key, len_key = jax.random.split(key)
    direction = jax.random.uniform(dir_key, (3, EDGES), jnp.float32, -1.0, 1.0)
    direction = direction + jnp.where(direction >= 0.0, 0.2, -0.2)
    length = jnp.sqrt(jnp.sum(direction * direction, axis=0))
    distance = jax.random.uniform(len_key, (EDGES,), jnp.float32, 1.5, 4.2)
    return direction / length[None] * distance[None]


def draw_edge_live(key, part):
    key = jax.random.fold_in(key, 102)
    count_key, full_key = jax.random.split(key)
    blocks = EDGES // EB
    counts = jax.random.randint(count_key, (blocks,), EB // 2, EB + 1)
    chosen = jax.random.randint(full_key, (), 0, blocks)
    counts = jnp.where(jnp.arange(blocks) == chosen, EB, counts)
    position = jnp.arange(EDGES) % EB
    return (position < jnp.repeat(counts, EB)).astype(jnp.int32)


def draw_energy_head(key, part):
    key = jax.random.fold_in(key, 103)
    read_key, scale_key = jax.random.split(key)
    readout = jax.random.normal(read_key, (D,), jnp.float32) / math.sqrt(D)
    readout = jnp.clip(readout, -0.9, 0.9)
    scales = jax.random.uniform(scale_key, (SPECIES,), jnp.float32, 0.5, 2.0)
    return jnp.concatenate([readout, scales])


def orthogonal_blocks(key):
    sign_key, perm_key = jax.random.split(key)
    rows = jnp.arange(BS)[:, None].astype(jnp.float32)
    cols = jnp.arange(BS)[None, :].astype(jnp.float32)
    cosine = math.sqrt(2.0 / BS) * jnp.cos(math.pi * (2.0 * cols + 1.0) * rows / (2.0 * BS))
    cosine = jnp.where(rows == 0.0, cosine / math.sqrt(2.0), cosine)
    perms = jax.vmap(lambda one_key: jax.random.permutation(one_key, BS))(jax.random.split(perm_key, NBLK))
    columns = jnp.take(cosine, perms, axis=1).transpose(1, 0, 2)
    signs = jnp.where(jax.random.bernoulli(sign_key, 0.5, (NBLK, BS, 1)), 1.0, -1.0)
    return (columns * signs).astype(jnp.float32)


def stat_blocks(key):
    diag_key, off_key = jax.random.split(key)
    level = 0.05 / 0.95 * BS * 1e-06
    diagonal = level * jnp.exp(jax.random.uniform(diag_key, (NBLK, BS), jnp.float32, 0.0, math.log(4.0)))
    noise = jax.random.uniform(off_key, (NBLK, BS, BS), jnp.float32, -1.0, 1.0)
    symmetric = (noise + noise.transpose(0, 2, 1)) * (0.2 * level / BS)
    eye = jnp.eye(BS, dtype=jnp.float32)[None]
    return symmetric * (1.0 - eye) + diagonal[:, :, None] * eye


def draw_soap_left(key, part):
    return orthogonal_blocks(jax.random.fold_in(key, 104))


def draw_soap_right(key, part):
    return orthogonal_blocks(jax.random.fold_in(key, 105))


def draw_soap_lstat(key, part):
    return stat_blocks(jax.random.fold_in(key, 106))


def draw_soap_rstat(key, part):
    return stat_blocks(jax.random.fold_in(key, 107))


def place_ends(values, stream_key, smallest, top_value):
    spot = [jax.random.randint(jax.random.fold_in(stream_key, axis), (), 0, length) for axis, length in enumerate(values.shape)]
    main_axis = values.shape.index(max(values.shape))
    beside = spot[:main_axis] + [(spot[main_axis] + 1) % values.shape[main_axis]] + spot[main_axis + 1:]
    return values.at[tuple(spot)].set(smallest).at[tuple(beside)].set(top_value)


def levels(own_key, dims, pieces, smallest, largest):
    level = 1.0
    for dim, parts in pieces:
        draws = jax.random.uniform(jax.random.fold_in(jax.random.fold_in(own_key, 6), dim), (parts,), jnp.float32, smallest / len(pieces), largest / len(pieces))
        level = level * jnp.repeat(jnp.exp(draws), dims[dim] // parts).reshape((-1,) + (1,) * (len(dims) - 1 - dim))
    return level


def bell_draw(rng, shape, spread, bound, shards=(), held_as=jnp.bfloat16):
    level = levels(rng, shape, shards, -0.22, 0.18) if shards else 1.0
    drawn = jax.random.normal(rng, shape, jnp.float32) * spread * level
    return jnp.minimum(jnp.maximum(drawn, -bound), bound).astype(held_as)


def setup_inputs(seed: int = 0) -> dict:
    keys = jax.random.split(jax.random.key(seed), 35)
    edge_vec = draw_edge_vec(jax.random.fold_in(keys[34], 71), 0)
    edge_live = draw_edge_live(jax.random.fold_in(keys[34], 71), 0)
    source = place_ends(jax.random.randint(keys[2], (EDGES,), 0, ATOMS), jax.random.fold_in(keys[2], 1), 0, ATOMS - 1).astype(jnp.int32)
    target = place_ends(jax.random.randint(keys[3], (EDGES,), 0, ATOMS), jax.random.fold_in(keys[3], 1), 0, ATOMS - 1).astype(jnp.int32)
    species = place_ends(jax.random.randint(keys[4], (ATOMS,), 0, SPECIES), jax.random.fold_in(keys[4], 1), 0, SPECIES - 1).astype(jnp.int32)
    force_label = bell_draw(keys[5], (3, ATOMS), 1.0, 6.0, ((1, 32),), jnp.float32)
    force_mask = place_ends((jax.random.randint(keys[6], (ATOMS,), 0, 4) < 3).astype(jnp.int32), jax.random.fold_in(keys[6], 1), 0, 1)
    block_owner = jax.random.permutation(keys[7], NBLK).astype(jnp.int32)
    pair_in_weight = bell_draw(keys[8], (NB + 2 * SPECIES, D), (NB + 2 * SPECIES) ** -0.5, 1.5, (), jnp.float32)
    pair_in_first = bell_draw(keys[9], (NB + 2 * SPECIES, D), 0.0001, 0.00061035156, (), jnp.float32)
    pair_in_second = jnp.clip(jnp.exp(jax.random.uniform(keys[10], (NB + 2 * SPECIES, D), jnp.float32, math.log(9.99999993922529e-09), math.log(3.999999975690116e-08))), 9.99999993922529e-09, 3.999999975690116e-08)
    pair_out_weight = bell_draw(keys[11], (D, D), D ** -0.5, 0.1875, (), jnp.float32)
    pair_out_first = bell_draw(keys[12], (D, D), 0.0001, 0.00061035156, (), jnp.float32)
    pair_out_second = jnp.clip(jnp.exp(jax.random.uniform(keys[13], (D, D), jnp.float32, math.log(9.99999993922529e-09), math.log(3.999999975690116e-08))), 9.99999993922529e-09, 3.999999975690116e-08)
    env_weight = bell_draw(keys[14], (LAYERS, C, D), D ** -0.5, 0.1875, (), jnp.float32)
    env_first = bell_draw(keys[15], (LAYERS, C, D), 0.0001, 0.00061035156, (), jnp.float32)
    env_second = jnp.clip(jnp.exp(jax.random.uniform(keys[16], (LAYERS, C, D), jnp.float32, math.log(9.99999993922529e-09), math.log(3.999999975690116e-08))), 9.99999993922529e-09, 3.999999975690116e-08)
    scalar_weight = bell_draw(keys[17], (LAYERS, C, D), C ** -0.5, 0.75, (), jnp.float32)
    scalar_first = bell_draw(keys[18], (LAYERS, C, D), 0.0001, 0.00061035156, (), jnp.float32)
    scalar_second = jnp.clip(jnp.exp(jax.random.uniform(keys[19], (LAYERS, C, D), jnp.float32, math.log(9.99999993922529e-09), math.log(3.999999975690116e-08))), 9.99999993922529e-09, 3.999999975690116e-08)
    mix_weight = bell_draw(keys[20], (LAYERS - 1, 3, C, C), C ** -0.5, 0.75, (), jnp.float32)
    mix_first = bell_draw(keys[21], (LAYERS - 1, 3, C, C), 0.0001, 0.00061035156, (), jnp.float32)
    mix_second = jnp.clip(jnp.exp(jax.random.uniform(keys[22], (LAYERS - 1, 3, C, C), jnp.float32, math.log(9.99999993922529e-09), math.log(3.999999975690116e-08))), 9.99999993922529e-09, 3.999999975690116e-08)
    energy_head = draw_energy_head(jax.random.fold_in(keys[34], 71), 0)
    head_first = bell_draw(keys[24], (D + SPECIES,), 0.0001, 0.00061035156, (), jnp.float32)
    head_second = jnp.clip(jnp.exp(jax.random.uniform(keys[25], (D + SPECIES,), jnp.float32, math.log(9.99999993922529e-09), math.log(3.999999975690116e-08))), 9.99999993922529e-09, 3.999999975690116e-08)
    soap_weight = bell_draw(keys[26], (NBLK, BS, BS), D ** -0.5, 0.1875, ((0, 32),), jnp.float32)
    soap_first = bell_draw(keys[27], (NBLK, BS, BS), 0.0001, 0.00061035156, ((0, 32),), jnp.float32)
    soap_second = jnp.clip(jnp.exp(math.log(3.999999975690116e-08) - 1.3862944 * jax.random.uniform(keys[28], (NBLK, BS, BS), jnp.float32) ** levels(keys[28], (NBLK, BS, BS), ((0, 32),), -0.2, 0.2)), 9.99999993922529e-09, 3.999999975690116e-08)
    soap_left = draw_soap_left(jax.random.fold_in(keys[34], 71), 0)
    soap_right = draw_soap_right(jax.random.fold_in(keys[34], 71), 0)
    soap_lstat = draw_soap_lstat(jax.random.fold_in(keys[34], 71), 0)
    soap_rstat = draw_soap_rstat(jax.random.fold_in(keys[34], 71), 0)
    soap_average = bell_draw(keys[33], (NBLK, BS, BS), D ** -0.5, 0.1875, ((0, 32),), jnp.float32)
    return dict(edge_vec=edge_vec, edge_live=edge_live, source=source, target=target, species=species, force_label=force_label, force_mask=force_mask, block_owner=block_owner, pair_in_weight=pair_in_weight, pair_in_first=pair_in_first, pair_in_second=pair_in_second, pair_out_weight=pair_out_weight, pair_out_first=pair_out_first, pair_out_second=pair_out_second, env_weight=env_weight, env_first=env_first, env_second=env_second, scalar_weight=scalar_weight, scalar_first=scalar_first, scalar_second=scalar_second, mix_weight=mix_weight, mix_first=mix_first, mix_second=mix_second, energy_head=energy_head, head_first=head_first, head_second=head_second, soap_weight=soap_weight, soap_first=soap_first, soap_second=soap_second, soap_left=soap_left, soap_right=soap_right, soap_lstat=soap_lstat, soap_rstat=soap_rstat, soap_average=soap_average)


@jax.custom_vjp
def low(v):
    return lax.optimization_barrier(v.astype(jnp.bfloat16)).astype(jnp.float32)

@jax.custom_vjp
def low_back(v):
    return v

def low_keep(v):
    return (low(v), None)

def low_pass(kept, grad):
    return (grad,)

def back_keep(v):
    return (v, None)

def back_low(kept, grad):
    return (low(grad),)
low.defvjp(low_keep, low_pass)
low_back.defvjp(back_keep, back_low)
HIGH = lax.Precision.HIGHEST
CUTOFF = 5.0
ROOT_TWO = math.sqrt(2.0)
ROOT_THREE = math.sqrt(3.0)
ROOT_SIX = math.sqrt(6.0)
HARMONIC = math.sqrt(7.5)
RESIDUAL = 1.0 / math.sqrt(2.0)

def shape_basis():
    return [np.array([[0.0, 1, 0], [1, 0, 0], [0, 0, 0]]) / ROOT_TWO, np.array([[0.0, 0, 0], [0, 0, 1], [0, 1, 0]]) / ROOT_TWO, np.array([[0.0, 0, 1], [0, 0, 0], [1, 0, 0]]) / ROOT_TWO, np.array([[1.0, 0, 0], [0, -1, 0], [0, 0, 0]]) / ROOT_TWO, np.array([[-1.0, 0, 0], [0, -1, 0], [0, 0, 2]]) / ROOT_SIX]

def cross_three(left_vec, right_vec):
    return np.array([left_vec[1] * right_vec[2] - left_vec[2] * right_vec[1], left_vec[2] * right_vec[0] - left_vec[0] * right_vec[2], left_vec[0] * right_vec[1] - left_vec[1] * right_vec[0]])

def product_table():
    tensors = shape_basis()
    table = np.zeros((9, 9, 9))
    unit_rows = np.eye(9)
    for first in range(9):
        for second in range(9):
            left = unit_rows[first]
            right = unit_rows[second]
            left_mat = sum((left[4 + slot] * tensors[slot] for slot in range(5)))
            right_mat = sum((right[4 + slot] * tensors[slot] for slot in range(5)))
            left_vec = left[1:4]
            right_vec = right[1:4]
            scalar = left[0] * right[0] + left_vec @ right_vec + np.sum(left_mat * right_mat.T)
            vector = left[0] * right_vec + right[0] * left_vec + cross_three(left_vec, right_vec) + left_mat @ right_vec + right_mat @ left_vec
            matrix = left[0] * right_mat + right[0] * left_mat + (np.outer(left_vec, right_vec) + np.outer(right_vec, left_vec)) / 2 + (left_mat @ right_mat + right_mat @ left_mat) / 2
            table[first, second, 0] = scalar
            table[first, second, 1:4] = vector
            for slot in range(5):
                table[first, second, 4 + slot] = np.sum(tensors[slot] * matrix)
    return (table / 3.0).astype(np.float32)

def contract_last(left, right):
    return lax.dot_general(left, right, (((1,), (1,)), ((), ())), precision=HIGH)

def contract_first(left, right):
    return lax.dot_general(left, right, (((0,), (0,)), ((), ())), precision=HIGH)

def geometry(pair_in, pair_out, vectors, live_edges, onehot_source, onehot_target):
    distance = jnp.sqrt(lax.optimization_barrier(jnp.sum(vectors * vectors, axis=0)))
    unit_x = vectors[0] / distance
    unit_y = vectors[1] / distance
    unit_z = vectors[2] / distance
    ratio = distance / CUTOFF
    envelope = (1.0 - 28.0 * ratio ** 6 + 48.0 * ratio ** 7 - 21.0 * ratio ** 8) * live_edges
    orders = jnp.arange(1, NB + 1).astype(jnp.float32)[:, None]
    bessel = math.sqrt(2.0 / CUTOFF) * jnp.sin(orders * (math.pi / CUTOFF) * distance[None]) / distance[None]
    features = jnp.concatenate([bessel, onehot_source, onehot_target], axis=0)
    hidden = jax.nn.silu(contract_first(features, pair_in))
    latent = envelope[:, None] * jnp.dot(hidden, pair_out, precision=HIGH)
    harmonics = jnp.stack([jnp.ones_like(unit_x), ROOT_THREE * unit_x, ROOT_THREE * unit_y, ROOT_THREE * unit_z, HARMONIC * ROOT_TWO * unit_x * unit_y, HARMONIC * ROOT_TWO * unit_y * unit_z, HARMONIC * ROOT_TWO * unit_x * unit_z, HARMONIC * (unit_x * unit_x - unit_y * unit_y) / ROOT_TWO, HARMONIC * (2.0 * unit_z * unit_z - unit_x * unit_x - unit_y * unit_y) / ROOT_SIX])
    return (harmonics, envelope, latent)

def mix_blocks(mixing, tensor):
    return jnp.concatenate([jnp.einsum('cd,kde->kce', mixing[0], tensor[0:1], precision=HIGH), jnp.einsum('cd,kde->kce', mixing[1], tensor[1:4], precision=HIGH), jnp.einsum('cd,kde->kce', mixing[2], tensor[4:9], precision=HIGH)], axis=0)

def tensor_product(feature, environ, width):
    table = jnp.asarray(product_table()[:, :, :width])
    summed = feature[0][None] * jnp.einsum('bk,bce->kce', table[0], environ, precision=HIGH)
    for first in range(1, 9):
        summed = summed + feature[first][None] * jnp.einsum('bk,bce->kce', table[first], environ, precision=HIGH)
    return summed

def update(x_in, scal_in, second_w, latent, previous, envelope):
    preact = jnp.dot(latent, x_in, precision=HIGH) + contract_first(previous[0], scal_in)
    return (latent + envelope[:, None] * jnp.dot(jax.nn.silu(preact), second_w, precision=HIGH)) * RESIDUAL

def to_matrices(blocks):
    side = D // BS
    return blocks.reshape(NMAT, side, side, BS, BS).transpose(0, 1, 3, 2, 4).reshape(NMAT, D, D)

def energy_of(weights, vectors, block_owner, live_edges, source, onehot_source, onehot_target):
    pair_in, pair_out, env_weight, scalar_weight, mix_weight, energy_head, soap_weight = weights
    matrices = to_matrices(jnp.zeros_like(soap_weight).at[block_owner].set(soap_weight))
    harmonics, envelope, latent = geometry(pair_in, pair_out, vectors, live_edges, onehot_source, onehot_target)
    scale = math.sqrt(ATOMS / EDGES)
    previous = None
    for layer_no in range(LAYERS):
        embedded = harmonics[:, None, :] * contract_last(env_weight[layer_no], latent)[None]
        feature = embedded if layer_no == 0 else mix_blocks(mix_weight[layer_no - 1], previous)
        summed = jnp.zeros((9, C, ATOMS), jnp.float32).at[:, :, source].add(embedded)
        environ = summed[:, :, source] * scale
        width = 1 if layer_no == LAYERS - 1 else 9
        previous = tensor_product(feature, environ, width)
        latent = update(matrices[2 * layer_no], scalar_weight[layer_no], matrices[2 * layer_no + 1], latent, previous, envelope)
    per_edge = jnp.dot(latent, energy_head[:D], precision=HIGH)
    factor = jnp.dot(energy_head[D:], onehot_source, precision=HIGH)
    return jnp.sum(envelope * factor * per_edge)

def adamw(weight, first, second, grad):
    first_new = 0.9 * first + 0.1 * grad
    second_new = 0.99 * second + 0.01 * grad * grad
    normal = first_new / (1.0 - 0.9 ** ADAM_STEP) / (jnp.sqrt(second_new / (1.0 - 0.99 ** ADAM_STEP)) + 1e-08)
    return (weight - 0.01 * (normal + 0.01 * weight), first_new, second_new)

def orthogonalize(matrix):
    current = matrix / jnp.sqrt(jnp.sum(matrix * matrix))
    for step_no in range(NS_STEPS):
        current = 1.5 * current - 0.5 * jnp.dot(jnp.dot(current, current.T, precision=HIGH), current, precision=HIGH)
    return current

def soap_slot(grad, weight, first, second, left, right, lstat, rstat, average):
    rotated = jnp.dot(jnp.dot(left.T, grad, precision=HIGH), right, precision=HIGH)
    first_new = 0.9 * first + 0.1 * rotated
    second_new = 0.99 * second + 0.01 * rotated * rotated
    normal = first_new / (1.0 - 0.9 ** ADAM_STEP) / (jnp.sqrt(second_new / (1.0 - 0.99 ** ADAM_STEP)) + 1e-08)
    weight_new = weight - 0.01 * (jnp.dot(jnp.dot(left, normal, precision=HIGH), right.T, precision=HIGH) + 0.01 * weight)
    lstat_new = 0.95 * lstat + 0.05 * jnp.dot(grad, grad.T, precision=HIGH)
    rstat_new = 0.95 * rstat + 0.05 * jnp.dot(grad.T, grad, precision=HIGH)
    left_new = orthogonalize(jnp.dot(lstat_new, left, precision=HIGH))
    right_new = orthogonalize(jnp.dot(rstat_new, right, precision=HIGH))
    plain = jnp.dot(jnp.dot(left, first_new, precision=HIGH), right.T, precision=HIGH)
    first_out = jnp.dot(jnp.dot(left_new.T, plain, precision=HIGH), right_new, precision=HIGH)
    average_new = 0.99 * average + 0.01 * weight_new
    return (weight_new, first_out, second_new, left_new, right_new, lstat_new, rstat_new, average_new)

def reference(edge_vec, edge_live, source, target, species, force_label, force_mask, block_owner, pair_in_weight, pair_in_first, pair_in_second, pair_out_weight, pair_out_first, pair_out_second, env_weight, env_first, env_second, scalar_weight, scalar_first, scalar_second, mix_weight, mix_first, mix_second, energy_head, head_first, head_second, soap_weight, soap_first, soap_second, soap_left, soap_right, soap_lstat, soap_rstat, soap_average):
    live_edges = edge_live.astype(jnp.float32)
    kinds = jnp.arange(SPECIES, dtype=jnp.int32)[:, None]
    onehot_source = (species[source][None, :] == kinds).astype(jnp.float32)
    onehot_target = (species[target][None, :] == kinds).astype(jnp.float32)
    label_mask = force_mask.astype(jnp.float32)
    label_total = jnp.sum(label_mask)

    def loss_of(weights):

        def energy_at(vectors):
            return energy_of(weights, vectors, block_owner, live_edges, source, onehot_source, onehot_target)
        energy, backward = jax.vjp(energy_at, edge_vec)
        grad_vec = backward(jnp.ones_like(energy))[0]
        force = jnp.zeros((3, ATOMS), jnp.float32).at[:, source].add(grad_vec).at[:, target].add(-grad_vec)
        residual = force - force_label
        summed = jnp.sum(label_mask[None] * residual * residual)
        return (summed / label_total, summed)
    weights = (pair_in_weight, pair_out_weight, env_weight, scalar_weight, mix_weight, energy_head, soap_weight)
    loss, backward, loss_total = jax.vjp(loss_of, weights, has_aux=True)
    grads = backward(jnp.ones_like(loss))[0]
    new_pair_in = adamw(pair_in_weight, pair_in_first, pair_in_second, grads[0])
    new_pair_out = adamw(pair_out_weight, pair_out_first, pair_out_second, grads[1])
    new_env = adamw(env_weight, env_first, env_second, grads[2])
    new_scalar = adamw(scalar_weight, scalar_first, scalar_second, grads[3])
    new_mix = adamw(mix_weight, mix_first, mix_second, grads[4])
    new_head = adamw(energy_head, head_first, head_second, grads[5])
    soap = jax.vmap(soap_slot)(grads[6], soap_weight, soap_first, soap_second, soap_left, soap_right, soap_lstat, soap_rstat, soap_average)
    return (loss_total, label_total, new_pair_in[0], new_pair_in[1], new_pair_in[2], new_pair_out[0], new_pair_out[1], new_pair_out[2], new_env[0], new_env[1], new_env[2], new_scalar[0], new_scalar[1], new_scalar[2], new_mix[0], new_mix[1], new_mix[2], new_head[0], new_head[1], new_head[2], soap[0], soap[1], soap[2], soap[3], soap[4], soap[5], soap[6], soap[7])
```

```python
from functools import partial
import math

import jax
import jax.numpy as jnp
import numpy as np
from jax import lax
from jax.sharding import PartitionSpec as P

D = 1024
NB = 8
SPECIES = 4
LAYERS = 2
BS = 128
NS_STEPS = 4
ADAM_STEP = 10
SIDE = D // BS
AX = ("irrep", "edge")

HIGH = lax.Precision.HIGH
FULL = lax.Precision.HIGHEST
CUTOFF = 5.0
ROOT_TWO = math.sqrt(2.0)
ROOT_THREE = math.sqrt(3.0)
ROOT_SIX = math.sqrt(6.0)
HARMONIC = math.sqrt(7.5)
RES = 1.0 / math.sqrt(2.0)


def shape_basis():
    return [
        np.array([[0.0, 1, 0], [1, 0, 0], [0, 0, 0]]) / ROOT_TWO,
        np.array([[0.0, 0, 0], [0, 0, 1], [0, 1, 0]]) / ROOT_TWO,
        np.array([[0.0, 0, 1], [0, 0, 0], [1, 0, 0]]) / ROOT_TWO,
        np.array([[1.0, 0, 0], [0, -1, 0], [0, 0, 0]]) / ROOT_TWO,
        np.array([[-1.0, 0, 0], [0, -1, 0], [0, 0, 2]]) / ROOT_SIX,
    ]


def cross_three(left_vec, right_vec):
    return np.array(
        [
            left_vec[1] * right_vec[2] - left_vec[2] * right_vec[1],
            left_vec[2] * right_vec[0] - left_vec[0] * right_vec[2],
            left_vec[0] * right_vec[1] - left_vec[1] * right_vec[0],
        ]
    )


def product_table():
    tensors = shape_basis()
    table = np.zeros((9, 9, 9))
    unit_rows = np.eye(9)
    for first in range(9):
        for second in range(9):
            left = unit_rows[first]
            right = unit_rows[second]
            left_mat = sum((left[4 + slot] * tensors[slot] for slot in range(5)))
            right_mat = sum((right[4 + slot] * tensors[slot] for slot in range(5)))
            left_vec = left[1:4]
            right_vec = right[1:4]
            scalar = left[0] * right[0] + left_vec @ right_vec + np.sum(left_mat * right_mat.T)
            vector = (
                left[0] * right_vec
                + right[0] * left_vec
                + cross_three(left_vec, right_vec)
                + left_mat @ right_vec
                + right_mat @ left_vec
            )
            matrix = (
                left[0] * right_mat
                + right[0] * left_mat
                + (np.outer(left_vec, right_vec) + np.outer(right_vec, left_vec)) / 2
                + (left_mat @ right_mat + right_mat @ left_mat) / 2
            )
            table[first, second, 0] = scalar
            table[first, second, 1:4] = vector
            for slot in range(5):
                table[first, second, 4 + slot] = np.sum(tensors[slot] * matrix)
    return (table / 3.0).astype(np.float32)


TABLE = product_table()
TERMS = [
    (a, b, k, float(TABLE[a, b, k]))
    for a in range(9)
    for b in range(9)
    for k in range(9)
    if abs(TABLE[a, b, k]) > 1e-7
]


def dot(left, right, dims, precision=HIGH):
    return lax.dot_general(left, right, ((dims[0], dims[1]), ((), ())), precision=precision)


def nn(left, right):
    return dot(left, right, ((1,), (0,)))


def tn(left, right):
    return dot(left, right, ((0,), (0,)))


def nt(left, right):
    return dot(left, right, ((1,), (1,)))


def device_of(y, x, z, core):
    return (y * 2 + x) * 8 + z * 2 + core


CUBE = [(y, x, z, c) for y in range(2) for x in range(2) for z in range(4) for c in range(2)]
HOP_X = [(device_of(y, x, z, c), device_of(y, 1 - x, z, c)) for y, x, z, c in CUBE]
HOP_Y = [(device_of(y, x, z, c), device_of(1 - y, x, z, c)) for y, x, z, c in CUBE]
HOP_XY = [(device_of(y, x, z, c), device_of(1 - y, 1 - x, z, c)) for y, x, z, c in CUBE]
HOP_CORE = [(device_of(y, x, z, c), device_of(y, x, z, 1 - c)) for y, x, z, c in CUBE]


def along_z(pairs):
    return [
        (device_of(y, x, s, c), device_of(y, x, t, c))
        for s, t in pairs
        for y in range(2)
        for x in range(2)
        for c in range(2)
    ]


HOP_IN = along_z([(0, 1), (3, 2)])
HOP_MID = along_z([(1, 2), (2, 1)])
HOP_OUT = along_z([(1, 0), (2, 3)])
HOP_Z = [along_z([(s, s ^ k) for s in range(4)]) for k in range(1, 4)]


def hop(value, pairs):
    return lax.ppermute(value, AX, pairs)


def place():
    irrep = lax.axis_index("irrep")
    edge = lax.axis_index("edge")
    return irrep // 2, irrep % 2, edge // 2, edge % 2


Z_ORDER = np.array([[3, 2, 1, 0], [3, 2, 0, 1], [0, 1, 3, 2], [0, 1, 2, 3]], np.int32)


def relative_devices():
    y, x, z, core = place()
    zs = jnp.asarray(Z_ORDER)[z]
    two = jnp.arange(2, dtype=jnp.int32)
    irrep = (two[None, :] ^ y) * 2 + (two[:, None] ^ x)
    return (
        irrep[None, :, :, None] * 8 + zs[:, None, None, None] * 2 + (two ^ core)[None, None, None, :]
    )


def reduce_plane(block):
    half = block.shape[2] // 2
    upper, lower = block[:, :, :half], block[:, :, half:]
    a1 = upper[0] + hop(upper[1], HOP_X)
    b1 = lower[:, 0] + hop(lower[:, 1], HOP_Y)
    a2 = a1[0] + hop(a1[1], HOP_Y)
    b2 = b1[0] + hop(b1[1], HOP_X)
    return jnp.concatenate([a2, b2], axis=0)


def reduce_chips(chunks):
    q0 = reduce_plane(chunks[0])
    p0 = q0 + hop(q0, HOP_IN)
    q1 = reduce_plane(chunks[1])
    q2 = reduce_plane(chunks[2])
    q3 = reduce_plane(chunks[3])
    p1 = q1 + hop(q1, HOP_IN)
    p2 = q2 + hop(p0, HOP_MID)
    return q3 + hop(q2, HOP_IN) + hop(p1, HOP_MID) + hop(p2, HOP_OUT)


def spread_plane(own):
    half = own.shape[0] // 2
    upper, lower = own[:half], own[half:]
    a1 = jnp.stack([upper, hop(upper, HOP_Y)])
    b1 = jnp.stack([lower, hop(lower, HOP_X)])
    a2 = jnp.stack([a1, hop(a1, HOP_X)])
    b2 = jnp.stack([b1, hop(b1, HOP_Y)], axis=1)
    return jnp.concatenate([a2, b2], axis=2)


def spread_chips(own):
    from_inner = hop(own, HOP_OUT)
    from_mid = hop(own, HOP_MID)
    from_outer = hop(own, HOP_IN)
    c2 = from_inner + from_outer
    far = hop(from_outer, HOP_MID)
    c1 = from_mid + hop(from_mid, HOP_OUT)
    c0 = far + hop(far, HOP_OUT)
    return [spread_plane(c) for c in (c0, c1, c2, own)]


def is_cube(sizes):
    return sizes == (4, 8)


def gather_small(value, sizes):
    if not is_cube(sizes):
        return lax.all_gather(value, AX, axis=0, tiled=False)
    y, x, z, core = place()
    plane = jnp.stack([value, hop(value, HOP_X), hop(value, HOP_Y), hop(value, HOP_XY)])
    column = jnp.stack([plane] + [hop(plane, pairs) for pairs in HOP_Z])
    every = jnp.stack([column, hop(column, HOP_CORE)])
    flat = every.reshape((32,) + value.shape)
    ids = np.arange(32, dtype=np.int32)
    core_of, z_of, x_of, y_of = ids % 2, ids // 2 % 4, ids // 8 % 2, ids // 16
    index = (core_of ^ core) * 16 + (z_of ^ z) * 4 + (y_of ^ y) * 2 + (x_of ^ x)
    return flat[index]


def sum_small(value, sizes):
    if not is_cube(sizes):
        return lax.psum(value, AX)
    total = value + hop(value, HOP_CORE)
    plane = total + hop(total, HOP_X) + (hop(total, HOP_Y) + hop(total, HOP_XY))
    one, two, three = [hop(plane, pairs) for pairs in HOP_Z]
    return (plane + one) + (two + three)


def geometry(vec, live):
    dist = jnp.sqrt(jnp.sum(vec * vec, axis=0))
    inv = 1.0 / dist
    unit = vec * inv[None]
    ratio = dist / CUTOFF
    r5 = ratio**5
    env = (1.0 - r5 * ratio * (28.0 - 48.0 * ratio + 21.0 * ratio * ratio)) * live
    denv = -(168.0 / CUTOFF) * r5 * (1.0 - ratio) * (1.0 - ratio) * live
    order = jnp.arange(1, NB + 1).astype(jnp.float32)[:, None] * (math.pi / CUTOFF)
    angle = order * dist[None]
    norm = math.sqrt(2.0 / CUTOFF)
    bessel = norm * jnp.sin(angle) * inv[None]
    dbessel = norm * order * jnp.cos(angle) * inv[None] - bessel * inv[None]
    return inv, unit, env, denv, bessel, dbessel


def harmonics(unit):
    x, y, z = unit
    h = HARMONIC
    return jnp.stack(
        [
            jnp.ones_like(x),
            ROOT_THREE * x,
            ROOT_THREE * y,
            ROOT_THREE * z,
            h * ROOT_TWO * x * y,
            h * ROOT_TWO * y * z,
            h * ROOT_TWO * x * z,
            h * (x * x - y * y) / ROOT_TWO,
            h * (2.0 * z * z - x * x - y * y) / ROOT_SIX,
        ]
    )


def harmonics_dot(unit, dunit):
    x, y, z = unit
    dx, dy, dz = dunit
    h = HARMONIC
    return jnp.stack(
        [
            jnp.zeros_like(x),
            ROOT_THREE * dx,
            ROOT_THREE * dy,
            ROOT_THREE * dz,
            h * ROOT_TWO * (dx * y + x * dy),
            h * ROOT_TWO * (dy * z + y * dz),
            h * ROOT_TWO * (dx * z + x * dz),
            h * ROOT_TWO * (x * dx - y * dy),
            (2.0 * h / ROOT_SIX) * (2.0 * z * dz - x * dx - y * dy),
        ]
    )


def harmonics_back(unit, bar):
    x, y, z = unit
    a, b = HARMONIC * ROOT_TWO, 2.0 * HARMONIC / ROOT_SIX
    return jnp.stack(
        [
            ROOT_THREE * bar[1] + a * (y * bar[4] + z * bar[6] + x * bar[7]) - b * x * bar[8],
            ROOT_THREE * bar[2] + a * (x * bar[4] + z * bar[5] - y * bar[7]) - b * y * bar[8],
            ROOT_THREE * bar[3] + a * (y * bar[5] + x * bar[6]) + 2.0 * b * z * bar[8],
        ]
    )


def silu(v):
    return v * jax.nn.sigmoid(v)


def silu_one(v):
    s = jax.nn.sigmoid(v)
    return s * (1.0 + v * (1.0 - s))


def silu_two(v):
    s = jax.nn.sigmoid(v)
    return s * (1.0 - s) * (2.0 + v * (1.0 - 2.0 * s))


def bilinear(sets, out, size):
    total = [None] * size
    for index in TERMS:
        a, b, k, value = index
        slot = index[out]
        for (li, left), (ri, right) in sets:
            term = left[index[li]] * right[index[ri]]
            term = value * term
            total[slot] = term if total[slot] is None else total[slot] + term
    return jnp.stack(total)


def product(feature, environ):
    return bilinear([((0, feature), (1, environ))], 2, 9)


def mix(mixing, tensor, transposed):
    op = tn if transposed else nn
    out = []
    for order, (start, stop) in enumerate(((0, 1), (1, 4), (4, 9))):
        for k in range(start, stop):
            out.append(op(mixing[order], tensor[k]))
    return jnp.stack(out)


def mix_gradient(left, right):
    out = []
    for start, stop in ((0, 1), (1, 4), (4, 9)):
        out.append(sum(nt(left[k], right[k]) for k in range(start, stop)))
    return out


def chain(weights, load_matrices, environ, force_to_tangent, vec, live, species_source, species_target):
    pair_in, pair_out, env_weight, scalar_weight, mix_weight, energy_head = weights
    head = energy_head[:D]
    factor = jnp.sum(
        energy_head[D:, None] * species_source, axis=0
    )
    inv, unit, env, denv, bessel, dbessel = geometry(vec, live)
    shape = harmonics(unit)
    feat = jnp.concatenate([bessel, species_source, species_target], axis=0)
    col = lambda v: v[:, None]
    pre0 = tn(feat, pair_in)
    hid = silu(pre0)
    out0 = nn(hid, pair_out)
    lat0 = col(env) * out0
    w0 = nt(env_weight[0], lat0)
    emb0 = shape[:, None] * w0[None]
    env0 = environ(emb0)
    res0 = product(emb0, env0)
    matrices = load_matrices(res0)
    pre1 = nn(lat0, matrices[0]) + tn(res0[0], scalar_weight[0])
    act1 = silu(pre1)
    out1 = nn(act1, matrices[1])
    lat1 = (lat0 + col(env) * out1) * RES
    w1 = nt(env_weight[1], lat1)
    emb1 = shape[:, None] * w1[None]
    env1 = environ(emb1)
    feat1 = mix(mix_weight, res0, False)
    res1 = jnp.sum(feat1 * env1, axis=0) / 3.0
    pre2 = nn(lat1, matrices[2]) + tn(res1, scalar_weight[1])
    act2 = silu(pre2)
    top = dot(matrices[3], head, ((1,), (0,)))
    slope = env * factor
    per1 = jnp.sum(lat1 * head[None], axis=1)
    per2 = jnp.sum(act2 * top[None], axis=1)
    env_bar = RES * factor * (per1 + 2.0 * env * per2)
    alpha = RES * slope
    lead = alpha * env
    slope2 = silu_one(pre2)
    pre2_bar = col(lead) * top[None] * slope2
    lat1_bar = col(alpha) * head[None] + nt(pre2_bar, matrices[2])
    res1_bar = nt(scalar_weight[1], pre2_bar)
    feat1_bar = res1_bar[None] * env1 / 3.0
    emb1_bar = environ(res1_bar[None] * feat1 / 3.0)
    shape_bar = jnp.sum(emb1_bar * w1[None], axis=1)
    w1_bar = jnp.sum(shape[:, None] * emb1_bar, axis=0)
    lat1_bar = lat1_bar + tn(w1_bar, env_weight[1])
    res0_bar = mix(mix_weight, feat1_bar, True)
    env_bar = env_bar + RES * jnp.sum(lat1_bar * out1, axis=1)
    out1_bar = RES * col(env) * lat1_bar
    act1_bar = nt(out1_bar, matrices[1])
    slope1 = silu_one(pre1)
    pre1_bar = act1_bar * slope1
    lat0_bar = RES * lat1_bar + nt(pre1_bar, matrices[0])
    res0_bar = res0_bar.at[0].add(nt(scalar_weight[0], pre1_bar))
    emb0_bar = bilinear([((2, res0_bar), (1, env0))], 0, 9) + environ(
        bilinear([((2, res0_bar), (0, emb0))], 1, 9)
    )
    shape_bar = shape_bar + jnp.sum(emb0_bar * w0[None], axis=1)
    w0_bar = jnp.sum(shape[:, None] * emb0_bar, axis=0)
    lat0_bar = lat0_bar + tn(w0_bar, env_weight[0])
    env_bar = env_bar + jnp.sum(lat0_bar * out0, axis=1)
    out0_bar = col(env) * lat0_bar
    hid_bar = nt(out0_bar, pair_out)
    slope0 = silu_one(pre0)
    pre0_bar = hid_bar * slope0
    bessel_bar = nt(pair_in[:NB], pre0_bar)
    dist_bar = env_bar * denv + jnp.sum(bessel_bar * dbessel, axis=0)
    unit_bar = harmonics_back(unit, shape_bar)
    along = jnp.sum(unit * unit_bar, axis=0)
    vec_bar = dist_bar[None] * unit + (unit_bar - unit * along[None]) * inv[None]
    vec_dot, loss_parts = force_to_tangent(vec_bar)
    dist_dot = jnp.sum(unit * vec_dot, axis=0)
    unit_dot = (vec_dot - unit * dist_dot[None]) * inv[None]
    env_dot = denv * dist_dot
    bessel_dot = dbessel * dist_dot[None]
    shape_dot = harmonics_dot(unit, unit_dot)
    pre0_dot = tn(bessel_dot, pair_in[:NB])
    hid_dot = slope0 * pre0_dot
    lat0_dot = col(env_dot) * out0 + col(env) * nn(hid_dot, pair_out)
    w0_dot = nt(env_weight[0], lat0_dot)
    emb0_dot = shape_dot[:, None] * w0[None] + shape[:, None] * w0_dot[None]
    env0_dot = environ(emb0_dot)
    res0_dot = bilinear(
        [((0, emb0_dot), (1, env0)), ((0, emb0), (1, env0_dot))], 2, 9
    )
    pre1_dot = nn(lat0_dot, matrices[0]) + tn(res0_dot[0], scalar_weight[0])
    act1_dot = slope1 * pre1_dot
    lat1_dot = (lat0_dot + col(env_dot) * out1 + col(env) * nn(act1_dot, matrices[1])) * RES
    w1_dot = nt(env_weight[1], lat1_dot)
    emb1_dot = shape_dot[:, None] * w1[None] + shape[:, None] * w1_dot[None]
    env1_dot = environ(emb1_dot)
    feat1_dot = mix(mix_weight, res0_dot, False)
    res1_dot = jnp.sum(feat1_dot * env1 + feat1 * env1_dot, axis=0) / 3.0
    pre2_dot = nn(lat1_dot, matrices[2]) + tn(res1_dot, scalar_weight[1])
    act2_dot = slope2 * pre2_dot
    lead_dot = 2.0 * RES * slope * env_dot
    last = jnp.sum(col(lead_dot) * act2 + col(lead) * act2_dot, axis=0)
    head_grad = RES * jnp.sum(
        col(factor * env_dot) * lat1 + col(slope) * lat1_dot, axis=0
    ) + jnp.sum(last[:, None] * matrices[3], axis=0)
    per1_dot = jnp.sum(lat1_dot * head[None], axis=1)
    per2_dot = jnp.sum(act2_dot * top[None], axis=1)
    energy_dot = env_dot * RES * (per1 + env * per2) + env * RES * (
        per1_dot + env_dot * per2 + env * per2_dot
    )
    scale_grad = jnp.sum(species_source * energy_dot[None], axis=1)
    head_grad = jnp.concatenate([head_grad, scale_grad])
    pre2_hat = top[None] * (col(lead_dot) * slope2 + col(lead) * silu_two(pre2) * pre2_dot)
    lat1_hat = col(RES * factor * env_dot) * head[None] + nt(pre2_hat, matrices[2])
    res1_hat = nt(scalar_weight[1], pre2_hat)
    feat1_hat = (res1_hat[None] * env1 + res1_bar[None] * env1_dot) / 3.0
    emb1_hat = environ((res1_hat[None] * feat1 + res1_bar[None] * feat1_dot) / 3.0)
    w1_hat = jnp.sum(shape_dot[:, None] * emb1_bar + shape[:, None] * emb1_hat, axis=0)
    lat1_hat = lat1_hat + tn(w1_hat, env_weight[1])
    res0_hat = mix(mix_weight, feat1_hat, True)
    out1_hat = RES * (col(env_dot) * lat1_bar + col(env) * lat1_hat)
    act1_hat = nt(out1_hat, matrices[1])
    pre1_hat = act1_hat * slope1 + act1_bar * silu_two(pre1) * pre1_dot
    lat0_hat = RES * lat1_hat + nt(pre1_hat, matrices[0])
    res0_hat = res0_hat.at[0].add(nt(scalar_weight[0], pre1_hat))
    emb0_hat = bilinear(
        [((2, res0_hat), (1, env0)), ((2, res0_bar), (1, env0_dot))], 0, 9
    ) + environ(bilinear([((2, res0_hat), (0, emb0)), ((2, res0_bar), (0, emb0_dot))], 1, 9))
    w0_hat = jnp.sum(shape_dot[:, None] * emb0_bar + shape[:, None] * emb0_hat, axis=0)
    lat0_hat = lat0_hat + tn(w0_hat, env_weight[0])
    out0_hat = col(env_dot) * lat0_bar + col(env) * lat0_hat
    pre0_hat = nt(out0_hat, pair_out) * slope0 + hid_bar * silu_two(pre0) * pre0_dot
    both = lambda first, second: jnp.concatenate([first, second], axis=0)
    pair_in_grad = nn(feat, pre0_hat)
    pair_in_grad = pair_in_grad.at[:NB].add(nn(bessel_dot, pre0_bar))
    mix_grad = jnp.stack(
        [
            first + second
            for first, second in zip(
                mix_gradient(feat1_bar, res0_dot), mix_gradient(feat1_hat, res0)
            )
        ]
    )
    env_grad = jnp.stack(
        [nn(w0_bar, lat0_dot) + nn(w0_hat, lat0), nn(w1_bar, lat1_dot) + nn(w1_hat, lat1)]
    )
    scalar_grad = jnp.stack(
        [
            nn(res0_dot[0], pre1_bar) + nn(res0[0], pre1_hat),
            nn(res1_dot, pre2_bar) + nn(res1, pre2_hat),
        ]
    )
    pair_out_grad = tn(both(hid_dot, hid), both(out0_bar, out0_hat))
    matrix_grad = [
        tn(both(lat0_dot, lat0), both(pre1_bar, pre1_hat)),
        tn(both(act1_dot, act1), both(out1_bar, out1_hat)),
        tn(both(lat1_dot, lat1), both(pre2_bar, pre2_hat)),
        last[:, None] * head[None],
    ]
    return (
        pair_in_grad,
        pair_out_grad,
        env_grad,
        scalar_grad,
        mix_grad,
        head_grad,
        matrix_grad,
        loss_parts,
    )


def adamw(weight, first, second, grad):
    first_new = 0.9 * first + 0.1 * grad
    second_new = 0.99 * second + 0.01 * grad * grad
    normal = (
        first_new
        / (1.0 - 0.9**ADAM_STEP)
        / (jnp.sqrt(second_new / (1.0 - 0.99**ADAM_STEP)) + 1e-08)
    )
    return (weight - 0.01 * (normal + 0.01 * weight), first_new, second_new)


def orthogonalize(matrix):
    current = matrix / jnp.sqrt(jnp.sum(matrix * matrix))
    for step_no in range(NS_STEPS):
        current = 1.5 * current - 0.5 * nn(nt(current, current), current)
    return current


def soap_slot(grad, weight, first, second, left, right, lstat, rstat, average):
    rotated = nn(tn(left, grad), right)
    first_new = 0.9 * first + 0.1 * rotated
    second_new = 0.99 * second + 0.01 * rotated * rotated
    normal = (
        first_new
        / (1.0 - 0.9**ADAM_STEP)
        / (jnp.sqrt(second_new / (1.0 - 0.99**ADAM_STEP)) + 1e-08)
    )
    weight_new = weight - 0.01 * (nt(nn(left, normal), right) + 0.01 * weight)
    lstat_new = 0.95 * lstat + 0.05 * nt(grad, grad)
    rstat_new = 0.95 * rstat + 0.05 * tn(grad, grad)
    left_new = orthogonalize(nn(lstat_new, left))
    right_new = orthogonalize(nn(rstat_new, right))
    plain = nt(nn(left, first_new), right)
    first_out = nn(tn(left_new, plain), right_new)
    average_new = 0.99 * average + 0.01 * weight_new
    return (
        weight_new,
        first_out,
        second_new,
        left_new,
        right_new,
        lstat_new,
        rstat_new,
        average_new,
    )


def gather_blocks(soap_weight, block_owner, sizes):
    inverse = jnp.zeros_like(block_owner).at[block_owner].set(
        jnp.arange(block_owner.shape[0], dtype=jnp.int32)
    )
    if not is_cube(sizes):
        return lax.all_gather(soap_weight, AX, axis=0, tiled=True)[inverse]
    per = soap_weight.shape[0]
    pieces = []
    for piece in spread_chips(soap_weight):
        pieces.append(jnp.stack([piece, hop(piece, HOP_CORE)], axis=2))
    every = jnp.concatenate(pieces, axis=0).reshape((-1,) + soap_weight.shape[1:])
    where = jnp.zeros((32,), jnp.int32).at[relative_devices().reshape(-1)].set(
        jnp.arange(32, dtype=jnp.int32)
    )
    return every[where[inverse // per] * per + inverse % per]


def to_matrices(blocks):
    return (
        blocks.reshape(2 * LAYERS, SIDE, SIDE, BS, BS).transpose(0, 1, 3, 2, 4).reshape(2 * LAYERS, D, D)
    )


def to_blocks(matrices):
    return (
        matrices.reshape(2 * LAYERS, SIDE, BS, SIDE, BS)
        .transpose(0, 1, 3, 2, 4)
        .reshape(2 * LAYERS * SIDE * SIDE, BS, BS)
    )


def scatter_blocks(blocks, block_owner, sizes, slots):
    if not is_cube(sizes):
        return lax.psum_scatter(blocks[block_owner], AX, scatter_dimension=0, tiled=True)
    core = lax.axis_index("edge") % 2
    chip = relative_devices()[..., :1] // 2 * (2 * slots)
    owner = block_owner[(chip + jnp.arange(2 * slots, dtype=jnp.int32)).reshape(-1)]
    laid = blocks[owner].reshape(4, 2, 2, 2 * slots, 2, BS // 2, BS)
    swapped = jnp.where(core == 0, laid, laid[:, :, :, :, ::-1])
    chunks = [swapped[p, :, :, :, 0] + hop(swapped[p, :, :, :, 1], HOP_CORE) for p in range(4)]
    total = reduce_chips(chunks)
    mine = jnp.where(core == 0, total[:slots], total[slots:])
    other = hop(jnp.where(core == 0, total[slots:], total[:slots]), HOP_CORE)
    return jnp.where(
        core == 0,
        jnp.concatenate([mine, other], axis=1),
        jnp.concatenate([other, mine], axis=1),
    )


ROWS = 336


def sum_large(trees, sizes):
    if not is_cube(sizes):
        return lax.psum(trees, AX)
    core = lax.axis_index("edge") % 2
    flat = jnp.concatenate([leaf.reshape(-1) for leaf in trees])
    count = flat.shape[0]
    flat = jnp.pad(flat, (0, 32 * ROWS * BS - count)).reshape(32, ROWS, BS)
    devices = relative_devices()
    laid = flat[devices.reshape(-1)].reshape(4, 2, 2, 2, ROWS, BS)
    chunks = [laid[p, :, :, 0] + hop(laid[p, :, :, 1], HOP_CORE) for p in range(4)]
    total = reduce_chips(chunks)
    pieces = []
    for piece in spread_chips(total):
        pieces.append(jnp.stack([piece, hop(piece, HOP_CORE)], axis=2))
    every = jnp.concatenate(pieces, axis=0).reshape(32, ROWS, BS)
    where = jnp.zeros((32,), jnp.int32).at[devices.reshape(-1)].set(
        jnp.arange(32, dtype=jnp.int32)
    )
    flat = every[where].reshape(-1)
    out, start = [], 0
    for leaf in trees:
        out.append(flat[start : start + leaf.size].reshape(leaf.shape))
        start += leaf.size
    return out


def local(
    sizes,
    edge_vec,
    edge_live,
    source,
    target,
    species,
    force_label,
    force_mask,
    block_owner,
    pair_in_weight,
    pair_in_first,
    pair_in_second,
    pair_out_weight,
    pair_out_first,
    pair_out_second,
    env_weight,
    env_first,
    env_second,
    scalar_weight,
    scalar_first,
    scalar_second,
    mix_weight,
    mix_first,
    mix_second,
    energy_head,
    head_first,
    head_second,
    soap_weight,
    soap_first,
    soap_second,
    soap_left,
    soap_right,
    soap_lstat,
    soap_rstat,
    soap_average,
):
    devices = sizes[0] * sizes[1]
    edges = edge_vec.shape[1]
    per_atoms = force_label.shape[1]
    atoms = per_atoms * devices
    me = lax.axis_index("irrep") * sizes[1] + lax.axis_index("edge")
    scale = math.sqrt(per_atoms / edges)
    as_float = lambda v: v.astype(jnp.float32)

    labels = jnp.concatenate([force_label, as_float(force_mask)[None]], axis=0).reshape(-1)
    packed = jnp.concatenate(
        [
            edge_vec,
            as_float(source)[None],
            as_float(target)[None],
            as_float(edge_live)[None],
            jnp.pad(labels, (0, edges - labels.shape[0]))[None],
        ],
        axis=0,
    )
    every = gather_small(packed, sizes)
    label_all = every[:, 6, : 4 * per_atoms].reshape(devices, 4, per_atoms)
    label_all = label_all.transpose(1, 0, 2).reshape(4, atoms)
    label_mask = label_all[3]
    label_total = jnp.sum(label_mask)
    payload = every[:, :5].transpose(0, 2, 1).reshape(devices * edges, 5)
    all_source = every[:, 3].reshape(-1).astype(jnp.int32)
    all_live = every[:, 5].reshape(-1)

    low = (all_source[:, None] % 32 == jnp.arange(32)[None]).astype(jnp.bfloat16)
    high = (all_source[None] // 32 == jnp.arange(-(-atoms // 32))[:, None]) & (all_live[None] > 0)
    counts = jnp.dot(
        high.astype(jnp.bfloat16), low, preferred_element_type=jnp.float32
    ).reshape(-1)[:atoms]
    atom_ids = jnp.arange(atoms)
    before = jnp.dot(
        (atom_ids[:, None] > atom_ids[None]).astype(jnp.float32), counts, precision=FULL
    )
    middle = (2.0 * before + counts).astype(jnp.int32)
    total = jnp.sum(counts).astype(jnp.int32)
    owner = jnp.minimum((middle * devices) // (2 * total), devices - 1)
    loads = jnp.sum(
        jnp.where(owner[None] == jnp.arange(devices)[:, None], counts[None], 0.0), axis=1
    )
    fits = jnp.max(loads) <= edges
    first_atom = jnp.sum(owner < me)
    last_atom = jnp.sum(owner <= me)
    mine = (all_live > 0) & (all_source >= first_atom) & (all_source < last_atom)
    flags = as_float(mine).reshape(-1, 128)
    tri = jnp.arange(128)
    inside = jnp.dot(flags, as_float(tri[:, None] <= tri[None]))
    row_ids = jnp.arange(flags.shape[0])
    row_sum = jnp.sum(flags, axis=1)
    offset = jnp.sum(
        jnp.where(row_ids[None] < row_ids[:, None], row_sum[None], 0.0), axis=1
    )
    rank = (inside + offset[:, None]).reshape(-1)
    slot_ids = jnp.arange(edges).astype(jnp.float32)
    index = jnp.sum((rank[None] <= slot_ids[:, None]).astype(jnp.float32), axis=1).astype(jnp.int32)
    valid = slot_ids < rank[-1]
    chosen = payload[jnp.minimum(index, devices * edges - 1)].T
    safe = jnp.asarray([1.5, 0.0, 0.0], jnp.float32)[:, None]
    my_vec = jnp.where(valid[None], chosen[:3], safe)
    my_source = jnp.where(valid, chosen[3], 0.0).astype(jnp.int32)
    my_target = jnp.where(valid, chosen[4], 0.0).astype(jnp.int32)
    my_live = as_float(valid)

    weights = (pair_in_weight, pair_out_weight, env_weight, scalar_weight, mix_weight[0], energy_head)
    slots = soap_weight.shape[0]
    kinds = jnp.arange(SPECIES, dtype=jnp.int32)[:, None]
    matrices_all = to_matrices(gather_blocks(soap_weight, block_owner, sizes))

    def run(vec, live, src, tgt, environ_of, hold):
        from_atom = (src[:, None] == atom_ids[None]).astype(jnp.float32)
        to_atom = (tgt[:, None] == atom_ids[None]).astype(jnp.float32)
        spec = (species[None] == kinds).astype(jnp.float32)
        species_source = dot(spec, from_atom, ((1,), (1,)), None)
        species_target = dot(spec, to_atom, ((1,), (1,)), None)
        ends = from_atom - to_atom

        def force_to_tangent(vec_bar):
            force = sum_small(nn(vec_bar, ends), sizes)
            residual = force - label_all[:3]
            loss = jnp.sum(label_mask[None] * residual * residual)
            cot = 2.0 * label_mask[None] * residual / label_total
            return nt(cot, ends), loss

        return chain(
            weights,
            lambda after: matrices_all,
            environ_of(from_atom),
            force_to_tangent,
            vec,
            live,
            species_source,
            species_target,
        )

    def environ_local(from_atom):
        same = dot(from_atom, from_atom, ((1,), (1,)), None)
        return lambda tensor: scale * nn(tensor.reshape(-1, edges), same).reshape(tensor.shape)

    def environ_global(from_atom):
        def apply(tensor):
            sums = lax.psum(nn(tensor.reshape(-1, edges), from_atom), AX)
            return scale * nt(sums, from_atom).reshape(tensor.shape)

        return apply

    def pack(out):
        return tuple(out[:6]) + (jnp.stack(out[6]), out[7])

    grads = lax.cond(
        fits,
        lambda: pack(run(my_vec, my_live, my_source, my_target, environ_local, None)),
        lambda: pack(run(edge_vec, as_float(edge_live), source, target, environ_global, None)),
    )
    pair_in_grad, pair_out_grad, env_grad, scalar_grad, mix_grad, head_grad = sum_large(
        grads[:6], sizes
    )
    own_grads = scatter_blocks(to_blocks(grads[6]), block_owner, sizes, slots)
    loss_sum = grads[7]
    new_pair_in = adamw(pair_in_weight, pair_in_first, pair_in_second, pair_in_grad)
    new_pair_out = adamw(pair_out_weight, pair_out_first, pair_out_second, pair_out_grad)
    new_env = adamw(env_weight, env_first, env_second, env_grad)
    new_scalar = adamw(scalar_weight, scalar_first, scalar_second, scalar_grad)
    new_mix = adamw(mix_weight, mix_first, mix_second, mix_grad[None])
    new_head = adamw(energy_head, head_first, head_second, head_grad)
    soap = jax.vmap(soap_slot)(
        own_grads,
        soap_weight,
        soap_first,
        soap_second,
        soap_left,
        soap_right,
        soap_lstat,
        soap_rstat,
        soap_average,
    )
    return (
        (loss_sum, label_total)
        + new_pair_in
        + new_pair_out
        + new_env
        + new_scalar
        + new_mix
        + new_head
        + tuple(soap)
    )


def solution(mesh):
    shared, split = P(), P(AX)
    column = P(None, AX)
    blocks = P(AX, None, None)
    placed = (
        (column, split, split, split, shared, column, split, shared) + (shared,) * 18 + (blocks,) * 8
    )
    return jax.shard_map(
        partial(local, (mesh.shape["irrep"], mesh.shape["edge"])),
        mesh=mesh,
        in_specs=placed,
        out_specs=(shared,) * 20 + (blocks,) * 8,
        check_vma=False,
    )
```

```python
from functools import partial
import math
from types import SimpleNamespace

import jax
import jax.numpy as jnp
import numpy as np
from jax import lax
from jax.experimental import pallas as pl
from jax.experimental.pallas import tpu as pltpu
from jax.sharding import PartitionSpec as P

D = 1024
NB = 8
SPECIES = 4
LAYERS = 2
BS = 128
NS_STEPS = 4
ADAM_STEP = 10
SIDE = D // BS
AX = ("irrep", "edge")

HIGH = lax.Precision.HIGH
FULL = lax.Precision.HIGHEST
CUTOFF = 5.0
ROOT_TWO = math.sqrt(2.0)
ROOT_THREE = math.sqrt(3.0)
ROOT_SIX = math.sqrt(6.0)
HARMONIC = math.sqrt(7.5)
RES = 1.0 / math.sqrt(2.0)


def shape_basis():
    return [
        np.array([[0.0, 1, 0], [1, 0, 0], [0, 0, 0]]) / ROOT_TWO,
        np.array([[0.0, 0, 0], [0, 0, 1], [0, 1, 0]]) / ROOT_TWO,
        np.array([[0.0, 0, 1], [0, 0, 0], [1, 0, 0]]) / ROOT_TWO,
        np.array([[1.0, 0, 0], [0, -1, 0], [0, 0, 0]]) / ROOT_TWO,
        np.array([[-1.0, 0, 0], [0, -1, 0], [0, 0, 2]]) / ROOT_SIX,
    ]


def cross_three(left_vec, right_vec):
    return np.array(
        [
            left_vec[1] * right_vec[2] - left_vec[2] * right_vec[1],
            left_vec[2] * right_vec[0] - left_vec[0] * right_vec[2],
            left_vec[0] * right_vec[1] - left_vec[1] * right_vec[0],
        ]
    )


def product_table():
    tensors = shape_basis()
    table = np.zeros((9, 9, 9))
    unit_rows = np.eye(9)
    for first in range(9):
        for second in range(9):
            left = unit_rows[first]
            right = unit_rows[second]
            left_mat = sum((left[4 + slot] * tensors[slot] for slot in range(5)))
            right_mat = sum((right[4 + slot] * tensors[slot] for slot in range(5)))
            left_vec = left[1:4]
            right_vec = right[1:4]
            scalar = left[0] * right[0] + left_vec @ right_vec + np.sum(left_mat * right_mat.T)
            vector = (
                left[0] * right_vec
                + right[0] * left_vec
                + cross_three(left_vec, right_vec)
                + left_mat @ right_vec
                + right_mat @ left_vec
            )
            matrix = (
                left[0] * right_mat
                + right[0] * left_mat
                + (np.outer(left_vec, right_vec) + np.outer(right_vec, left_vec)) / 2
                + (left_mat @ right_mat + right_mat @ left_mat) / 2
            )
            table[first, second, 0] = scalar
            table[first, second, 1:4] = vector
            for slot in range(5):
                table[first, second, 4 + slot] = np.sum(tensors[slot] * matrix)
    return (table / 3.0).astype(np.float32)


TABLE = product_table()
TERMS = [
    (a, b, k, float(TABLE[a, b, k]))
    for a in range(9)
    for b in range(9)
    for k in range(9)
    if abs(TABLE[a, b, k]) > 1e-7
]


def dot(left, right, dims, precision=HIGH):
    return lax.dot_general(left, right, ((dims[0], dims[1]), ((), ())), precision=precision)


def nn(left, right):
    return dot(left, right, ((1,), (0,)))


def tn(left, right):
    return dot(left, right, ((0,), (0,)))


def nt(left, right):
    return dot(left, right, ((1,), (1,)))


def device_of(y, x, z, core):
    return (y * 2 + x) * 8 + z * 2 + core


CUBE = [(y, x, z, c) for y in range(2) for x in range(2) for z in range(4) for c in range(2)]
HOP_X = [(device_of(y, x, z, c), device_of(y, 1 - x, z, c)) for y, x, z, c in CUBE]
HOP_Y = [(device_of(y, x, z, c), device_of(1 - y, x, z, c)) for y, x, z, c in CUBE]
HOP_XY = [(device_of(y, x, z, c), device_of(1 - y, 1 - x, z, c)) for y, x, z, c in CUBE]
HOP_CORE = [(device_of(y, x, z, c), device_of(y, x, z, 1 - c)) for y, x, z, c in CUBE]


def along_z(pairs):
    return [
        (device_of(y, x, s, c), device_of(y, x, t, c))
        for s, t in pairs
        for y in range(2)
        for x in range(2)
        for c in range(2)
    ]


HOP_IN = along_z([(0, 1), (3, 2)])
HOP_MID = along_z([(1, 2), (2, 1)])
HOP_OUT = along_z([(1, 0), (2, 3)])
HOP_Z = [along_z([(s, s ^ k) for s in range(4)]) for k in range(1, 4)]


def hop(value, pairs):
    return lax.ppermute(value, AX, pairs)


def place():
    irrep = lax.axis_index("irrep")
    edge = lax.axis_index("edge")
    return irrep // 2, irrep % 2, edge // 2, edge % 2


Z_ORDER = np.array([[3, 2, 1, 0], [3, 2, 0, 1], [0, 1, 3, 2], [0, 1, 2, 3]], np.int32)


def relative_devices():
    y, x, z, core = place()
    zs = jnp.asarray(Z_ORDER)[z]
    two = jnp.arange(2, dtype=jnp.int32)
    irrep = (two[None, :] ^ y) * 2 + (two[:, None] ^ x)
    return (
        irrep[None, :, :, None] * 8 + zs[:, None, None, None] * 2 + (two ^ core)[None, None, None, :]
    )


def reduce_chips(chunks):
    first, planes_done = [], []

    def second(p):
        (a0, a1), (b0, b1) = first[p]
        planes_done.append(
            jnp.concatenate([a0 + hop(a1, HOP_Y), b0 + hop(b1, HOP_X)], axis=0)
        )

    for p in range(4):
        block = chunks[p]
        if p >= 2:
            block, first[p - 2] = lax.optimization_barrier((block, first[p - 2]))
            second(p - 2)
        half = block.shape[2] // 2
        upper, lower = block[:, :, :half], block[:, :, half:]
        a = upper[0] + hop(upper[1], HOP_X)
        b = lower[:, 0] + hop(lower[:, 1], HOP_Y)
        first.append(((a[0], a[1]), (b[0], b[1])))
    second(2)
    second(3)
    q0, q1, q2, q3 = planes_done
    p0 = q0 + hop(q0, HOP_IN)
    p1 = q1 + hop(q1, HOP_IN)
    p2 = q2 + hop(p0, HOP_MID)
    return q3 + hop(q2, HOP_IN) + hop(p1, HOP_MID) + hop(p2, HOP_OUT), p2


def is_cube(sizes):
    return sizes == (4, 8)


def gather_small(value, sizes):
    if not is_cube(sizes):
        return lax.all_gather(value, AX, axis=0, tiled=False)
    y, x, z, core = place()
    plane = jnp.stack([value, hop(value, HOP_X), hop(value, HOP_Y), hop(value, HOP_XY)])
    column = jnp.stack([plane] + [hop(plane, pairs) for pairs in HOP_Z])
    every = jnp.stack([column, hop(column, HOP_CORE)])
    flat = every.reshape((32,) + value.shape)
    ids = np.arange(32, dtype=np.int32)
    core_of, z_of, x_of, y_of = ids % 2, ids // 2 % 4, ids // 8 % 2, ids // 16
    index = (core_of ^ core) * 16 + (z_of ^ z) * 4 + (y_of ^ y) * 2 + (x_of ^ x)
    return flat[index]


def sum_small(value, sizes):
    if not is_cube(sizes):
        return lax.psum(value, AX)
    total = value + hop(value, HOP_CORE)
    plane = total + hop(total, HOP_X) + (hop(total, HOP_Y) + hop(total, HOP_XY))
    one, two, three = [hop(plane, pairs) for pairs in HOP_Z]
    return (plane + one) + (two + three)


def geometry(vec, live):
    dist = jnp.sqrt(jnp.sum(vec * vec, axis=0))
    inv = 1.0 / dist
    unit = vec * inv[None]
    ratio = dist / CUTOFF
    r5 = ratio**5
    env = (1.0 - r5 * ratio * (28.0 - 48.0 * ratio + 21.0 * ratio * ratio)) * live
    denv = -(168.0 / CUTOFF) * r5 * (1.0 - ratio) * (1.0 - ratio) * live
    order = jnp.arange(1, NB + 1).astype(jnp.float32)[:, None] * (math.pi / CUTOFF)
    angle = order * dist[None]
    norm = math.sqrt(2.0 / CUTOFF)
    bessel = norm * jnp.sin(angle) * inv[None]
    dbessel = norm * order * jnp.cos(angle) * inv[None] - bessel * inv[None]
    return inv, unit, env, denv, bessel, dbessel


def harmonics(unit):
    x, y, z = unit
    h = HARMONIC
    return jnp.stack(
        [
            jnp.ones_like(x),
            ROOT_THREE * x,
            ROOT_THREE * y,
            ROOT_THREE * z,
            h * ROOT_TWO * x * y,
            h * ROOT_TWO * y * z,
            h * ROOT_TWO * x * z,
            h * (x * x - y * y) / ROOT_TWO,
            h * (2.0 * z * z - x * x - y * y) / ROOT_SIX,
        ]
    )


def harmonics_dot(unit, dunit):
    x, y, z = unit
    dx, dy, dz = dunit
    h = HARMONIC
    return jnp.stack(
        [
            jnp.zeros_like(x),
            ROOT_THREE * dx,
            ROOT_THREE * dy,
            ROOT_THREE * dz,
            h * ROOT_TWO * (dx * y + x * dy),
            h * ROOT_TWO * (dy * z + y * dz),
            h * ROOT_TWO * (dx * z + x * dz),
            h * ROOT_TWO * (x * dx - y * dy),
            (2.0 * h / ROOT_SIX) * (2.0 * z * dz - x * dx - y * dy),
        ]
    )


def harmonics_back(unit, bar):
    x, y, z = unit
    a, b = HARMONIC * ROOT_TWO, 2.0 * HARMONIC / ROOT_SIX
    return jnp.stack(
        [
            ROOT_THREE * bar[1] + a * (y * bar[4] + z * bar[6] + x * bar[7]) - b * x * bar[8],
            ROOT_THREE * bar[2] + a * (x * bar[4] + z * bar[5] - y * bar[7]) - b * y * bar[8],
            ROOT_THREE * bar[3] + a * (y * bar[5] + x * bar[6]) + 2.0 * b * z * bar[8],
        ]
    )


def silu(v):
    return v * jax.nn.sigmoid(v)


def silu_one(v):
    s = jax.nn.sigmoid(v)
    return s * (1.0 + v * (1.0 - s))


def silu_two(v):
    s = jax.nn.sigmoid(v)
    return s * (1.0 - s) * (2.0 + v * (1.0 - 2.0 * s))


def bilinear(sets, out, size):
    total = [None] * size
    for index in TERMS:
        a, b, k, value = index
        slot = index[out]
        for (li, left), (ri, right) in sets:
            term = left[index[li]] * right[index[ri]]
            term = value * term
            total[slot] = term if total[slot] is None else total[slot] + term
    return jnp.stack(total)


def product(feature, environ):
    return bilinear([((0, feature), (1, environ))], 2, 9)


def mix(mixing, tensor, transposed):
    op = tn if transposed else nn
    out = []
    for order, (start, stop) in enumerate(((0, 1), (1, 4), (4, 9))):
        for k in range(start, stop):
            out.append(op(mixing[order], tensor[k]))
    return jnp.stack(out)


def mix_gradient(left, right):
    out = []
    for start, stop in ((0, 1), (1, 4), (4, 9)):
        out.append(sum(nt(left[k], right[k]) for k in range(start, stop)))
    return out


def chain(weights, load_matrices, environ, force_to_tangent, vec, live, species_source, species_target):
    pair_in, pair_out, env_weight, scalar_weight, mix_weight, energy_head = weights
    head = energy_head[:D]
    factor = jnp.sum(
        energy_head[D:, None] * species_source, axis=0
    )
    inv, unit, env, denv, bessel, dbessel = geometry(vec, live)
    shape = harmonics(unit)
    feat = jnp.concatenate([bessel, species_source, species_target], axis=0)
    col = lambda v: v[:, None]
    pre0 = tn(feat, pair_in)
    hid = silu(pre0)
    out0 = nn(hid, pair_out)
    lat0 = col(env) * out0
    w0 = nt(env_weight[0], lat0)
    emb0 = shape[:, None] * w0[None]
    env0 = environ(emb0)
    res0 = product(emb0, env0)
    matrices = load_matrices(res0)
    pre1 = nn(lat0, matrices[0]) + tn(res0[0], scalar_weight[0])
    act1 = silu(pre1)
    out1 = nn(act1, matrices[1])
    lat1 = (lat0 + col(env) * out1) * RES
    w1 = nt(env_weight[1], lat1)
    emb1 = shape[:, None] * w1[None]
    env1 = environ(emb1)
    feat1 = mix(mix_weight, res0, False)
    res1 = jnp.sum(feat1 * env1, axis=0) / 3.0
    pre2 = nn(lat1, matrices[2]) + tn(res1, scalar_weight[1])
    act2 = silu(pre2)
    top = dot(matrices[3], head, ((1,), (0,)))
    slope = env * factor
    per1 = jnp.sum(lat1 * head[None], axis=1)
    per2 = jnp.sum(act2 * top[None], axis=1)
    env_bar = RES * factor * (per1 + 2.0 * env * per2)
    alpha = RES * slope
    lead = alpha * env
    slope2 = silu_one(pre2)
    pre2_bar = col(lead) * top[None] * slope2
    lat1_bar = col(alpha) * head[None] + nt(pre2_bar, matrices[2])
    res1_bar = nt(scalar_weight[1], pre2_bar)
    feat1_bar = res1_bar[None] * env1 / 3.0
    emb1_bar = environ(res1_bar[None] * feat1 / 3.0)
    shape_bar = jnp.sum(emb1_bar * w1[None], axis=1)
    w1_bar = jnp.sum(shape[:, None] * emb1_bar, axis=0)
    lat1_bar = lat1_bar + tn(w1_bar, env_weight[1])
    res0_bar = mix(mix_weight, feat1_bar, True)
    env_bar = env_bar + RES * jnp.sum(lat1_bar * out1, axis=1)
    out1_bar = RES * col(env) * lat1_bar
    act1_bar = nt(out1_bar, matrices[1])
    slope1 = silu_one(pre1)
    pre1_bar = act1_bar * slope1
    lat0_bar = RES * lat1_bar + nt(pre1_bar, matrices[0])
    res0_bar = res0_bar.at[0].add(nt(scalar_weight[0], pre1_bar))
    emb0_bar = bilinear([((2, res0_bar), (1, env0))], 0, 9) + environ(
        bilinear([((2, res0_bar), (0, emb0))], 1, 9)
    )
    shape_bar = shape_bar + jnp.sum(emb0_bar * w0[None], axis=1)
    w0_bar = jnp.sum(shape[:, None] * emb0_bar, axis=0)
    lat0_bar = lat0_bar + tn(w0_bar, env_weight[0])
    env_bar = env_bar + jnp.sum(lat0_bar * out0, axis=1)
    out0_bar = col(env) * lat0_bar
    hid_bar = nt(out0_bar, pair_out)
    slope0 = silu_one(pre0)
    pre0_bar = hid_bar * slope0
    bessel_bar = nt(pair_in[:NB], pre0_bar)
    dist_bar = env_bar * denv + jnp.sum(bessel_bar * dbessel, axis=0)
    unit_bar = harmonics_back(unit, shape_bar)
    along = jnp.sum(unit * unit_bar, axis=0)
    vec_bar = dist_bar[None] * unit + (unit_bar - unit * along[None]) * inv[None]
    vec_dot, loss_parts = force_to_tangent(vec_bar)
    dist_dot = jnp.sum(unit * vec_dot, axis=0)
    unit_dot = (vec_dot - unit * dist_dot[None]) * inv[None]
    env_dot = denv * dist_dot
    bessel_dot = dbessel * dist_dot[None]
    shape_dot = harmonics_dot(unit, unit_dot)
    pre0_dot = tn(bessel_dot, pair_in[:NB])
    hid_dot = slope0 * pre0_dot
    lat0_dot = col(env_dot) * out0 + col(env) * nn(hid_dot, pair_out)
    w0_dot = nt(env_weight[0], lat0_dot)
    emb0_dot = shape_dot[:, None] * w0[None] + shape[:, None] * w0_dot[None]
    env0_dot = environ(emb0_dot)
    res0_dot = bilinear(
        [((0, emb0_dot), (1, env0)), ((0, emb0), (1, env0_dot))], 2, 9
    )
    pre1_dot = nn(lat0_dot, matrices[0]) + tn(res0_dot[0], scalar_weight[0])
    act1_dot = slope1 * pre1_dot
    lat1_dot = (lat0_dot + col(env_dot) * out1 + col(env) * nn(act1_dot, matrices[1])) * RES
    w1_dot = nt(env_weight[1], lat1_dot)
    emb1_dot = shape_dot[:, None] * w1[None] + shape[:, None] * w1_dot[None]
    env1_dot = environ(emb1_dot)
    feat1_dot = mix(mix_weight, res0_dot, False)
    res1_dot = jnp.sum(feat1_dot * env1 + feat1 * env1_dot, axis=0) / 3.0
    pre2_dot = nn(lat1_dot, matrices[2]) + tn(res1_dot, scalar_weight[1])
    act2_dot = slope2 * pre2_dot
    lead_dot = 2.0 * RES * slope * env_dot
    last = jnp.sum(col(lead_dot) * act2 + col(lead) * act2_dot, axis=0)
    head_grad = RES * jnp.sum(
        col(factor * env_dot) * lat1 + col(slope) * lat1_dot, axis=0
    ) + jnp.sum(last[:, None] * matrices[3], axis=0)
    per1_dot = jnp.sum(lat1_dot * head[None], axis=1)
    per2_dot = jnp.sum(act2_dot * top[None], axis=1)
    energy_dot = env_dot * RES * (per1 + env * per2) + env * RES * (
        per1_dot + env_dot * per2 + env * per2_dot
    )
    scale_grad = jnp.sum(species_source * energy_dot[None], axis=1)
    head_grad = jnp.concatenate([head_grad, scale_grad])
    pre2_hat = top[None] * (col(lead_dot) * slope2 + col(lead) * silu_two(pre2) * pre2_dot)
    lat1_hat = col(RES * factor * env_dot) * head[None] + nt(pre2_hat, matrices[2])
    res1_hat = nt(scalar_weight[1], pre2_hat)
    feat1_hat = (res1_hat[None] * env1 + res1_bar[None] * env1_dot) / 3.0
    emb1_hat = environ((res1_hat[None] * feat1 + res1_bar[None] * feat1_dot) / 3.0)
    w1_hat = jnp.sum(shape_dot[:, None] * emb1_bar + shape[:, None] * emb1_hat, axis=0)
    lat1_hat = lat1_hat + tn(w1_hat, env_weight[1])
    res0_hat = mix(mix_weight, feat1_hat, True)
    out1_hat = RES * (col(env_dot) * lat1_bar + col(env) * lat1_hat)
    act1_hat = nt(out1_hat, matrices[1])
    pre1_hat = act1_hat * slope1 + act1_bar * silu_two(pre1) * pre1_dot
    lat0_hat = RES * lat1_hat + nt(pre1_hat, matrices[0])
    res0_hat = res0_hat.at[0].add(nt(scalar_weight[0], pre1_hat))
    emb0_hat = bilinear(
        [((2, res0_hat), (1, env0)), ((2, res0_bar), (1, env0_dot))], 0, 9
    ) + environ(bilinear([((2, res0_hat), (0, emb0)), ((2, res0_bar), (0, emb0_dot))], 1, 9))
    w0_hat = jnp.sum(shape_dot[:, None] * emb0_bar + shape[:, None] * emb0_hat, axis=0)
    lat0_hat = lat0_hat + tn(w0_hat, env_weight[0])
    out0_hat = col(env_dot) * lat0_bar + col(env) * lat0_hat
    pre0_hat = nt(out0_hat, pair_out) * slope0 + hid_bar * silu_two(pre0) * pre0_dot
    both = lambda first, second: jnp.concatenate([first, second], axis=0)
    pair_in_grad = nn(feat, pre0_hat)
    pair_in_grad = pair_in_grad.at[:NB].add(nn(bessel_dot, pre0_bar))
    mix_grad = jnp.stack(
        [
            first + second
            for first, second in zip(
                mix_gradient(feat1_bar, res0_dot), mix_gradient(feat1_hat, res0)
            )
        ]
    )
    env_grad = jnp.stack(
        [nn(w0_bar, lat0_dot) + nn(w0_hat, lat0), nn(w1_bar, lat1_dot) + nn(w1_hat, lat1)]
    )
    scalar_grad = jnp.stack(
        [
            nn(res0_dot[0], pre1_bar) + nn(res0[0], pre1_hat),
            nn(res1_dot, pre2_bar) + nn(res1, pre2_hat),
        ]
    )
    pair_out_grad = tn(both(hid_dot, hid), both(out0_bar, out0_hat))
    matrix_grad = [
        tn(both(lat0_dot, lat0), both(pre1_bar, pre1_hat)),
        tn(both(act1_dot, act1), both(out1_bar, out1_hat)),
        tn(both(lat1_dot, lat1), both(pre2_bar, pre2_hat)),
        last[:, None] * head[None],
    ]
    return (
        pair_in_grad,
        pair_out_grad,
        env_grad,
        scalar_grad,
        mix_grad,
        head_grad,
        matrix_grad,
        loss_parts,
    )


def split(v):
    high = v.astype(jnp.bfloat16)
    return high, (v - high.astype(jnp.float32)).astype(jnp.bfloat16)


def split_outside(v):
    high = lax.reduce_precision(v, exponent_bits=8, mantissa_bits=7)
    return high.astype(jnp.bfloat16), (v - high).astype(jnp.bfloat16)


def one_pass(left, right, dims=((1,), (0,))):
    return lax.dot_general(left, right, (dims, ((), ())), preferred_element_type=jnp.float32)


def three_pass(left, right, dims=((1,), (0,))):
    lh, ll = left
    rh, rl = right
    return one_pass(lh, rh, dims) + (one_pass(lh, rl, dims) + one_pass(ll, rh, dims))


NT = ((1,), (1,))


def kernel_call(
    body,
    ins,
    outs,
    scratch,
    late=None,
    sent=None,
    hbm=None,
    smem=None,
    hbm_out=None,
    flops=0,
    limit=60,
):
    late, sent, hbm, smem, hbm_out = late or {}, sent or {}, hbm or {}, smem or {}, hbm_out or {}
    leaves, tree = jax.tree.flatten((ins, smem, hbm, late))
    out_leaves, out_tree = jax.tree.flatten((outs, hbm_out, sent))
    buffers = jax.tree.map(lambda v: pltpu.VMEM(v.shape, v.dtype), (late, sent))
    late_count, sent_count = len(jax.tree.leaves(late)), len(jax.tree.leaves(sent))
    own = (scratch, buffers)
    own_leaves, own_tree = jax.tree.flatten(own)

    def kernel(*refs):
        n, m = len(leaves), len(leaves) + len(out_leaves)
        given = jax.tree.unflatten(tree, refs[:n])
        made = jax.tree.unflatten(out_tree, refs[n:m])
        temps, (landed, leaving) = jax.tree.unflatten(own_tree, refs[m : m + len(own_leaves)])
        sems = refs[m + len(own_leaves) :]
        r = SimpleNamespace(
            **given[0], **given[1], **given[2], **made[0], **made[1], **temps, **landed, **leaving
        )
        coming, going, started = {}, {}, []
        index = 0
        for name in sorted(late):
            sources, targets = jax.tree.leaves(given[3][name]), jax.tree.leaves(landed[name])
            coming[id(landed[name])] = []
            for source, target in zip(sources, targets):
                coming[id(landed[name])].append(
                    pltpu.make_async_copy(source, target, sems[0].at[index])
                )
                index += 1
        index = 0
        for name in sorted(sent):
            sources, targets = jax.tree.leaves(leaving[name]), jax.tree.leaves(made[2][name])
            going[id(leaving[name])] = []
            for source, target in zip(sources, targets):
                going[id(leaving[name])].append(
                    pltpu.make_async_copy(source, target, sems[1].at[index])
                )
                index += 1

        def fetch(*items):
            for item in items:
                for copy in coming[id(item)]:
                    copy.start()

        def need(*items):
            for item in items:
                for copy in coming[id(item)]:
                    copy.wait()

        def send(*items):
            for item in items:
                for copy in going[id(item)]:
                    copy.start()
                    started.append(copy)

        r.fetch, r.need, r.send = fetch, need, send
        body(r)
        for copy in started:
            copy.wait()
        assert len(started) == sent_count

    vmem, hbm_spec = pl.BlockSpec(memory_space=pltpu.VMEM), pl.BlockSpec(memory_space=pl.ANY)
    count = lambda v: len(jax.tree.leaves(v))
    in_specs = [vmem] * count(ins) + [pl.BlockSpec(memory_space=pltpu.SMEM)] * count(smem)
    in_specs += [hbm_spec] * (count(hbm) + count(late))
    out_specs = [vmem] * count(outs) + [hbm_spec] * (count(hbm_out) + count(sent))
    size = sum(v.size * v.dtype.itemsize for v in leaves + out_leaves)
    result = pl.pallas_call(
        kernel,
        out_shape=out_leaves,
        in_specs=in_specs,
        out_specs=out_specs,
        scratch_shapes=own_leaves
        + [pltpu.SemaphoreType.DMA((max(late_count, 1),)), pltpu.SemaphoreType.DMA((max(sent_count, 1),))],
        compiler_params=pltpu.CompilerParams(vmem_limit_bytes=limit * 2**20),
        cost_estimate=pl.CostEstimate(flops=flops, bytes_accessed=size, transcendentals=0),
    )(*leaves)
    made = jax.tree.unflatten(out_tree, result)
    return SimpleNamespace(**made[0], **made[1], **made[2])


def f32(*shape):
    return jax.ShapeDtypeStruct(shape, jnp.float32)


def b16(*shape):
    return jax.ShapeDtypeStruct(shape, jnp.bfloat16)


def pair_of(*shape):
    return (b16(*shape), b16(*shape))


def pair(refs, rows=None):
    high, low = refs
    return (high[...], low[...]) if rows is None else (high[rows, :], low[rows, :])


def put(refs, rows, value):
    high, low = split(value)
    refs[0][rows, :] = high
    refs[1][rows, :] = low


HALF = D // 2


class Stream:
    def __init__(self, r, sources):
        self.r, self.sources, self.step = r, sources, 0
        self.copies(0, True)

    def copies(self, step, start):
        rows = pl.ds((step % 2) * HALF, HALF)
        refs, index = self.sources[step // 2]
        for part, ref in enumerate(refs):
            view = ref.at[rows, :] if index is None else ref.at[index, rows, :]
            copy = pltpu.make_async_copy(
                view, self.r.held.at[step % 2, part], self.r.arrived.at[step % 2, part]
            )
            copy.start() if start else copy.wait()

    def product(self, right, store, extra=None):
        held = self.r.held
        for half in range(2):
            step = self.step
            self.step += 1
            if step + 1 < 2 * len(self.sources):
                self.copies(step + 1, True)
            self.copies(step, False)
            rows = pl.ds(half * HALF, HALF)
            acc = three_pass((held[half, 0], held[half, 1]), pair(right))
            if extra is not None:
                acc = acc + three_pass(pair(extra[0], rows), extra[1])
            store[rows, :] = acc


def stream_scratch():
    return dict(
        held=pltpu.VMEM((2, 2, HALF, D), jnp.bfloat16),
        arrived=pltpu.SemaphoreType.DMA((2, 2)),
    )


def each(body, carry=(), step=128, count=D):
    def run(i, state):
        return body(pl.ds(pl.multiple_of(i * step, step), step), *state)

    return lax.fori_loop(0, count // step, run, carry)


def fold(v):
    return jnp.sum(v.reshape(v.shape[0] // 8, 8, v.shape[1]), axis=0)


def planes(channels, edges, body):
    lanes = edges // 128

    def run(i, state):
        base = pl.multiple_of((i // lanes) * 16, 16)
        lane = pl.ds(pl.multiple_of((i % lanes) * 128, 128), 128)
        body(base, lane)
        return state

    lax.fori_loop(0, (channels // 16) * lanes, run, 0)


def get9(ref, channels, base, lane):
    return [ref[pl.ds(k * channels + base, 16), lane] for k in range(9)]


def put9(ref, channels, base, lane, values):
    for k, v in enumerate(values):
        ref[pl.ds(k * channels + base, 16), lane] = v


def put9_split(r, channels, base, lane, values):
    for k, v in enumerate(values):
        high, low = split(v)
        r.t_h[pl.ds(k * channels + base, 16), lane] = high
        r.t_l[pl.ds(k * channels + base, 16), lane] = low


def row9(ref, lane):
    return [ref[k : k + 1, lane] for k in range(9)]


def terms_sum(sets, out):
    total = [None] * 9
    pairs = {}
    for index in TERMS:
        for n, ((li, left), (ri, right)) in enumerate(sets):
            key = (n, index[li], index[ri])
            if key not in pairs:
                pairs[key] = left[index[li]] * right[index[ri]]
    for index in TERMS:
        for n, ((li, left), (ri, right)) in enumerate(sets):
            term = index[3] * pairs[(n, index[li], index[ri])]
            slot = index[out]
            total[slot] = term if total[slot] is None else total[slot] + term
    return total


TILE9 = 192


def same_atom(r, scale, store, rows9):
    @pl.loop(0, rows9 // TILE9)
    def _(t):
        rows = pl.ds(pl.multiple_of(t * TILE9, TILE9), TILE9)
        store[rows, :] = scale * (
            one_pass(r.t_h[rows, :], r.same[...]) + one_pass(r.t_l[rows, :], r.same[...])
        )


def mixed(r, mixing, store, rows9):
    @pl.loop(0, rows9 // TILE9)
    def _(t):
        rows = pl.ds(pl.multiple_of(t * TILE9, TILE9), TILE9)
        store[rows, :] = three_pass(pair(mixing, rows), (r.t_h[...], r.t_l[...]))


def clear_tail(r, rows9):
    tail = r.t_h.shape[0] - rows9
    r.t_h[rows9:, :] = jnp.zeros((tail, r.t_h.shape[1]), jnp.bfloat16)
    r.t_l[rows9:, :] = jnp.zeros((tail, r.t_l.shape[1]), jnp.bfloat16)


def plane_scratch(rows9, edges):
    depth = -(-rows9 // 128) * 128
    return dict(
        t_h=pltpu.VMEM((depth, edges), jnp.bfloat16), t_l=pltpu.VMEM((depth, edges), jnp.bfloat16)
    )


def sig(v):
    return 1.0 / (1.0 + jnp.exp(-v))


def silu_parts(v):
    s = sig(v)
    return v * s, s * (1.0 + v * (1.0 - s))


def silu_slopes(v):
    s = sig(v)
    t = 1.0 - s
    return s * (1.0 + v * t), s * t * (2.0 + v * (t - s))


def first_layer(r, channels, edges, scale):
    rows9 = 9 * channels
    stream = Stream(r, [(r.out_t, None)])
    feat = split(r.feat[...])

    @pl.loop(0, 2)
    def _(t):
        rows = pl.ds(pl.multiple_of(t * 512, 512), 512)
        r.pre0[rows, :] = three_pass(pair(r.in_t, rows), feat)

    def hidden(rows):
        put(r.hid, rows, silu_parts(r.pre0[rows, :])[0])
        return ()

    r.send(r.pre0)
    each(hidden)
    r.send(r.hid)
    stream.product(r.hid, r.out0)

    def latent(rows):
        put(r.lat0, rows, r.rows[0:1, :] * r.out0[rows, :])
        return ()

    r.send(r.out0)
    each(latent)
    r.send(r.lat0)
    r.w0[...] = three_pass(pair(r.env0w), pair(r.lat0))

    def embed(base, lane):
        w = r.w0[pl.ds(base, 16), lane]
        put9_split(r, channels, base, lane, [y * w for y in row9(r.shape, lane)])

    planes(channels, edges, embed)
    same_atom(r, scale, r.env0, rows9)
    r.send(r.env0)

    def multiply(base, lane):
        w = r.w0[pl.ds(base, 16), lane]
        emb = [y * w for y in row9(r.shape, lane)]
        env = get9(r.env0, channels, base, lane)
        put9(r.res0, channels, base, lane, terms_sum([((0, emb), (1, env))], 2))

    planes(channels, edges, multiply)
    r.send(r.res0)


def energy_up(r, channels, edges, scale):
    rows9 = 9 * channels
    env, factor = lambda: r.rows[0:1, :], lambda: r.rows[1:2, :]
    alpha = lambda: RES * r.rows[0:1, :] * r.rows[1:2, :]
    stream = Stream(
        r,
        [
            (r.mt, 0),
            (r.mt, 1),
            (r.mt, 2),
        ],
    )
    r.fetch(r.out0, r.mix)
    clear_tail(r, rows9)
    nothing = jnp.zeros((8, edges), jnp.float32)
    stream.product(r.lat0, r.pre1, (r.sc0_t, split(r.res0[0:channels, :])))

    def act1(rows):
        put(r.act1, rows, silu_parts(r.pre1[rows, :])[0])
        return ()

    r.send(r.pre1)
    each(act1)
    r.send(r.act1)
    stream.product(r.act1, r.out1)

    def lat1(rows, per):
        value = RES * env() * (r.out0[rows, :] + r.out1[rows, :])
        put(r.lat1, rows, value)
        return (per + fold(value * r.head[rows, :]),)

    r.send(r.out1)
    r.need(r.out0)
    (per1,) = each(lat1, (nothing,))
    r.send(r.lat1)
    r.w1[...] = three_pass(pair(r.env1w), pair(r.lat1))

    def embed(base, lane):
        w = r.w1[pl.ds(base, 16), lane]
        put9_split(r, channels, base, lane, [y * w for y in row9(r.shape, lane)])

    planes(channels, edges, embed)
    same_atom(r, scale, r.env1, rows9)
    r.send(r.env1)

    def take(base, lane):
        put9_split(r, channels, base, lane, get9(r.res0, channels, base, lane))

    planes(channels, edges, take)
    r.need(r.mix)
    mixed(r, r.mix, r.feat1, rows9)
    r.send(r.feat1)

    def scalar(base, lane):
        f, e = get9(r.feat1, channels, base, lane), get9(r.env1, channels, base, lane)
        r.res1[pl.ds(base, 16), lane] = sum(a * b for a, b in zip(f, e)) * (1.0 / 3.0)

    planes(channels, edges, scalar)
    stream.product(r.lat1, r.pre2, (r.sc1_t, split(r.res1[...])))

    def act2(rows, per):
        act, slope = silu_parts(r.pre2[rows, :])
        put(r.pre2_bar, rows, (alpha() * env()) * r.top[rows, :] * slope)
        return (per + fold(act * r.top[rows, :]),)

    r.send(r.pre2)
    (per2,) = each(act2, (nothing,))
    r.send(r.pre2_bar)
    per1 = jnp.sum(per1, axis=0, keepdims=True)
    per2 = jnp.sum(per2, axis=0, keepdims=True)
    r.per[...] = jnp.zeros_like(r.per)
    r.per[0:1, :] = per1
    r.per[1:2, :] = per2


def energy_down(r, channels, edges, scale):
    rows9 = 9 * channels
    env, factor = lambda: r.rows[0:1, :], lambda: r.rows[1:2, :]
    alpha = lambda: RES * r.rows[0:1, :] * r.rows[1:2, :]
    stream = Stream(r, [(r.m, 2), (r.m, 1), (r.m, 0), (r.out, None)])
    r.fetch(r.feat1, r.env1)
    clear_tail(r, rows9)
    nothing = jnp.zeros((8, edges), jnp.float32)
    stream.product(r.pre2_bar, r.lat1_bar)
    r.fetch(r.out1, r.mix_t, r.pre1)
    r.need(r.feat1, r.env1)
    r.res1_bar[...] = three_pass(pair(r.sc1), pair(r.pre2_bar))

    def back1(base, lane):
        g = r.res1_bar[pl.ds(base, 16), lane] * (1.0 / 3.0)
        put9_split(r, channels, base, lane, [g * f for f in get9(r.feat1, channels, base, lane)])
        put9(r.feat1_bar, channels, base, lane, [g * e for e in get9(r.env1, channels, base, lane)])

    planes(channels, edges, back1)
    r.send(r.feat1_bar)
    same_atom(r, scale, r.emb1_bar, rows9)
    r.send(r.emb1_bar)
    r.shape_bar[...] = jnp.zeros_like(r.shape_bar)

    def collect(w_ref, emb_ref, out_ref):
        def run(base, lane):
            w = w_ref[pl.ds(base, 16), lane]
            emb = get9(emb_ref, channels, base, lane)
            out_ref[pl.ds(base, 16), lane] = sum(y * v for y, v in zip(row9(r.shape, lane), emb))
            for k in range(9):
                r.shape_bar[k : k + 1, lane] += jnp.sum(emb[k] * w, axis=0, keepdims=True)

        planes(channels, edges, run)

    collect(r.w1, r.emb1_bar, r.w1_bar)
    w_pair = split(r.w1_bar[...])

    @pl.loop(0, 2)
    def _(t):
        rows = pl.ds(pl.multiple_of(t * 512, 512), 512)
        r.lat1_bar[rows, :] += three_pass(pair(r.env1w_t, rows), w_pair)

    def out1_bar(rows, total):
        value = r.lat1_bar[rows, :] + alpha() * r.head[rows, :]
        r.lat1_bar[rows, :] = value
        put(r.out1_bar, rows, (RES * env()) * value)
        return (total + fold(value * r.out1[rows, :]),)

    r.need(r.out1)
    (env_bar1,) = each(out1_bar, (nothing,))
    r.send(r.lat1_bar, r.out1_bar)
    r.fetch(r.env0, r.out0)
    stream.product(r.out1_bar, r.act1_bar)
    r.send(r.act1_bar)
    r.need(r.mix_t)

    def take_bar(base, lane):
        put9_split(r, channels, base, lane, get9(r.feat1_bar, channels, base, lane))

    planes(channels, edges, take_bar)
    mixed(r, r.mix_t, r.res0_bar, rows9)

    def pre1_bar(rows):
        put(r.pre1_bar, rows, r.act1_bar[rows, :] * silu_parts(r.pre1[rows, :])[1])
        return ()

    r.need(r.pre1)
    each(pre1_bar)
    r.send(r.pre1_bar)
    stream.product(r.pre1_bar, r.lat0_bar)
    r.res0_bar[0:channels, :] += three_pass(pair(r.sc0), pair(r.pre1_bar))
    r.send(r.res0_bar)
    r.fetch(r.pre0)

    def back0(base, lane):
        w = r.w0[pl.ds(base, 16), lane]
        emb = [y * w for y in row9(r.shape, lane)]
        g = get9(r.res0_bar, channels, base, lane)
        put9_split(r, channels, base, lane, terms_sum([((2, g), (0, emb))], 1))

    planes(channels, edges, back0)
    same_atom(r, scale, r.emb0_bar, rows9)

    def back0_feature(base, lane):
        g = get9(r.res0_bar, channels, base, lane)
        e = get9(r.env0, channels, base, lane)
        more = terms_sum([((2, g), (1, e))], 0)
        have = get9(r.emb0_bar, channels, base, lane)
        put9(r.emb0_bar, channels, base, lane, [a + b for a, b in zip(have, more)])

    r.need(r.env0)
    planes(channels, edges, back0_feature)
    r.send(r.emb0_bar)
    collect(r.w0, r.emb0_bar, r.w0_bar)
    w_pair0 = split(r.w0_bar[...])

    @pl.loop(0, 2)
    def _(t):
        rows = pl.ds(pl.multiple_of(t * 512, 512), 512)
        r.lat0_bar[rows, :] += three_pass(pair(r.env0w_t, rows), w_pair0)

    def out0_bar(rows, total):
        value = r.lat0_bar[rows, :] + RES * r.lat1_bar[rows, :]
        r.lat0_bar[rows, :] = value
        put(r.out0_bar, rows, env() * value)
        return (total + fold(value * r.out0[rows, :]),)

    r.need(r.out0)
    (env_bar0,) = each(out0_bar, (nothing,))
    r.send(r.lat0_bar, r.out0_bar)
    stream.product(r.out0_bar, r.hid_bar)

    def pre0_bar(rows):
        put(r.pre0_bar, rows, r.hid_bar[rows, :] * silu_parts(r.pre0[rows, :])[1])
        return ()

    r.send(r.hid_bar)
    r.need(r.pre0)
    each(pre0_bar)
    r.send(r.pre0_bar)
    r.bessel_bar[...] = three_pass(pair(r.in_w), pair(r.pre0_bar))
    down = lambda v: jnp.sum(v, axis=0, keepdims=True)
    r.env_bar[...] = jnp.zeros_like(r.env_bar)
    r.env_bar[0:1, :] = (
        RES * factor() * (r.per[0:1, :] + 2.0 * env() * r.per[1:2, :])
        + RES * down(env_bar1)
        + down(env_bar0)
    )


def tangent_up(r, channels, edges, scale):
    rows9 = 9 * channels
    env, factor, env_dot = (
        lambda: r.rows[0:1, :],
        lambda: r.rows[1:2, :],
        lambda: r.rows[2:3, :],
    )
    lead = lambda: RES * env() * env() * factor()
    lead_dot = lambda: 2.0 * RES * env() * factor() * env_dot()
    stream = Stream(
        r,
        [
            (r.out_t, None),
            (r.mt, 0),
            (r.mt, 1),
            (r.mt, 2),
        ],
    )
    r.fetch(r.pre0, r.out0)
    clear_tail(r, rows9)
    nothing = jnp.zeros((8, edges), jnp.float32)
    bessel = split(r.bessel_dot[...])

    @pl.loop(0, 2)
    def _(t):
        rows = pl.ds(pl.multiple_of(t * 512, 512), 512)
        r.pre0_dot[rows, :] = three_pass(pair(r.in_t, rows), bessel)

    def hidden(rows):
        put(r.hid_dot, rows, r.pre0_dot[rows, :] * silu_parts(r.pre0[rows, :])[1])
        return ()

    r.send(r.pre0_dot)
    r.need(r.pre0)
    each(hidden)
    r.send(r.hid_dot)
    r.fetch(r.env0)
    stream.product(r.hid_dot, r.tmp)

    def lat0(rows):
        value = env_dot() * r.out0[rows, :] + env() * r.tmp[rows, :]
        r.keep[rows, :] = value
        put(r.lat0_dot, rows, value)
        return ()

    r.need(r.out0)
    each(lat0)
    r.send(r.lat0_dot)
    r.fetch(r.pre1, r.out1)
    r.w0_dot[...] = three_pass(pair(r.env0w), pair(r.lat0_dot))

    def embed_dot(w_ref, w_dot_ref, base, lane):
        w, wd = w_ref[pl.ds(base, 16), lane], w_dot_ref[pl.ds(base, 16), lane]
        return [
            yd * w + y * wd for y, yd in zip(row9(r.shape, lane), row9(r.shape_dot, lane))
        ]

    def embed0(base, lane):
        put9_split(r, channels, base, lane, embed_dot(r.w0, r.w0_dot, base, lane))

    planes(channels, edges, embed0)
    same_atom(r, scale, r.env0_dot, rows9)
    r.send(r.env0_dot)
    r.need(r.env0)

    def multiply(base, lane):
        w = r.w0[pl.ds(base, 16), lane]
        emb = [y * w for y in row9(r.shape, lane)]
        emb_dot = embed_dot(r.w0, r.w0_dot, base, lane)
        e, ed = get9(r.env0, channels, base, lane), get9(r.env0_dot, channels, base, lane)
        put9(
            r.res0_dot,
            channels,
            base,
            lane,
            terms_sum([((0, emb_dot), (1, e)), ((0, emb), (1, ed))], 2),
        )

    planes(channels, edges, multiply)
    r.send(r.res0_dot)
    r.fetch(r.lat1, r.mix)
    stream.product(r.lat0_dot, r.pre1_dot, (r.sc0_t, split(r.res0_dot[0:channels, :])))

    def act1(rows):
        put(r.act1_dot, rows, r.pre1_dot[rows, :] * silu_parts(r.pre1[rows, :])[1])
        return ()

    r.send(r.pre1_dot)
    r.need(r.pre1)
    each(act1)
    r.send(r.act1_dot)
    r.fetch(r.feat1, r.env1, r.pre2)
    stream.product(r.act1_dot, r.tmp)

    def lat1(rows, per):
        value = RES * (
            r.keep[rows, :] + env_dot() * r.out1[rows, :] + env() * r.tmp[rows, :]
        )
        put(r.lat1_dot, rows, value)
        lat = r.lat1[0][rows, :].astype(jnp.float32) + r.lat1[1][rows, :].astype(jnp.float32)
        part = factor() * (env_dot() * lat + env() * value)
        r.head_part[rows, :] = sum(part[:, s : s + 128] for s in range(0, edges, 128))
        return (per + fold(value * r.head[rows, :]),)

    r.need(r.out1, r.lat1)
    (per1,) = each(lat1, (nothing,))
    r.send(r.lat1_dot)
    r.w1_dot[...] = three_pass(pair(r.env1w), pair(r.lat1_dot))

    def embed1(base, lane):
        put9_split(r, channels, base, lane, embed_dot(r.w1, r.w1_dot, base, lane))

    planes(channels, edges, embed1)
    same_atom(r, scale, r.env1_dot, rows9)
    r.send(r.env1_dot)
    r.need(r.mix)

    def take(base, lane):
        put9_split(r, channels, base, lane, get9(r.res0_dot, channels, base, lane))

    planes(channels, edges, take)
    mixed(r, r.mix, r.feat1_dot, rows9)
    r.send(r.feat1_dot)
    r.need(r.feat1, r.env1)

    def scalar(base, lane):
        f, fd = get9(r.feat1, channels, base, lane), get9(r.feat1_dot, channels, base, lane)
        e, ed = get9(r.env1, channels, base, lane), get9(r.env1_dot, channels, base, lane)
        total = sum(fd[k] * e[k] + f[k] * ed[k] for k in range(9))
        r.res1_dot[pl.ds(base, 16), lane] = total * (1.0 / 3.0)

    planes(channels, edges, scalar)
    stream.product(r.lat1_dot, r.tmp, (r.sc1_t, split(r.res1_dot[...])))

    def act2(rows, per):
        v, vd, top = r.pre2[rows, :], r.tmp[rows, :], r.top[rows, :]
        s = sig(v)
        t = 1.0 - s
        slope, curve = s * (1.0 + v * t), s * t * (2.0 + v * (t - s))
        act_dot = slope * vd
        part = lead_dot() * (v * s) + lead() * act_dot
        r.last_part[rows, :] = sum(part[:, k : k + 128] for k in range(0, edges, 128))
        put(r.pre2_hat, rows, top * (lead_dot() * slope + lead() * curve * vd))
        return (per + fold(act_dot * top),)

    r.need(r.pre2)
    (per2,) = each(act2, (nothing,))
    r.send(r.pre2_hat)
    r.per_dot[...] = jnp.zeros_like(r.per_dot)
    r.per_dot[0:1, :] = jnp.sum(per1, axis=0, keepdims=True)
    r.per_dot[1:2, :] = jnp.sum(per2, axis=0, keepdims=True)


def tangent_down(r, channels, edges, scale):
    rows9 = 9 * channels
    env, factor, env_dot = (
        lambda: r.rows[0:1, :],
        lambda: r.rows[1:2, :],
        lambda: r.rows[2:3, :],
    )
    stream = Stream(
        r,
        [
            (r.m, 2),
            (r.m, 1),
            (r.m, 0),
            (r.out, None),
        ],
    )
    r.fetch(r.feat1, r.feat1_dot, r.env1, r.env1_dot)
    clear_tail(r, rows9)
    stream.product(r.pre2_hat, r.hat1)
    r.fetch(r.emb1_bar, r.lat1_bar)
    r.need(r.feat1, r.feat1_dot, r.env1, r.env1_dot)
    r.small[...] = three_pass(pair(r.sc1), pair(r.pre2_hat))

    def back1(base, lane):
        gh = r.small[pl.ds(base, 16), lane] * (1.0 / 3.0)
        g = r.res1_bar[pl.ds(base, 16), lane] * (1.0 / 3.0)
        f, fd = get9(r.feat1, channels, base, lane), get9(r.feat1_dot, channels, base, lane)
        e, ed = get9(r.env1, channels, base, lane), get9(r.env1_dot, channels, base, lane)
        put9_split(r, channels, base, lane, [gh * f[k] + g * fd[k] for k in range(9)])
        put9(r.feat1_hat, channels, base, lane, [gh * e[k] + g * ed[k] for k in range(9)])

    planes(channels, edges, back1)
    r.send(r.feat1_hat)
    r.fetch(r.mix_t, r.pre1, r.act1_bar, r.pre1_dot)
    same_atom(r, scale, r.plane, rows9)

    def collect(bar_ref, out_ref):
        def run(base, lane):
            bar = get9(bar_ref, channels, base, lane)
            hat = get9(r.plane, channels, base, lane)
            y, yd = row9(r.shape, lane), row9(r.shape_dot, lane)
            out_ref[pl.ds(base, 16), lane] = sum(
                yd[k] * bar[k] + y[k] * hat[k] for k in range(9)
            )

        planes(channels, edges, run)

    r.need(r.emb1_bar)
    collect(r.emb1_bar, r.w1_hat)
    w_pair = split(r.w1_hat[...])

    @pl.loop(0, 2)
    def _(t):
        rows = pl.ds(pl.multiple_of(t * 512, 512), 512)
        r.hat1[rows, :] += three_pass(pair(r.env1w_t, rows), w_pair)

    def out1(rows):
        value = r.hat1[rows, :] + (RES * factor() * env_dot()) * r.head[rows, :]
        r.hat1[rows, :] = value
        put(r.out1_hat, rows, RES * (env_dot() * r.lat1_bar[rows, :] + env() * value))
        return ()

    r.need(r.lat1_bar)
    each(out1)
    r.send(r.out1_hat)
    r.fetch(r.res0_bar, r.env0, r.env0_dot)
    stream.product(r.out1_hat, r.tmp)
    r.need(r.mix_t)

    def take(base, lane):
        put9_split(r, channels, base, lane, get9(r.feat1_hat, channels, base, lane))

    planes(channels, edges, take)
    mixed(r, r.mix_t, r.res0_hat, rows9)

    def pre1(rows):
        slope, curve = silu_slopes(r.pre1[rows, :])
        put(
            r.pre1_hat,
            rows,
            r.tmp[rows, :] * slope + r.act1_bar[rows, :] * curve * r.pre1_dot[rows, :],
        )
        return ()

    r.need(r.pre1, r.act1_bar, r.pre1_dot)
    each(pre1)
    r.send(r.pre1_hat)
    r.fetch(r.emb0_bar, r.lat0_bar)
    stream.product(r.pre1_hat, r.tmp)
    r.res0_hat[0:channels, :] += three_pass(pair(r.sc0), pair(r.pre1_hat))

    def embed_pair(base, lane):
        w, wd = r.w0[pl.ds(base, 16), lane], r.w0_dot[pl.ds(base, 16), lane]
        y, yd = row9(r.shape, lane), row9(r.shape_dot, lane)
        emb = [a * w for a in y]
        emb_dot = [b * w + a * wd for a, b in zip(y, yd)]
        return emb, emb_dot

    def back0(base, lane):
        emb, emb_dot = embed_pair(base, lane)
        gh, g = get9(r.res0_hat, channels, base, lane), get9(r.res0_bar, channels, base, lane)
        put9_split(
            r, channels, base, lane, terms_sum([((2, gh), (0, emb)), ((2, g), (0, emb_dot))], 1)
        )

    r.need(r.res0_bar)
    planes(channels, edges, back0)
    r.fetch(r.pre0, r.hid_bar, r.pre0_dot)
    same_atom(r, scale, r.plane, rows9)

    def back0_feature(base, lane):
        gh, g = get9(r.res0_hat, channels, base, lane), get9(r.res0_bar, channels, base, lane)
        e, ed = get9(r.env0, channels, base, lane), get9(r.env0_dot, channels, base, lane)
        more = terms_sum([((2, gh), (1, e)), ((2, g), (1, ed))], 0)
        have = get9(r.plane, channels, base, lane)
        put9(r.plane, channels, base, lane, [a + b for a, b in zip(have, more)])

    r.need(r.env0, r.env0_dot)
    planes(channels, edges, back0_feature)
    r.need(r.emb0_bar)
    collect(r.emb0_bar, r.w0_hat)
    w_pair0 = split(r.w0_hat[...])

    @pl.loop(0, 2)
    def _(t):
        rows = pl.ds(pl.multiple_of(t * 512, 512), 512)
        r.tmp[rows, :] += three_pass(pair(r.env0w_t, rows), w_pair0)

    def out0(rows):
        value = r.tmp[rows, :] + RES * r.hat1[rows, :]
        put(r.out0_hat, rows, env_dot() * r.lat0_bar[rows, :] + env() * value)
        return ()

    r.need(r.lat0_bar)
    each(out0)
    r.send(r.out0_hat)
    stream.product(r.out0_hat, r.tmp)

    def pre0(rows):
        slope, curve = silu_slopes(r.pre0[rows, :])
        put(
            r.pre0_hat,
            rows,
            r.tmp[rows, :] * slope + r.hid_bar[rows, :] * curve * r.pre0_dot[rows, :],
        )
        return ()

    r.need(r.pre0, r.hid_bar, r.pre0_dot)
    each(pre0)
    r.send(r.pre0_hat)


def small_gradients(r, channels, edges):
    r.fetch(r.hid, r.out0_hat, r.pre0_bar, r.pre0_hat)
    tiles = [pl.ds(t * HALF, HALF) for t in range(2)]
    for rows in tiles:
        r.out_grad[rows, :] = three_pass(pair(r.hid_dot, rows), pair(r.out0_bar), NT)
    r.need(r.hid, r.out0_hat)
    for rows in tiles:
        r.out_grad[rows, :] += three_pass(pair(r.hid, rows), pair(r.out0_hat), NT)
    r.send(r.out_grad)
    r.need(r.pre0_bar, r.pre0_hat)
    r.fetch(r.feat1_bar, r.res0_dot, r.feat1_hat, r.res0)
    r.in_grad[...] = three_pass(split(r.bessel_dot[...]), pair(r.pre0_bar), NT) + three_pass(
        split(r.feat[...]), pair(r.pre0_hat), NT
    )
    r.fetch(r.lat0_dot, r.lat0, r.pre1_bar, r.pre1_hat)

    def twice(first, second, third, fourth):
        return three_pass(split(first), pair(second), NT) + three_pass(split(third), pair(fourth), NT)

    r.need(r.feat1_bar, r.res0_dot, r.feat1_hat, r.res0)
    r.fetch(r.lat1_dot, r.lat1, r.pre2_bar, r.pre2_hat)
    r.need(r.lat0_dot, r.lat0, r.pre1_bar, r.pre1_hat)
    r.env_grad[0] = twice(r.w0_bar[...], r.lat0_dot, r.w0_hat[...], r.lat0)
    r.sc_grad[0] = twice(r.res0_dot[0:channels, :], r.pre1_bar, r.res0[0:channels, :], r.pre1_hat)
    r.need(r.lat1_dot, r.lat1, r.pre2_bar, r.pre2_hat)
    r.env_grad[1] = twice(r.w1_bar[...], r.lat1_dot, r.w1_hat[...], r.lat1)
    r.sc_grad[1] = twice(r.res1_dot[...], r.pre2_bar, r.res1[...], r.pre2_hat)
    for order, (start, stop) in enumerate(((0, 1), (1, 4), (4, 9))):
        total = None
        for k in range(start, stop):
            part = slice(k * channels, (k + 1) * channels)
            term = three_pass(split(r.feat1_bar[part, :]), split(r.res0_dot[part, :]), NT)
            term = term + three_pass(split(r.feat1_hat[part, :]), split(r.res0[part, :]), NT)
            total = term if total is None else total + term
        r.mix_grad[order] = total


def load_blocks(r):
    depth = 3

    def incoming(step):
        slot = lax.rem(step, depth)
        return [
            pltpu.make_async_copy(
                r.piece.at[r.where[step * SIDE + j]], r.blocks.at[slot, j], r.sem.at[slot, j]
            )
            for j in range(SIDE)
        ]

    def outgoing(step):
        slot, m, i = step % 2, step // SIDE, step % SIDE
        rows = pl.ds(pl.multiple_of(i * BS, BS), BS)
        plain = [
            pltpu.make_async_copy(
                r.flat.at[slot, part], r.m[part].at[m, rows, :], r.out_sem.at[slot, part]
            )
            for part in range(2)
        ]
        turned = [
            pltpu.make_async_copy(
                r.turned.at[slot, part], r.mt[part].at[m, :, rows], r.out_sem.at[slot, 2 + part]
            )
            for part in range(2)
        ]
        return plain + turned

    steps = 3 * SIDE
    for step in range(depth - 1):
        for copy in incoming(step):
            copy.start()
    eye = (
        lax.broadcasted_iota(jnp.int32, (BS, BS), 0) == lax.broadcasted_iota(jnp.int32, (BS, BS), 1)
    ).astype(jnp.bfloat16)

    @pl.loop(0, steps)
    def _(step):
        @pl.when(step + depth - 1 < steps)
        def _():
            for copy in incoming(step + depth - 1):
                copy.start()

        for copy in incoming(step):
            copy.wait()

        @pl.when(step >= 2)
        def _():
            for copy in outgoing(step - 2):
                copy.wait()

        slot, source = step % 2, lax.rem(step, depth)
        for j in range(SIDE):
            part = slice(j * BS, (j + 1) * BS)
            high, low = split(r.blocks[source, j])
            r.flat[slot, 0, :, part] = high
            r.flat[slot, 1, :, part] = low
            r.turned[slot, 0, part, :] = one_pass(eye, high, NT).astype(jnp.bfloat16)
            r.turned[slot, 1, part, :] = one_pass(eye, low, NT).astype(jnp.bfloat16)
        for copy in outgoing(step):
            copy.start()

    def last(i):
        return [
            pltpu.make_async_copy(
                r.piece.at[r.where[(3 * SIDE + i) * SIDE + j]],
                r.last.at[pl.ds(i * BS, BS), pl.ds(j * BS, BS)],
                r.last_sem.at[i, j],
            )
            for j in range(SIDE)
        ]

    for i in range(SIDE):
        for copy in last(i):
            copy.start()
    for step in (steps - 2, steps - 1):
        for copy in outgoing(step):
            copy.wait()
    head = r.head[...]
    for i in range(SIDE):
        for copy in last(i):
            copy.wait()

    def top(rows):
        r.top[rows, :] = jnp.sum(r.last[rows, :] * head, axis=1, keepdims=True)
        return ()

    each(top)


def block_gradients(r, channels, edges, targets):
    names = [(r.lat0_dot, r.lat0, r.pre1_bar, r.pre1_hat)]
    names.append((r.act1_dot, r.act1, r.out1_bar, r.out1_hat))
    names.append((r.lat1_dot, r.lat1, r.pre2_bar, r.pre2_hat))
    tile = HALF
    count = tile // BS * SIDE

    def incoming(m):
        return [
            pltpu.make_async_copy(ref, r.held.at[m % 2, a, part], r.arrived.at[m % 2, a, part])
            for a, refs in enumerate(names[m])
            for part, ref in enumerate(refs)
        ]

    for copy in incoming(0):
        copy.start()

    def spot(q):
        rows = pl.ds(pl.multiple_of((q // SIDE) * BS, BS), BS)
        return rows, pl.ds(pl.multiple_of((q % SIDE) * BS, BS), BS)

    def wait_tile(slot):
        whole = r.out[0].at[pl.ds(0, count)]
        pltpu.make_async_copy(whole, whole, r.sent_sem.at[slot]).wait()

    def send_tile(first, slot):
        def one(q, state):
            which, where = r.which[first + q], r.where[first + q]
            for n in range(targets):

                @pl.when(which == n)
                def _(n=n):
                    pltpu.make_async_copy(
                        r.stage.at[slot, *spot(q)], r.out[n].at[where], r.sent_sem.at[slot]
                    ).start()

            return state

        lax.fori_loop(0, count, one, 0)

    for m in (3, 0, 1, 2):
        if m < 3:
            if m + 1 < 3:
                for copy in incoming(m + 1):
                    copy.start()
            for copy in incoming(m):
                copy.wait()
            held = lambda a, which=slice(None): (
                r.held[m % 2, a, 0, which, :],
                r.held[m % 2, a, 1, which, :],
            )
        for t in range(2):
            if m != 3:
                wait_tile(t)
            rows = pl.ds(t * tile, tile)
            if m < 3:
                r.stage[t] = three_pass(held(0, rows), held(2), NT) + three_pass(
                    held(1, rows), held(3), NT
                )
            else:
                r.stage[t] = r.lead[rows, :] * r.head[...]
            send_tile((m * SIDE + t * (tile // BS)) * SIDE, t)
    wait_tile(0)
    wait_tile(1)


def soap_kernel(count, *refs):
    grad, weight, first, second, left, right, lstat, rstat, average = refs[:9]
    outs = refs[9:]
    tn_dims = ((0,), (0,))

    def mm(a, b, dims=((1,), (0,))):
        return [three_pass(split(x), split(y), dims) for x, y in zip(a, b)]

    load = lambda ref: [ref[s] for s in range(count)]
    g, l, rr = load(grad), load(left), load(right)
    rotated = mm(mm(l, g, tn_dims), rr)
    first_new = [0.9 * first[s] + 0.1 * rotated[s] for s in range(count)]
    second_new = [0.99 * second[s] + 0.01 * rotated[s] * rotated[s] for s in range(count)]
    normal = [
        a * (1.0 / (1.0 - 0.9**ADAM_STEP)) / (jnp.sqrt(b * (1.0 / (1.0 - 0.99**ADAM_STEP))) + 1e-08)
        for a, b in zip(first_new, second_new)
    ]
    step = mm(mm(l, normal), rr, NT)
    for s in range(count):
        new = weight[s] - 0.01 * (step[s] + 0.01 * weight[s])
        outs[0][s] = new
        outs[7][s] = 0.99 * average[s] + 0.01 * new
        outs[2][s] = second_new[s]
    plain = mm(mm(l, first_new), rr, NT)
    ls = [0.95 * lstat[s] + 0.05 * v for s, v in enumerate(mm(g, g, NT))]
    rs = [0.95 * rstat[s] + 0.05 * v for s, v in enumerate(mm(g, g, tn_dims))]
    for s in range(count):
        outs[5][s] = ls[s]
        outs[6][s] = rs[s]
    x = mm(ls, l) + mm(rs, rr)
    x = [v / jnp.sqrt(jnp.sum(v * v)) for v in x]
    for _ in range(NS_STEPS):
        x = [1.5 * a - 0.5 * b for a, b in zip(x, mm(mm(x, x, NT), x))]
    ln, rn = x[:count], x[count:]
    out = mm(mm(ln, plain, tn_dims), rn)
    for s in range(count):
        outs[3][s] = ln[s]
        outs[4][s] = rn[s]
        outs[1][s] = out[s]


def soap_update(arrays):
    slots = arrays[0].shape[0]
    count = 2 if slots % 2 == 0 else 1
    spec = pl.BlockSpec((count, BS, BS), lambda s: (s, 0, 0))
    return pl.pallas_call(
        partial(soap_kernel, count),
        grid=(slots // count,),
        out_shape=[f32(slots, BS, BS)] * 8,
        in_specs=[spec] * 9,
        out_specs=[spec] * 8,
        compiler_params=pltpu.CompilerParams(vmem_limit_bytes=40 * 2**20),
    )(*arrays)


def adamw(weight, first, second, grad):
    first_new = 0.9 * first + 0.1 * grad
    second_new = 0.99 * second + 0.01 * grad * grad
    normal = (
        first_new
        / (1.0 - 0.9**ADAM_STEP)
        / (jnp.sqrt(second_new / (1.0 - 0.99**ADAM_STEP)) + 1e-08)
    )
    return (weight - 0.01 * (normal + 0.01 * weight), first_new, second_new)


def to_matrices(blocks):
    return (
        blocks.reshape(2 * LAYERS, SIDE, SIDE, BS, BS).transpose(0, 1, 3, 2, 4).reshape(2 * LAYERS, D, D)
    )


def to_blocks(matrices):
    return (
        matrices.reshape(2 * LAYERS, SIDE, BS, SIDE, BS)
        .transpose(0, 1, 3, 2, 4)
        .reshape(2 * LAYERS * SIDE * SIDE, BS, BS)
    )


def tables(block_owner, slots, sizes):
    ids = jnp.arange(block_owner.shape[0], dtype=jnp.int32)
    inverse = jnp.sum(jnp.where(block_owner[None] == ids[:, None], ids[None], 0), axis=1)
    if not is_cube(sizes):
        return jnp.zeros_like(inverse), inverse, inverse
    y, x, z, core = place()
    device, slot = inverse // slots, inverse % slots
    rank = jnp.sum(
        jnp.where(
            jnp.asarray(Z_ORDER)[z][:, None] == (device // 2 % 4)[None],
            jnp.arange(4, dtype=jnp.int32)[:, None],
            0,
        ),
        axis=0,
    )
    which = ((device % 2) ^ core) * 4 + rank
    where = (((device // 8 % 2) ^ x) * 2 + ((device // 16) ^ y)) * slots + slot
    return which, where, inverse


def sum_pieces(pieces, sizes, slots):
    if not is_cube(sizes):
        total = lax.psum_scatter(pieces[0], AX, scatter_dimension=0, tiled=True)
        return total, total
    chunks = [pieces[p] + hop(pieces[4 + p], HOP_CORE) for p in range(4)]
    return reduce_chips([c.reshape(2, 2, slots, BS, BS) for c in chunks])


def block_diagonal(mixing, depth):
    channels = mixing.shape[-1]
    rows = []
    for k in range(9):
        block = mixing[0 if k == 0 else 1 if k < 4 else 2]
        rows.append(jnp.pad(block, ((0, 0), (k * channels, depth - (k + 1) * channels))))
    return jnp.concatenate(rows, axis=0)


def fast_chain(weights, every, inverse, targets, which, where, scale, force_to_tangent, vec, live, src, ss, st):
    pair_in, pair_out, env_weight, scalar_weight, mix_weight, energy_head = weights
    channels, edges = env_weight.shape[1], vec.shape[1]
    rows9 = 9 * channels
    depth = -(-rows9 // 128) * 128
    head = energy_head[:D]
    factor = jnp.sum(energy_head[D:, None] * ss, axis=0)
    inv, unit, env, denv, bessel, dbessel = geometry(vec, live)
    pad_rows = lambda v, n: jnp.pad(v, ((0, n - v.shape[0]), (0, 0)))
    shape = pad_rows(harmonics(unit), 16)
    feat = jnp.concatenate([bessel, ss, st], axis=0)
    rows = pad_rows(jnp.stack([env, factor]), 8)
    same = (src[:, None] == src[None]).astype(jnp.bfloat16)
    cut = split_outside
    in_t, in_w, out_t, out_w = cut(pair_in.T), cut(pair_in), cut(pair_out.T), cut(pair_out)
    env_w, env_t = cut(env_weight), cut(env_weight.transpose(0, 2, 1))
    sc_w, sc_t = cut(scalar_weight), cut(scalar_weight.transpose(0, 2, 1))
    layer = lambda parts, l: tuple(v[l] for v in parts)
    mix_w = cut(block_diagonal(mix_weight, depth))
    mix_t = cut(block_diagonal(mix_weight.transpose(0, 2, 1), depth))
    wide, plane, narrow = (D, edges), (rows9, edges), (channels, edges)
    unit_flops = 6 * D * D * edges
    temps = dict(**stream_scratch(), **plane_scratch(rows9, edges))
    args = (channels, edges, scale)

    one = kernel_call(
        lambda r: first_layer(r, *args),
        dict(shape=shape, rows=rows, same=same, feat=feat, in_t=in_t, env0w=layer(env_w, 0)),
        dict(w0=f32(*narrow)),
        temps,
        sent=dict(
            pre0=f32(*wide),
            out0=f32(*wide),
            hid=pair_of(*wide),
            lat0=pair_of(*wide),
            env0=f32(*plane),
            res0=f32(*plane),
        ),
        hbm=dict(out_t=out_t),
        flops=unit_flops,
    )
    loaded = kernel_call(
        load_blocks,
        dict(head=head[None]),
        dict(last=f32(D, D), top=f32(D, 1)),
        dict(
            blocks=pltpu.VMEM((3, SIDE, BS, BS), jnp.float32),
            flat=pltpu.VMEM((2, 2, BS, D), jnp.bfloat16),
            turned=pltpu.VMEM((2, 2, D, BS), jnp.bfloat16),
            sem=pltpu.SemaphoreType.DMA((3, SIDE)),
            out_sem=pltpu.SemaphoreType.DMA((2, 4)),
            last_sem=pltpu.SemaphoreType.DMA((SIDE, SIDE)),
        ),
        hbm=dict(piece=every),
        hbm_out=dict(m=pair_of(3, D, D), mt=pair_of(3, D, D)),
        smem=dict(where=inverse),
    )
    head_col = head[:, None]
    up = kernel_call(
        lambda r: energy_up(r, *args),
        dict(
            shape=shape,
            rows=rows,
            same=same,
            head=head_col,
            top=loaded.top,
            lat0=one.lat0,
            res0=one.res0,
            sc0_t=layer(sc_t, 0),
            sc1_t=layer(sc_t, 1),
            env1w=layer(env_w, 1),
        ),
        dict(w1=f32(*narrow), res1=f32(*narrow), per=f32(8, edges)),
        temps,
        late=dict(out0=one.out0, mix=mix_w),
        sent=dict(
            pre1=f32(*wide),
            out1=f32(*wide),
            pre2=f32(*wide),
            act1=pair_of(*wide),
            lat1=pair_of(*wide),
            pre2_bar=pair_of(*wide),
            env1=f32(*plane),
            feat1=f32(*plane),
        ),
        hbm=dict(mt=loaded.mt),
        flops=3 * unit_flops,
    )
    down = kernel_call(
        lambda r: energy_down(r, *args),
        dict(
            shape=shape,
            rows=rows,
            same=same,
            head=head_col,
            w0=one.w0,
            w1=up.w1,
            per=up.per,
            pre2_bar=up.pre2_bar,
            sc0=layer(sc_w, 0),
            sc1=layer(sc_w, 1),
            env0w_t=layer(env_t, 0),
            env1w_t=layer(env_t, 1),
            in_w=in_w,
        ),
        dict(
            res1_bar=f32(*narrow),
            w1_bar=f32(*narrow),
            w0_bar=f32(*narrow),
            shape_bar=f32(16, edges),
            env_bar=f32(8, edges),
            bessel_bar=f32(16, edges),
        ),
        temps,
        late=dict(
            pre0=one.pre0,
            out0=one.out0,
            env0=one.env0,
            pre1=up.pre1,
            out1=up.out1,
            env1=up.env1,
            feat1=up.feat1,
            mix_t=mix_t,
        ),
        sent=dict(
            lat1_bar=f32(*wide),
            act1_bar=f32(*wide),
            lat0_bar=f32(*wide),
            hid_bar=f32(*wide),
            out1_bar=pair_of(*wide),
            pre1_bar=pair_of(*wide),
            out0_bar=pair_of(*wide),
            pre0_bar=pair_of(*wide),
            feat1_bar=f32(*plane),
            emb1_bar=f32(*plane),
            res0_bar=f32(*plane),
            emb0_bar=f32(*plane),
        ),
        hbm=dict(m=loaded.m, out=out_w),
        flops=4 * unit_flops,
    )
    dist_bar = down.env_bar[0] * denv + jnp.sum(down.bessel_bar[:NB] * dbessel, axis=0)
    unit_bar = harmonics_back(unit, down.shape_bar)
    along = jnp.sum(unit * unit_bar, axis=0)
    vec_bar = dist_bar[None] * unit + (unit_bar - unit * along[None]) * inv[None]
    vec_dot, loss = force_to_tangent(vec_bar)
    dist_dot = jnp.sum(unit * vec_dot, axis=0)
    unit_dot = (vec_dot - unit * dist_dot[None]) * inv[None]
    env_dot = denv * dist_dot
    bessel_dot = pad_rows(dbessel * dist_dot[None], 2 * NB)
    shape_dot = pad_rows(harmonics_dot(unit, unit_dot), 16)
    rows = pad_rows(jnp.stack([env, factor, env_dot]), 8)
    tan = kernel_call(
        lambda r: tangent_up(r, *args),
        dict(
            shape=shape,
            rows=rows,
            same=same,
            shape_dot=shape_dot,
            bessel_dot=bessel_dot,
            head=head_col,
            top=loaded.top,
            w0=one.w0,
            w1=up.w1,
            in_t=in_t,
            sc0_t=layer(sc_t, 0),
            sc1_t=layer(sc_t, 1),
            env0w=layer(env_w, 0),
            env1w=layer(env_w, 1),
        ),
        dict(
            w0_dot=f32(*narrow),
            w1_dot=f32(*narrow),
            res1_dot=f32(*narrow),
            head_part=f32(D, 128),
            last_part=f32(D, 128),
            per_dot=f32(8, edges),
        ),
        dict(
            **temps,
            tmp=pltpu.VMEM(wide, jnp.float32),
            keep=pltpu.VMEM(wide, jnp.float32),
        ),
        late=dict(
            pre0=one.pre0,
            out0=one.out0,
            env0=one.env0,
            pre1=up.pre1,
            out1=up.out1,
            pre2=up.pre2,
            env1=up.env1,
            feat1=up.feat1,
            lat1=up.lat1,
            mix=mix_w,
        ),
        sent=dict(
            pre0_dot=f32(*wide),
            pre1_dot=f32(*wide),
            hid_dot=pair_of(*wide),
            lat0_dot=pair_of(*wide),
            act1_dot=pair_of(*wide),
            lat1_dot=pair_of(*wide),
            pre2_hat=pair_of(*wide),
            env0_dot=f32(*plane),
            res0_dot=f32(*plane),
            env1_dot=f32(*plane),
            feat1_dot=f32(*plane),
        ),
        hbm=dict(out_t=out_t, mt=loaded.mt),
        flops=4 * unit_flops,
    )
    hat = kernel_call(
        lambda r: tangent_down(r, *args),
        dict(
            shape=shape,
            rows=rows,
            same=same,
            shape_dot=shape_dot,
            head=head_col,
            pre2_hat=tan.pre2_hat,
            w0=one.w0,
            w0_dot=tan.w0_dot,
            res1_bar=down.res1_bar,
            sc0=layer(sc_w, 0),
            sc1=layer(sc_w, 1),
            env0w_t=layer(env_t, 0),
            env1w_t=layer(env_t, 1),
        ),
        dict(w1_hat=f32(*narrow), w0_hat=f32(*narrow)),
        dict(
            **temps,
            hat1=pltpu.VMEM(wide, jnp.float32),
            tmp=pltpu.VMEM(wide, jnp.float32),
            small=pltpu.VMEM(narrow, jnp.float32),
            plane=pltpu.VMEM(plane, jnp.float32),
            res0_hat=pltpu.VMEM(plane, jnp.float32),
        ),
        late=dict(
            pre0=one.pre0,
            env0=one.env0,
            pre1=up.pre1,
            env1=up.env1,
            feat1=up.feat1,
            lat1_bar=down.lat1_bar,
            act1_bar=down.act1_bar,
            lat0_bar=down.lat0_bar,
            hid_bar=down.hid_bar,
            emb1_bar=down.emb1_bar,
            emb0_bar=down.emb0_bar,
            res0_bar=down.res0_bar,
            pre0_dot=tan.pre0_dot,
            pre1_dot=tan.pre1_dot,
            env1_dot=tan.env1_dot,
            feat1_dot=tan.feat1_dot,
            env0_dot=tan.env0_dot,
            mix_t=mix_t,
        ),
        sent=dict(
            out1_hat=pair_of(*wide),
            pre1_hat=pair_of(*wide),
            out0_hat=pair_of(*wide),
            pre0_hat=pair_of(*wide),
            feat1_hat=f32(*plane),
        ),
        hbm=dict(m=loaded.m, out=out_w),
        flops=4 * unit_flops,
    )
    lead_sum = jnp.sum(tan.last_part, axis=1)
    head_grad = RES * jnp.sum(tan.head_part, axis=1) + jnp.sum(
        lead_sum[:, None] * loaded.last, axis=0
    )
    per1, per2 = up.per[0], up.per[1]
    energy_dot = env_dot * RES * (per1 + env * per2) + env * RES * (
        tan.per_dot[0] + env_dot * per2 + env * tan.per_dot[1]
    )
    head_grad = jnp.concatenate([head_grad, jnp.sum(ss * energy_dot[None], axis=1)])
    made = kernel_call(
        lambda r: block_gradients(r, channels, edges, targets),
        dict(
            lead=lead_sum[:, None],
            head=head[None],
        ),
        {},
        dict(
            held=pltpu.VMEM((2, 4, 2, D, edges), jnp.bfloat16),
            arrived=pltpu.SemaphoreType.DMA((2, 4, 2)),
            stage=pltpu.VMEM((2, HALF, D), jnp.float32),
            sent_sem=pltpu.SemaphoreType.DMA((2,)),
        ),
        hbm=dict(
            lat0_dot=tan.lat0_dot,
            act1_dot=tan.act1_dot,
            lat1_dot=tan.lat1_dot,
            pre2_hat=tan.pre2_hat,
            lat0=one.lat0,
            act1=up.act1,
            lat1=up.lat1,
            pre2_bar=up.pre2_bar,
            pre1_bar=down.pre1_bar,
            out1_bar=down.out1_bar,
            pre1_hat=hat.pre1_hat,
            out1_hat=hat.out1_hat,
        ),
        hbm_out=dict(out=[f32(every.shape[0] // targets, BS, BS) for _ in range(targets)]),
        smem=dict(which=which, where=where),
        flops=6 * unit_flops,
    )

    feat = lax.optimization_barrier((feat, made.out[0]))[0]
    small = kernel_call(
        lambda r: small_gradients(r, channels, edges),
        dict(
            feat=feat,
            bessel_dot=bessel_dot,
            hid_dot=tan.hid_dot,
            out0_bar=down.out0_bar,
            w0_bar=down.w0_bar,
            w1_bar=down.w1_bar,
            w0_hat=hat.w0_hat,
            w1_hat=hat.w1_hat,
            res1=up.res1,
            res1_dot=tan.res1_dot,
        ),
        dict(
            in_grad=f32(2 * NB, D),
            mix_grad=f32(3, channels, channels),
            env_grad=f32(2, channels, D),
            sc_grad=f32(2, channels, D),
        ),
        {},
        late=dict(
            hid=one.hid,
            out0_hat=hat.out0_hat,
            pre0_bar=down.pre0_bar,
            pre0_hat=hat.pre0_hat,
            feat1_bar=down.feat1_bar,
            res0_dot=tan.res0_dot,
            feat1_hat=hat.feat1_hat,
            res0=one.res0,
            lat0_dot=tan.lat0_dot,
            lat0=one.lat0,
            pre1_bar=down.pre1_bar,
            pre1_hat=hat.pre1_hat,
            lat1_dot=tan.lat1_dot,
            lat1=up.lat1,
            pre2_bar=up.pre2_bar,
            pre2_hat=tan.pre2_hat,
        ),
        sent=dict(out_grad=f32(D, D)),
        flops=2 * unit_flops,
    )

    return small, head_grad, loss, made


def local(
    sizes,
    edge_vec,
    edge_live,
    source,
    target,
    species,
    force_label,
    force_mask,
    block_owner,
    pair_in_weight,
    pair_in_first,
    pair_in_second,
    pair_out_weight,
    pair_out_first,
    pair_out_second,
    env_weight,
    env_first,
    env_second,
    scalar_weight,
    scalar_first,
    scalar_second,
    mix_weight,
    mix_first,
    mix_second,
    energy_head,
    head_first,
    head_second,
    soap_weight,
    soap_first,
    soap_second,
    soap_left,
    soap_right,
    soap_lstat,
    soap_rstat,
    soap_average,
):
    devices = sizes[0] * sizes[1]
    edges = edge_vec.shape[1]
    per_atoms = force_label.shape[1]
    atoms = per_atoms * devices
    me = lax.axis_index("irrep") * sizes[1] + lax.axis_index("edge")
    scale = math.sqrt(per_atoms / edges)
    as_float = lambda v: v.astype(jnp.float32)

    labels = jnp.concatenate([force_label, as_float(force_mask)[None]], axis=0).reshape(-1)
    packed = jnp.concatenate(
        [
            edge_vec,
            as_float(source)[None],
            as_float(target)[None],
            as_float(edge_live)[None],
            jnp.pad(labels, (0, edges - labels.shape[0]))[None],
        ],
        axis=0,
    )
    every = gather_small(packed, sizes)
    label_all = every[:, 6, : 4 * per_atoms].reshape(devices, 4, per_atoms)
    label_all = label_all.transpose(1, 0, 2).reshape(4, atoms)
    label_mask = label_all[3]
    label_total = jnp.sum(label_mask)
    payload = every[:, :5].transpose(0, 2, 1).reshape(devices * edges, 5)
    all_source = every[:, 3].reshape(-1).astype(jnp.int32)
    all_live = every[:, 5].reshape(-1)

    low = (all_source[:, None] % 32 == jnp.arange(32)[None]).astype(jnp.bfloat16)
    high = (all_source[None] // 32 == jnp.arange(-(-atoms // 32))[:, None]) & (all_live[None] > 0)
    counts = jnp.dot(
        high.astype(jnp.bfloat16), low, preferred_element_type=jnp.float32
    ).reshape(-1)[:atoms]
    atom_ids = jnp.arange(atoms)
    before = jnp.dot(
        (atom_ids[:, None] > atom_ids[None]).astype(jnp.float32), counts, precision=FULL
    )
    middle = (2.0 * before + counts).astype(jnp.int32)
    total = jnp.sum(counts).astype(jnp.int32)
    owner = jnp.minimum((middle * devices) // (2 * total), devices - 1)
    loads = jnp.sum(
        jnp.where(owner[None] == jnp.arange(devices)[:, None], counts[None], 0.0), axis=1
    )
    fits = jnp.max(loads) <= edges
    first_atom = jnp.sum(owner < me)
    last_atom = jnp.sum(owner <= me)
    mine = (all_live > 0) & (all_source >= first_atom) & (all_source < last_atom)
    flags = as_float(mine).reshape(-1, 128)
    tri = jnp.arange(128)
    inside = jnp.dot(flags, as_float(tri[:, None] <= tri[None]))
    row_ids = jnp.arange(flags.shape[0])
    row_sum = jnp.sum(flags, axis=1)
    offset = jnp.sum(
        jnp.where(row_ids[None] < row_ids[:, None], row_sum[None], 0.0), axis=1
    )
    rank = (inside + offset[:, None]).reshape(-1)
    slot_ids = jnp.arange(edges).astype(jnp.float32)
    index = jnp.sum((rank[None] <= slot_ids[:, None]).astype(jnp.float32), axis=1).astype(jnp.int32)
    valid = slot_ids < rank[-1]
    chosen = payload[jnp.minimum(index, devices * edges - 1)].T
    safe = jnp.asarray([1.5, 0.0, 0.0], jnp.float32)[:, None]
    my_vec = jnp.where(valid[None], chosen[:3], safe)
    my_source = jnp.where(valid, chosen[3], -1.0).astype(jnp.int32)
    my_target = jnp.where(valid, chosen[4], -1.0).astype(jnp.int32)
    my_live = as_float(valid)

    weights = (pair_in_weight, pair_out_weight, env_weight, scalar_weight, mix_weight[0], energy_head)
    slots = soap_weight.shape[0]
    kinds = jnp.arange(SPECIES, dtype=jnp.int32)[:, None]
    every_block = lax.all_gather(soap_weight, AX, axis=0, tiled=True)
    targets = 8 if is_cube(sizes) else 1
    which, where, inverse = tables(block_owner, slots, sizes)

    def views(src, tgt):
        from_atom = (src[:, None] == atom_ids[None]).astype(jnp.float32)
        to_atom = (tgt[:, None] == atom_ids[None]).astype(jnp.float32)
        spec = (species[None] == kinds).astype(jnp.float32)
        species_source = dot(spec, from_atom, ((1,), (1,)), None)
        species_target = dot(spec, to_atom, ((1,), (1,)), None)
        ends = from_atom - to_atom

        def force_to_tangent(vec_bar):
            force = sum_small(dot(vec_bar, ends, ((1,), (0,)), FULL), sizes)
            residual = force - label_all[:3]
            loss = jnp.sum(label_mask[None] * residual * residual)
            cot = 2.0 * label_mask[None] * residual / label_total
            return dot(cot, ends, ((1,), (1,)), FULL), loss

        return from_atom, species_source, species_target, force_to_tangent

    def general():
        from_atom, ss, st, force_to_tangent = views(source, target)
        blocks = every_block[inverse]

        def environ(tensor):
            sums = lax.psum(nn(tensor.reshape(-1, edges), from_atom), AX)
            return scale * nt(sums, from_atom).reshape(tensor.shape)

        matrices = to_matrices(blocks)
        out = chain(
            weights,
            lambda after: matrices,
            environ,
            force_to_tangent,
            edge_vec,
            as_float(edge_live),
            ss,
            st,
        )
        flat = to_blocks(jnp.stack(out[6]))
        per = inverse.shape[0] // targets
        place_of = which * per + where
        order = jnp.zeros_like(place_of).at[place_of].set(jnp.arange(place_of.shape[0]))
        laid = flat[order].reshape(targets, per, BS, BS)
        return out[:6] + (tuple(laid[n] for n in range(targets)), out[7])

    def pack_first(in_grad, out_grad, mix_grad, head_grad):
        rest = jnp.concatenate([mix_grad.reshape(-1), head_grad])
        rest = jnp.pad(rest, (0, -rest.shape[0] % (8 * D))).reshape(-1, D)
        return jnp.concatenate([in_grad, rest], axis=0), out_grad

    flat_rows = lambda env_grad, sc_grad: (env_grad.reshape(-1, D), sc_grad.reshape(-1, D))
    def replace(state):
        out = general()
        parts = pack_first(out[0], out[1], out[4], out[5]) + flat_rows(out[2], out[3])
        own, _ = sum_pieces(out[6], sizes, slots)
        return (jnp.asarray(False), own, lax.psum(parts, AX), out[7])

    rest_rows = 8 * (-(-(mix_weight.size + energy_head.shape[0]) // (8 * D))) + 2 * NB
    zeros = lambda n: jnp.zeros((n, D), jnp.float32)
    wide_rows = env_weight.shape[0] * env_weight.shape[1]
    _, general_own, general_shared, general_loss = lax.while_loop(
        lambda state: state[0],
        replace,
        (
            jnp.logical_not(fits),
            jnp.zeros_like(soap_weight),
            (zeros(rest_rows), zeros(D), zeros(wide_rows), zeros(wide_rows)),
            jnp.zeros((), jnp.float32),
        ),
    )
    every_block, general_loss = lax.optimization_barrier((every_block, general_loss))
    _, my_ss, my_st, my_force = views(my_source, my_target)
    fast = fast_chain(
        weights, every_block, inverse, targets, which, where, scale, my_force, my_vec, my_live, my_source, my_ss, my_st
    )

    small, head_part, fast_loss, made = fast
    local_sums = pack_first(small.in_grad, small.out_grad, small.mix_grad, head_part)
    local_sums = local_sums + flat_rows(small.env_grad, small.sc_grad)
    summed = lax.psum(local_sums, AX)
    loss_sum = jnp.where(fits, fast_loss, general_loss)

    own_grads, nearly = sum_pieces(tuple(made.out), sizes, slots)
    own_grads = jnp.where(fits, own_grads, general_own)
    soap = soap_update(
        (
            own_grads,
            soap_weight,
            soap_first,
            soap_second,
            soap_left,
            soap_right,
            soap_lstat,
            soap_rstat,
            soap_average,
        )
    )
    (summed, general_shared), soap = lax.optimization_barrier(((summed, general_shared), tuple(soap)))
    misc, pair_out_grad, env_grad, scalar_grad = jax.tree.map(
        lambda a, b: jnp.where(fits, a, b), summed, general_shared
    )
    pair_in_grad = misc[: 2 * NB]
    rest = misc[2 * NB :].reshape(-1)
    mix_grad = rest[: mix_weight.size].reshape(mix_weight.shape[1:])
    head_grad = rest[mix_weight.size : mix_weight.size + energy_head.shape[0]]
    env_grad = env_grad.reshape(env_weight.shape)
    scalar_grad = scalar_grad.reshape(scalar_weight.shape)
    new_pair_in = adamw(pair_in_weight, pair_in_first, pair_in_second, pair_in_grad)
    new_pair_out = adamw(pair_out_weight, pair_out_first, pair_out_second, pair_out_grad)
    new_env = adamw(env_weight, env_first, env_second, env_grad)
    new_scalar = adamw(scalar_weight, scalar_first, scalar_second, scalar_grad)
    new_mix = adamw(mix_weight, mix_first, mix_second, mix_grad[None])
    new_head = adamw(energy_head, head_first, head_second, head_grad)
    return (
        (loss_sum, label_total)
        + new_pair_in
        + new_pair_out
        + new_env
        + new_scalar
        + new_mix
        + new_head
        + tuple(soap)
    )


def solution(mesh):
    shared, split = P(), P(AX)
    column = P(None, AX)
    blocks = P(AX, None, None)
    placed = (
        (column, split, split, split, shared, column, split, shared) + (shared,) * 18 + (blocks,) * 8
    )
    return jax.shard_map(
        partial(local, (mesh.shape["irrep"], mesh.shape["edge"])),
        mesh=mesh,
        in_specs=placed,
        out_specs=(shared,) * 20 + (blocks,) * 8,
        check_vma=False,
    )
```

```python
from functools import partial
import math
from types import SimpleNamespace

import jax
import jax.numpy as jnp
import numpy as np
from jax import lax
from jax.experimental import pallas as pl
from jax.experimental.pallas import tpu as pltpu
from jax.sharding import PartitionSpec as P

D = 1024
NB = 8
SPECIES = 4
LAYERS = 2
BS = 128
NS_STEPS = 4
ADAM_STEP = 10
SIDE = D // BS
AX = ("irrep", "edge")

HIGH = lax.Precision.HIGH
FULL = lax.Precision.HIGHEST
CUTOFF = 5.0
ROOT_TWO = math.sqrt(2.0)
ROOT_THREE = math.sqrt(3.0)
ROOT_SIX = math.sqrt(6.0)
HARMONIC = math.sqrt(7.5)
RES = 1.0 / math.sqrt(2.0)


def shape_basis():
    return [
        np.array([[0.0, 1, 0], [1, 0, 0], [0, 0, 0]]) / ROOT_TWO,
        np.array([[0.0, 0, 0], [0, 0, 1], [0, 1, 0]]) / ROOT_TWO,
        np.array([[0.0, 0, 1], [0, 0, 0], [1, 0, 0]]) / ROOT_TWO,
        np.array([[1.0, 0, 0], [0, -1, 0], [0, 0, 0]]) / ROOT_TWO,
        np.array([[-1.0, 0, 0], [0, -1, 0], [0, 0, 2]]) / ROOT_SIX,
    ]


def cross_three(left_vec, right_vec):
    return np.array(
        [
            left_vec[1] * right_vec[2] - left_vec[2] * right_vec[1],
            left_vec[2] * right_vec[0] - left_vec[0] * right_vec[2],
            left_vec[0] * right_vec[1] - left_vec[1] * right_vec[0],
        ]
    )


def product_table():
    tensors = shape_basis()
    table = np.zeros((9, 9, 9))
    unit_rows = np.eye(9)
    for first in range(9):
        for second in range(9):
            left = unit_rows[first]
            right = unit_rows[second]
            left_mat = sum((left[4 + slot] * tensors[slot] for slot in range(5)))
            right_mat = sum((right[4 + slot] * tensors[slot] for slot in range(5)))
            left_vec = left[1:4]
            right_vec = right[1:4]
            scalar = left[0] * right[0] + left_vec @ right_vec + np.sum(left_mat * right_mat.T)
            vector = (
                left[0] * right_vec
                + right[0] * left_vec
                + cross_three(left_vec, right_vec)
                + left_mat @ right_vec
                + right_mat @ left_vec
            )
            matrix = (
                left[0] * right_mat
                + right[0] * left_mat
                + (np.outer(left_vec, right_vec) + np.outer(right_vec, left_vec)) / 2
                + (left_mat @ right_mat + right_mat @ left_mat) / 2
            )
            table[first, second, 0] = scalar
            table[first, second, 1:4] = vector
            for slot in range(5):
                table[first, second, 4 + slot] = np.sum(tensors[slot] * matrix)
    return (table / 3.0).astype(np.float32)


TABLE = product_table()
TERMS = [
    (a, b, k, float(TABLE[a, b, k]))
    for a in range(9)
    for b in range(9)
    for k in range(9)
    if abs(TABLE[a, b, k]) > 1e-7
]


def dot(left, right, dims, precision=HIGH):
    return lax.dot_general(left, right, ((dims[0], dims[1]), ((), ())), precision=precision)


def nn(left, right):
    return dot(left, right, ((1,), (0,)))


def tn(left, right):
    return dot(left, right, ((0,), (0,)))


def nt(left, right):
    return dot(left, right, ((1,), (1,)))


def device_of(y, x, z, core):
    return (y * 2 + x) * 8 + z * 2 + core


CUBE = [(y, x, z, c) for y in range(2) for x in range(2) for z in range(4) for c in range(2)]
HOP_X = [(device_of(y, x, z, c), device_of(y, 1 - x, z, c)) for y, x, z, c in CUBE]
HOP_Y = [(device_of(y, x, z, c), device_of(1 - y, x, z, c)) for y, x, z, c in CUBE]
HOP_XY = [(device_of(y, x, z, c), device_of(1 - y, 1 - x, z, c)) for y, x, z, c in CUBE]
HOP_CORE = [(device_of(y, x, z, c), device_of(y, x, z, 1 - c)) for y, x, z, c in CUBE]


def along_z(pairs):
    return [
        (device_of(y, x, s, c), device_of(y, x, t, c))
        for s, t in pairs
        for y in range(2)
        for x in range(2)
        for c in range(2)
    ]


HOP_IN = along_z([(0, 1), (3, 2)])
HOP_MID = along_z([(1, 2), (2, 1)])
HOP_OUT = along_z([(1, 0), (2, 3)])
HOP_Z = [along_z([(s, s ^ k) for s in range(4)]) for k in range(1, 4)]


def hop(value, pairs):
    return lax.ppermute(value, AX, pairs)


def place():
    irrep = lax.axis_index("irrep")
    edge = lax.axis_index("edge")
    return irrep // 2, irrep % 2, edge // 2, edge % 2


Z_ORDER = np.array([[3, 2, 1, 0], [3, 2, 0, 1], [0, 1, 3, 2], [0, 1, 2, 3]], np.int32)


def relative_devices():
    y, x, z, core = place()
    zs = jnp.asarray(Z_ORDER)[z]
    two = jnp.arange(2, dtype=jnp.int32)
    irrep = (two[None, :] ^ y) * 2 + (two[:, None] ^ x)
    return (
        irrep[None, :, :, None] * 8 + zs[:, None, None, None] * 2 + (two ^ core)[None, None, None, :]
    )


def reduce_chips(chunks):
    first, planes_done = [], []

    def second(p):
        (a0, a1), (b0, b1) = first[p]
        planes_done.append(
            jnp.concatenate([a0 + hop(a1, HOP_Y), b0 + hop(b1, HOP_X)], axis=0)
        )

    for p in range(4):
        block = chunks[p]
        if p >= 2:
            block, first[p - 2] = lax.optimization_barrier((block, first[p - 2]))
            second(p - 2)
        half = block.shape[2] // 2
        upper, lower = block[:, :, :half], block[:, :, half:]
        a = upper[0] + hop(upper[1], HOP_X)
        b = lower[:, 0] + hop(lower[:, 1], HOP_Y)
        first.append(((a[0], a[1]), (b[0], b[1])))
    second(2)
    second(3)
    q0, q1, q2, q3 = planes_done
    p0 = q0 + hop(q0, HOP_IN)
    p1 = q1 + hop(q1, HOP_IN)
    p2 = q2 + hop(p0, HOP_MID)
    return q3 + hop(q2, HOP_IN) + hop(p1, HOP_MID) + hop(p2, HOP_OUT), p2


def is_cube(sizes):
    return sizes == (4, 8)


def gather_small(value, sizes):
    if not is_cube(sizes):
        return lax.all_gather(value, AX, axis=0, tiled=False)
    y, x, z, core = place()
    plane = jnp.stack([value, hop(value, HOP_X), hop(value, HOP_Y), hop(value, HOP_XY)])
    column = jnp.stack([plane] + [hop(plane, pairs) for pairs in HOP_Z])
    every = jnp.stack([column, hop(column, HOP_CORE)])
    flat = every.reshape((32,) + value.shape)
    ids = np.arange(32, dtype=np.int32)
    core_of, z_of, x_of, y_of = ids % 2, ids // 2 % 4, ids // 8 % 2, ids // 16
    index = (core_of ^ core) * 16 + (z_of ^ z) * 4 + (y_of ^ y) * 2 + (x_of ^ x)
    return flat[index]


def sum_small(value, sizes):
    if not is_cube(sizes):
        return lax.psum(value, AX)
    total = value + hop(value, HOP_CORE)
    plane = total + hop(total, HOP_X) + (hop(total, HOP_Y) + hop(total, HOP_XY))
    one, two, three = [hop(plane, pairs) for pairs in HOP_Z]
    return (plane + one) + (two + three)


def geometry(vec, live):
    dist = jnp.sqrt(jnp.sum(vec * vec, axis=0))
    inv = 1.0 / dist
    unit = vec * inv[None]
    ratio = dist / CUTOFF
    r5 = ratio**5
    env = (1.0 - r5 * ratio * (28.0 - 48.0 * ratio + 21.0 * ratio * ratio)) * live
    denv = -(168.0 / CUTOFF) * r5 * (1.0 - ratio) * (1.0 - ratio) * live
    order = jnp.arange(1, NB + 1).astype(jnp.float32)[:, None] * (math.pi / CUTOFF)
    angle = order * dist[None]
    norm = math.sqrt(2.0 / CUTOFF)
    bessel = norm * jnp.sin(angle) * inv[None]
    dbessel = norm * order * jnp.cos(angle) * inv[None] - bessel * inv[None]
    return inv, unit, env, denv, bessel, dbessel


def harmonics(unit):
    x, y, z = unit
    h = HARMONIC
    return jnp.stack(
        [
            jnp.ones_like(x),
            ROOT_THREE * x,
            ROOT_THREE * y,
            ROOT_THREE * z,
            h * ROOT_TWO * x * y,
            h * ROOT_TWO * y * z,
            h * ROOT_TWO * x * z,
            h * (x * x - y * y) / ROOT_TWO,
            h * (2.0 * z * z - x * x - y * y) / ROOT_SIX,
        ]
    )


def harmonics_dot_rows(unit, dunit):
    x, y, z = unit
    dx, dy, dz = dunit
    h = HARMONIC
    return (
        [
            jnp.zeros_like(x),
            ROOT_THREE * dx,
            ROOT_THREE * dy,
            ROOT_THREE * dz,
            h * ROOT_TWO * (dx * y + x * dy),
            h * ROOT_TWO * (dy * z + y * dz),
            h * ROOT_TWO * (dx * z + x * dz),
            h * ROOT_TWO * (x * dx - y * dy),
            (2.0 * h / ROOT_SIX) * (2.0 * z * dz - x * dx - y * dy),
        ]
    )


def harmonics_back_rows(unit, bar):
    x, y, z = unit
    a, b = HARMONIC * ROOT_TWO, 2.0 * HARMONIC / ROOT_SIX
    return (
        [
            ROOT_THREE * bar[1] + a * (y * bar[4] + z * bar[6] + x * bar[7]) - b * x * bar[8],
            ROOT_THREE * bar[2] + a * (x * bar[4] + z * bar[5] - y * bar[7]) - b * y * bar[8],
            ROOT_THREE * bar[3] + a * (y * bar[5] + x * bar[6]) + 2.0 * b * z * bar[8],
        ]
    )


def harmonics_dot(unit, dunit):
    return jnp.stack(harmonics_dot_rows(unit, dunit))


def harmonics_back(unit, bar):
    return jnp.stack(harmonics_back_rows(unit, bar))


def silu(v):
    return v * jax.nn.sigmoid(v)


def silu_one(v):
    s = jax.nn.sigmoid(v)
    return s * (1.0 + v * (1.0 - s))


def silu_two(v):
    s = jax.nn.sigmoid(v)
    return s * (1.0 - s) * (2.0 + v * (1.0 - 2.0 * s))


def bilinear(sets, out, size):
    total = [None] * size
    for index in TERMS:
        a, b, k, value = index
        slot = index[out]
        for (li, left), (ri, right) in sets:
            term = left[index[li]] * right[index[ri]]
            term = value * term
            total[slot] = term if total[slot] is None else total[slot] + term
    return jnp.stack(total)


def product(feature, environ):
    return bilinear([((0, feature), (1, environ))], 2, 9)


def mix(mixing, tensor, transposed):
    op = tn if transposed else nn
    out = []
    for order, (start, stop) in enumerate(((0, 1), (1, 4), (4, 9))):
        for k in range(start, stop):
            out.append(op(mixing[order], tensor[k]))
    return jnp.stack(out)


def mix_gradient(left, right):
    out = []
    for start, stop in ((0, 1), (1, 4), (4, 9)):
        out.append(sum(nt(left[k], right[k]) for k in range(start, stop)))
    return out


def chain(weights, load_matrices, environ, force_to_tangent, vec, live, species_source, species_target):
    pair_in, pair_out, env_weight, scalar_weight, mix_weight, energy_head = weights
    head = energy_head[:D]
    factor = jnp.sum(
        energy_head[D:, None] * species_source, axis=0
    )
    inv, unit, env, denv, bessel, dbessel = geometry(vec, live)
    shape = harmonics(unit)
    feat = jnp.concatenate([bessel, species_source, species_target], axis=0)
    col = lambda v: v[:, None]
    pre0 = tn(feat, pair_in)
    hid = silu(pre0)
    out0 = nn(hid, pair_out)
    lat0 = col(env) * out0
    w0 = nt(env_weight[0], lat0)
    emb0 = shape[:, None] * w0[None]
    env0 = environ(emb0)
    res0 = product(emb0, env0)
    matrices = load_matrices(res0)
    pre1 = nn(lat0, matrices[0]) + tn(res0[0], scalar_weight[0])
    act1 = silu(pre1)
    out1 = nn(act1, matrices[1])
    lat1 = (lat0 + col(env) * out1) * RES
    w1 = nt(env_weight[1], lat1)
    emb1 = shape[:, None] * w1[None]
    env1 = environ(emb1)
    feat1 = mix(mix_weight, res0, False)
    res1 = jnp.sum(feat1 * env1, axis=0) / 3.0
    pre2 = nn(lat1, matrices[2]) + tn(res1, scalar_weight[1])
    act2 = silu(pre2)
    top = dot(matrices[3], head, ((1,), (0,)))
    slope = env * factor
    per1 = jnp.sum(lat1 * head[None], axis=1)
    per2 = jnp.sum(act2 * top[None], axis=1)
    env_bar = RES * factor * (per1 + 2.0 * env * per2)
    alpha = RES * slope
    lead = alpha * env
    slope2 = silu_one(pre2)
    pre2_bar = col(lead) * top[None] * slope2
    lat1_bar = col(alpha) * head[None] + nt(pre2_bar, matrices[2])
    res1_bar = nt(scalar_weight[1], pre2_bar)
    feat1_bar = res1_bar[None] * env1 / 3.0
    emb1_bar = environ(res1_bar[None] * feat1 / 3.0)
    shape_bar = jnp.sum(emb1_bar * w1[None], axis=1)
    w1_bar = jnp.sum(shape[:, None] * emb1_bar, axis=0)
    lat1_bar = lat1_bar + tn(w1_bar, env_weight[1])
    res0_bar = mix(mix_weight, feat1_bar, True)
    env_bar = env_bar + RES * jnp.sum(lat1_bar * out1, axis=1)
    out1_bar = RES * col(env) * lat1_bar
    act1_bar = nt(out1_bar, matrices[1])
    slope1 = silu_one(pre1)
    pre1_bar = act1_bar * slope1
    lat0_bar = RES * lat1_bar + nt(pre1_bar, matrices[0])
    res0_bar = res0_bar.at[0].add(nt(scalar_weight[0], pre1_bar))
    emb0_bar = bilinear([((2, res0_bar), (1, env0))], 0, 9) + environ(
        bilinear([((2, res0_bar), (0, emb0))], 1, 9)
    )
    shape_bar = shape_bar + jnp.sum(emb0_bar * w0[None], axis=1)
    w0_bar = jnp.sum(shape[:, None] * emb0_bar, axis=0)
    lat0_bar = lat0_bar + tn(w0_bar, env_weight[0])
    env_bar = env_bar + jnp.sum(lat0_bar * out0, axis=1)
    out0_bar = col(env) * lat0_bar
    hid_bar = nt(out0_bar, pair_out)
    slope0 = silu_one(pre0)
    pre0_bar = hid_bar * slope0
    bessel_bar = nt(pair_in[:NB], pre0_bar)
    dist_bar = env_bar * denv + jnp.sum(bessel_bar * dbessel, axis=0)
    unit_bar = harmonics_back(unit, shape_bar)
    along = jnp.sum(unit * unit_bar, axis=0)
    vec_bar = dist_bar[None] * unit + (unit_bar - unit * along[None]) * inv[None]
    vec_dot, loss_parts = force_to_tangent(vec_bar)
    dist_dot = jnp.sum(unit * vec_dot, axis=0)
    unit_dot = (vec_dot - unit * dist_dot[None]) * inv[None]
    env_dot = denv * dist_dot
    bessel_dot = dbessel * dist_dot[None]
    shape_dot = harmonics_dot(unit, unit_dot)
    pre0_dot = tn(bessel_dot, pair_in[:NB])
    hid_dot = slope0 * pre0_dot
    lat0_dot = col(env_dot) * out0 + col(env) * nn(hid_dot, pair_out)
    w0_dot = nt(env_weight[0], lat0_dot)
    emb0_dot = shape_dot[:, None] * w0[None] + shape[:, None] * w0_dot[None]
    env0_dot = environ(emb0_dot)
    res0_dot = bilinear(
        [((0, emb0_dot), (1, env0)), ((0, emb0), (1, env0_dot))], 2, 9
    )
    pre1_dot = nn(lat0_dot, matrices[0]) + tn(res0_dot[0], scalar_weight[0])
    act1_dot = slope1 * pre1_dot
    lat1_dot = (lat0_dot + col(env_dot) * out1 + col(env) * nn(act1_dot, matrices[1])) * RES
    w1_dot = nt(env_weight[1], lat1_dot)
    emb1_dot = shape_dot[:, None] * w1[None] + shape[:, None] * w1_dot[None]
    env1_dot = environ(emb1_dot)
    feat1_dot = mix(mix_weight, res0_dot, False)
    res1_dot = jnp.sum(feat1_dot * env1 + feat1 * env1_dot, axis=0) / 3.0
    pre2_dot = nn(lat1_dot, matrices[2]) + tn(res1_dot, scalar_weight[1])
    act2_dot = slope2 * pre2_dot
    lead_dot = 2.0 * RES * slope * env_dot
    last = jnp.sum(col(lead_dot) * act2 + col(lead) * act2_dot, axis=0)
    head_grad = RES * jnp.sum(
        col(factor * env_dot) * lat1 + col(slope) * lat1_dot, axis=0
    ) + jnp.sum(last[:, None] * matrices[3], axis=0)
    per1_dot = jnp.sum(lat1_dot * head[None], axis=1)
    per2_dot = jnp.sum(act2_dot * top[None], axis=1)
    energy_dot = env_dot * RES * (per1 + env * per2) + env * RES * (
        per1_dot + env_dot * per2 + env * per2_dot
    )
    scale_grad = jnp.sum(species_source * energy_dot[None], axis=1)
    head_grad = jnp.concatenate([head_grad, scale_grad])
    pre2_hat = top[None] * (col(lead_dot) * slope2 + col(lead) * silu_two(pre2) * pre2_dot)
    lat1_hat = col(RES * factor * env_dot) * head[None] + nt(pre2_hat, matrices[2])
    res1_hat = nt(scalar_weight[1], pre2_hat)
    feat1_hat = (res1_hat[None] * env1 + res1_bar[None] * env1_dot) / 3.0
    emb1_hat = environ((res1_hat[None] * feat1 + res1_bar[None] * feat1_dot) / 3.0)
    w1_hat = jnp.sum(shape_dot[:, None] * emb1_bar + shape[:, None] * emb1_hat, axis=0)
    lat1_hat = lat1_hat + tn(w1_hat, env_weight[1])
    res0_hat = mix(mix_weight, feat1_hat, True)
    out1_hat = RES * (col(env_dot) * lat1_bar + col(env) * lat1_hat)
    act1_hat = nt(out1_hat, matrices[1])
    pre1_hat = act1_hat * slope1 + act1_bar * silu_two(pre1) * pre1_dot
    lat0_hat = RES * lat1_hat + nt(pre1_hat, matrices[0])
    res0_hat = res0_hat.at[0].add(nt(scalar_weight[0], pre1_hat))
    emb0_hat = bilinear(
        [((2, res0_hat), (1, env0)), ((2, res0_bar), (1, env0_dot))], 0, 9
    ) + environ(bilinear([((2, res0_hat), (0, emb0)), ((2, res0_bar), (0, emb0_dot))], 1, 9))
    w0_hat = jnp.sum(shape_dot[:, None] * emb0_bar + shape[:, None] * emb0_hat, axis=0)
    lat0_hat = lat0_hat + tn(w0_hat, env_weight[0])
    out0_hat = col(env_dot) * lat0_bar + col(env) * lat0_hat
    pre0_hat = nt(out0_hat, pair_out) * slope0 + hid_bar * silu_two(pre0) * pre0_dot
    both = lambda first, second: jnp.concatenate([first, second], axis=0)
    pair_in_grad = nn(feat, pre0_hat)
    pair_in_grad = pair_in_grad.at[:NB].add(nn(bessel_dot, pre0_bar))
    mix_grad = jnp.stack(
        [
            first + second
            for first, second in zip(
                mix_gradient(feat1_bar, res0_dot), mix_gradient(feat1_hat, res0)
            )
        ]
    )
    env_grad = jnp.stack(
        [nn(w0_bar, lat0_dot) + nn(w0_hat, lat0), nn(w1_bar, lat1_dot) + nn(w1_hat, lat1)]
    )
    scalar_grad = jnp.stack(
        [
            nn(res0_dot[0], pre1_bar) + nn(res0[0], pre1_hat),
            nn(res1_dot, pre2_bar) + nn(res1, pre2_hat),
        ]
    )
    pair_out_grad = tn(both(hid_dot, hid), both(out0_bar, out0_hat))
    matrix_grad = [
        tn(both(lat0_dot, lat0), both(pre1_bar, pre1_hat)),
        tn(both(act1_dot, act1), both(out1_bar, out1_hat)),
        tn(both(lat1_dot, lat1), both(pre2_bar, pre2_hat)),
        last[:, None] * head[None],
    ]
    return (
        pair_in_grad,
        pair_out_grad,
        env_grad,
        scalar_grad,
        mix_grad,
        head_grad,
        matrix_grad,
        loss_parts,
    )


def split(v):
    high = v.astype(jnp.bfloat16)
    return high, (v - high.astype(jnp.float32)).astype(jnp.bfloat16)


def split_outside(v):
    high = lax.reduce_precision(v, exponent_bits=8, mantissa_bits=7)
    return high.astype(jnp.bfloat16), (v - high).astype(jnp.bfloat16)


def one_pass(left, right, dims=((1,), (0,))):
    return lax.dot_general(left, right, (dims, ((), ())), preferred_element_type=jnp.float32)


def three_pass(left, right, dims=((1,), (0,))):
    lh, ll = left
    rh, rl = right
    return one_pass(lh, rh, dims) + (one_pass(lh, rl, dims) + one_pass(ll, rh, dims))


NT = ((1,), (1,))


def exact(left, ends, dims=((1,), (0,))):
    high, low = split(left)
    rest = left - high.astype(jnp.float32) - low.astype(jnp.float32)
    return (
        one_pass(high, ends, dims)
        + one_pass(low, ends, dims)
        + one_pass(rest.astype(jnp.bfloat16), ends, dims)
    )


def kernel_call(
    body,
    ins,
    outs,
    scratch,
    late=None,
    sent=None,
    hbm=None,
    smem=None,
    hbm_out=None,
    flops=0,
    limit=60,
):
    late, sent, hbm, smem, hbm_out = late or {}, sent or {}, hbm or {}, smem or {}, hbm_out or {}
    leaves, tree = jax.tree.flatten((ins, smem, hbm, late))
    out_leaves, out_tree = jax.tree.flatten((outs, hbm_out, sent))
    buffers = jax.tree.map(lambda v: pltpu.VMEM(v.shape, v.dtype), (late, sent))
    late_count, sent_count = len(jax.tree.leaves(late)), len(jax.tree.leaves(sent))
    own = (scratch, buffers)
    own_leaves, own_tree = jax.tree.flatten(own)

    def kernel(*refs):
        n, m = len(leaves), len(leaves) + len(out_leaves)
        given = jax.tree.unflatten(tree, refs[:n])
        made = jax.tree.unflatten(out_tree, refs[n:m])
        temps, (landed, leaving) = jax.tree.unflatten(own_tree, refs[m : m + len(own_leaves)])
        sems = refs[m + len(own_leaves) :]
        r = SimpleNamespace(
            **given[0], **given[1], **given[2], **made[0], **made[1], **temps, **landed, **leaving
        )
        coming, going, started = {}, {}, []
        index = 0
        for name in sorted(late):
            sources, targets = jax.tree.leaves(given[3][name]), jax.tree.leaves(landed[name])
            coming[id(landed[name])] = []
            for source, target in zip(sources, targets):
                coming[id(landed[name])].append(
                    pltpu.make_async_copy(source, target, sems[0].at[index])
                )
                index += 1
        index = 0
        for name in sorted(sent):
            sources, targets = jax.tree.leaves(leaving[name]), jax.tree.leaves(made[2][name])
            going[id(leaving[name])] = []
            for source, target in zip(sources, targets):
                going[id(leaving[name])].append(
                    pltpu.make_async_copy(source, target, sems[1].at[index])
                )
                index += 1

        def fetch(*items):
            for item in items:
                for copy in coming[id(item)]:
                    copy.start()

        def need(*items):
            for item in items:
                for copy in coming[id(item)]:
                    copy.wait()

        def send(*items):
            for item in items:
                for copy in going[id(item)]:
                    copy.start()
                    started.append(copy)

        r.fetch, r.need, r.send = fetch, need, send
        body(r)
        for copy in started:
            copy.wait()
        assert len(started) == sent_count

    vmem, hbm_spec = pl.BlockSpec(memory_space=pltpu.VMEM), pl.BlockSpec(memory_space=pl.ANY)
    count = lambda v: len(jax.tree.leaves(v))
    in_specs = [vmem] * count(ins) + [pl.BlockSpec(memory_space=pltpu.SMEM)] * count(smem)
    in_specs += [hbm_spec] * (count(hbm) + count(late))
    out_specs = [vmem] * count(outs) + [hbm_spec] * (count(hbm_out) + count(sent))
    size = sum(v.size * v.dtype.itemsize for v in leaves + out_leaves)
    result = pl.pallas_call(
        kernel,
        out_shape=out_leaves,
        in_specs=in_specs,
        out_specs=out_specs,
        scratch_shapes=own_leaves
        + [pltpu.SemaphoreType.DMA((max(late_count, 1),)), pltpu.SemaphoreType.DMA((max(sent_count, 1),))],
        compiler_params=pltpu.CompilerParams(vmem_limit_bytes=limit * 2**20),
        cost_estimate=pl.CostEstimate(flops=flops, bytes_accessed=size, transcendentals=0),
    )(*leaves)
    made = jax.tree.unflatten(out_tree, result)
    return SimpleNamespace(**made[0], **made[1], **made[2])


def f32(*shape):
    return jax.ShapeDtypeStruct(shape, jnp.float32)


def b16(*shape):
    return jax.ShapeDtypeStruct(shape, jnp.bfloat16)


def pair_of(*shape):
    return (b16(*shape), b16(*shape))


def pair(refs, rows=None):
    high, low = refs
    return (high[...], low[...]) if rows is None else (high[rows, :], low[rows, :])


def put(refs, rows, value):
    high, low = split(value)
    refs[0][rows, :] = high
    refs[1][rows, :] = low


HALF = D // 2


class Stream:
    def __init__(self, r, sources):
        self.r, self.sources, self.step = r, sources, 0
        self.copies(0, True)

    def copies(self, step, start):
        rows = pl.ds((step % 2) * HALF, HALF)
        refs, index = self.sources[step // 2]
        for part, ref in enumerate(refs):
            view = ref.at[rows, :] if index is None else ref.at[index, rows, :]
            copy = pltpu.make_async_copy(
                view, self.r.held.at[step % 2, part, pl.ds(0, HALF)], self.r.arrived.at[step % 2, part]
            )
            copy.start() if start else copy.wait()

    def product(self, right, store, extra=None, beside=None):
        held = self.r.held
        if beside is not None:
            (weight, target), tail = beside, HALF + beside[0][0].shape[0]
            for part in range(2):
                held[1, part, HALF:tail, :] = weight[part][...]
        for half in range(2):
            step = self.step
            self.step += 1
            if step + 1 < 2 * len(self.sources):
                self.copies(step + 1, True)
            self.copies(step, False)
            rows = pl.ds(half * HALF, HALF)
            end = tail if half and beside is not None else HALF
            acc = three_pass((held[half, 0, 0:end, :], held[half, 1, 0:end, :]), pair(right))
            if end > HALF:
                target[...] = acc[HALF:, :]
                acc = acc[:HALF, :]
            if extra is not None:
                acc = acc + three_pass(pair(extra[0], rows), extra[1])
            store[rows, :] = acc


def add_small(store, weight, right):
    for half in range(2):
        rows = pl.ds(half * HALF, HALF)
        store[rows, :] += three_pass(pair(weight, rows), right)


def stream_scratch():
    return dict(
        held=pltpu.VMEM((2, 2, HALF + BS, D), jnp.bfloat16),
        arrived=pltpu.SemaphoreType.DMA((2, 2)),
    )


def each(body, carry=(), step=128, count=D):
    def run(i, state):
        return body(pl.ds(pl.multiple_of(i * step, step), step), *state)

    return lax.fori_loop(0, count // step, run, carry)


def fold(v):
    return jnp.sum(v.reshape(v.shape[0] // 8, 8, v.shape[1]), axis=0)


def planes(channels, edges, body):
    lanes = edges // 128

    def run(i, state):
        base = pl.multiple_of((i // lanes) * 16, 16)
        lane = pl.ds(pl.multiple_of((i % lanes) * 128, 128), 128)
        body(base, lane)
        return state

    lax.fori_loop(0, (channels // 16) * lanes, run, 0)


def get9(ref, channels, base, lane):
    return [ref[pl.ds(k * channels + base, 16), lane] for k in range(9)]


def put9(ref, channels, base, lane, values):
    for k, v in enumerate(values):
        ref[pl.ds(k * channels + base, 16), lane] = v


def put9_split(r, channels, base, lane, values):
    for k, v in enumerate(values):
        high, low = split(v)
        r.t_h[pl.ds(k * channels + base, 16), lane] = high
        r.t_l[pl.ds(k * channels + base, 16), lane] = low


def row9(ref, lane):
    return [ref[k : k + 1, lane] for k in range(9)]


def terms_sum(sets, out):
    total = [None] * 9
    pairs = {}
    for index in TERMS:
        for n, ((li, left), (ri, right)) in enumerate(sets):
            key = (n, index[li], index[ri])
            if key not in pairs:
                pairs[key] = left[index[li]] * right[index[ri]]
    for index in TERMS:
        for n, ((li, left), (ri, right)) in enumerate(sets):
            term = index[3] * pairs[(n, index[li], index[ri])]
            slot = index[out]
            total[slot] = term if total[slot] is None else total[slot] + term
    return total


TILE9 = 192


def same_atom(r, scale, store, rows9):
    @pl.loop(0, rows9 // TILE9)
    def _(t):
        rows = pl.ds(pl.multiple_of(t * TILE9, TILE9), TILE9)
        store[rows, :] = scale * (
            one_pass(r.t_h[rows, :], r.same[...]) + one_pass(r.t_l[rows, :], r.same[...])
        )


def mixed(r, mixing, store, rows9):
    @pl.loop(0, rows9 // TILE9)
    def _(t):
        rows = pl.ds(pl.multiple_of(t * TILE9, TILE9), TILE9)
        store[rows, :] = three_pass(pair(mixing, rows), (r.t_h[...], r.t_l[...]))


def clear_tail(r, rows9):
    tail = r.t_h.shape[0] - rows9
    r.t_h[rows9:, :] = jnp.zeros((tail, r.t_h.shape[1]), jnp.bfloat16)
    r.t_l[rows9:, :] = jnp.zeros((tail, r.t_l.shape[1]), jnp.bfloat16)


def plane_scratch(rows9, edges):
    depth = -(-rows9 // 128) * 128
    return dict(
        t_h=pltpu.VMEM((depth, edges), jnp.bfloat16), t_l=pltpu.VMEM((depth, edges), jnp.bfloat16)
    )


def sig(v):
    return 1.0 / (1.0 + jnp.exp(-v))


def silu_parts(v):
    s = sig(v)
    return v * s, s * (1.0 + v * (1.0 - s))


def silu_slopes(v):
    s = sig(v)
    t = 1.0 - s
    return s * (1.0 + v * t), s * t * (2.0 + v * (t - s))


def first_layer(r, channels, edges, scale):
    rows9 = 9 * channels
    stream = Stream(r, [(r.out_t, None)])
    feat = split(r.feat[...])

    @pl.loop(0, 2)
    def _(t):
        rows = pl.ds(pl.multiple_of(t * 512, 512), 512)
        r.pre0[rows, :] = three_pass(pair(r.in_t, rows), feat)

    def hidden(rows):
        put(r.hid, rows, silu_parts(r.pre0[rows, :])[0])
        return ()

    r.send(r.pre0)
    each(hidden)
    r.send(r.hid)
    stream.product(r.hid, r.out0)

    def latent(rows):
        put(r.lat0, rows, r.rows[0:1, :] * r.out0[rows, :])
        return ()

    r.send(r.out0)
    each(latent)
    r.send(r.lat0)
    r.w0[...] = three_pass(pair(r.env0w), pair(r.lat0))

    def embed(base, lane):
        w = r.w0[pl.ds(base, 16), lane]
        put9_split(r, channels, base, lane, [y * w for y in row9(r.shape, lane)])

    planes(channels, edges, embed)
    same_atom(r, scale, r.env0, rows9)
    r.send(r.env0)

    def multiply(base, lane):
        w = r.w0[pl.ds(base, 16), lane]
        emb = [y * w for y in row9(r.shape, lane)]
        env = get9(r.env0, channels, base, lane)
        put9(r.res0, channels, base, lane, terms_sum([((0, emb), (1, env))], 2))

    planes(channels, edges, multiply)
    r.send(r.res0)


def energy_up(r, channels, edges, scale):
    rows9 = 9 * channels
    env, factor = lambda: r.rows[0:1, :], lambda: r.rows[1:2, :]
    alpha = lambda: RES * r.rows[0:1, :] * r.rows[1:2, :]
    stream = Stream(
        r,
        [
            (r.mt, 0),
            (r.mt, 1),
            (r.mt, 2),
        ],
    )
    r.fetch(r.out0, r.mix)
    clear_tail(r, rows9)
    nothing = jnp.zeros((8, edges), jnp.float32)
    stream.product(r.lat0, r.pre1, (r.sc0_t, split(r.res0[0:channels, :])))

    def act1(rows):
        put(r.act1, rows, silu_parts(r.pre1[rows, :])[0])
        return ()

    r.send(r.pre1)
    each(act1)
    r.send(r.act1)
    stream.product(r.act1, r.out1)

    def lat1(rows, per):
        value = RES * env() * (r.out0[rows, :] + r.out1[rows, :])
        put(r.lat1, rows, value)
        return (per + fold(value * r.head[rows, :]),)

    r.send(r.out1)
    r.need(r.out0)
    (per1,) = each(lat1, (nothing,))
    r.send(r.lat1)
    stream.product(r.lat1, r.pre2, beside=(r.env1w, r.w1))

    def embed(base, lane):
        w = r.w1[pl.ds(base, 16), lane]
        put9_split(r, channels, base, lane, [y * w for y in row9(r.shape, lane)])

    planes(channels, edges, embed)
    same_atom(r, scale, r.env1, rows9)
    r.send(r.env1)

    def take(base, lane):
        put9_split(r, channels, base, lane, get9(r.res0, channels, base, lane))

    planes(channels, edges, take)
    r.need(r.mix)
    mixed(r, r.mix, r.feat1, rows9)
    r.send(r.feat1)

    def scalar(base, lane):
        f, e = get9(r.feat1, channels, base, lane), get9(r.env1, channels, base, lane)
        r.res1[pl.ds(base, 16), lane] = sum(a * b for a, b in zip(f, e)) * (1.0 / 3.0)

    planes(channels, edges, scalar)
    add_small(r.pre2, r.sc1_t, split(r.res1[...]))

    def act2(rows, per):
        act, slope = silu_parts(r.pre2[rows, :])
        put(r.pre2_bar, rows, (alpha() * env()) * r.top[rows, :] * slope)
        return (per + fold(act * r.top[rows, :]),)

    r.send(r.pre2)
    (per2,) = each(act2, (nothing,))
    r.send(r.pre2_bar)
    per1 = jnp.sum(per1, axis=0, keepdims=True)
    per2 = jnp.sum(per2, axis=0, keepdims=True)
    r.per[...] = jnp.zeros_like(r.per)
    r.per[0:1, :] = per1
    r.per[1:2, :] = per2


def energy_down(r, channels, edges, scale):
    rows9 = 9 * channels
    env, factor = lambda: r.rows[0:1, :], lambda: r.rows[1:2, :]
    alpha = lambda: RES * r.rows[0:1, :] * r.rows[1:2, :]
    stream = Stream(r, [(r.m, 2), (r.m, 1), (r.m, 0), (r.out, None)])
    r.fetch(r.feat1, r.env1)
    clear_tail(r, rows9)
    nothing = jnp.zeros((8, edges), jnp.float32)
    stream.product(r.pre2_bar, r.lat1_bar, beside=(r.sc1, r.res1_bar))
    r.fetch(r.out1, r.mix_t, r.pre1)
    r.need(r.feat1, r.env1)

    def back1(base, lane):
        g = r.res1_bar[pl.ds(base, 16), lane] * (1.0 / 3.0)
        put9_split(r, channels, base, lane, [g * f for f in get9(r.feat1, channels, base, lane)])
        put9(r.feat1_bar, channels, base, lane, [g * e for e in get9(r.env1, channels, base, lane)])

    planes(channels, edges, back1)
    r.send(r.feat1_bar)
    same_atom(r, scale, r.emb1_bar, rows9)
    r.send(r.emb1_bar)
    r.shape_bar[...] = jnp.zeros_like(r.shape_bar)

    def collect(w_ref, emb_ref, out_ref):
        def run(base, lane):
            w = w_ref[pl.ds(base, 16), lane]
            emb = get9(emb_ref, channels, base, lane)
            out_ref[pl.ds(base, 16), lane] = sum(y * v for y, v in zip(row9(r.shape, lane), emb))
            for k in range(9):
                r.shape_bar[k : k + 1, lane] += jnp.sum(emb[k] * w, axis=0, keepdims=True)

        planes(channels, edges, run)

    collect(r.w1, r.emb1_bar, r.w1_bar)
    w_pair = split(r.w1_bar[...])

    @pl.loop(0, 2)
    def _(t):
        rows = pl.ds(pl.multiple_of(t * 512, 512), 512)
        r.lat1_bar[rows, :] += three_pass(pair(r.env1w_t, rows), w_pair)

    def out1_bar(rows, total):
        value = r.lat1_bar[rows, :] + alpha() * r.head[rows, :]
        r.lat1_bar[rows, :] = value
        put(r.out1_bar, rows, (RES * env()) * value)
        return (total + fold(value * r.out1[rows, :]),)

    r.need(r.out1)
    (env_bar1,) = each(out1_bar, (nothing,))
    r.send(r.lat1_bar, r.out1_bar)
    r.fetch(r.env0, r.out0)
    stream.product(r.out1_bar, r.act1_bar)
    r.send(r.act1_bar)
    r.need(r.mix_t)

    def take_bar(base, lane):
        put9_split(r, channels, base, lane, get9(r.feat1_bar, channels, base, lane))

    planes(channels, edges, take_bar)
    mixed(r, r.mix_t, r.res0_bar, rows9)

    def pre1_bar(rows):
        put(r.pre1_bar, rows, r.act1_bar[rows, :] * silu_parts(r.pre1[rows, :])[1])
        return ()

    r.need(r.pre1)
    each(pre1_bar)
    r.send(r.pre1_bar)
    stream.product(r.pre1_bar, r.lat0_bar, beside=(r.sc0, r.w0_bar))
    r.res0_bar[0:channels, :] += r.w0_bar[...]
    r.send(r.res0_bar)
    r.fetch(r.pre0)

    def back0(base, lane):
        w = r.w0[pl.ds(base, 16), lane]
        emb = [y * w for y in row9(r.shape, lane)]
        g = get9(r.res0_bar, channels, base, lane)
        put9_split(r, channels, base, lane, terms_sum([((2, g), (0, emb))], 1))

    planes(channels, edges, back0)
    same_atom(r, scale, r.emb0_bar, rows9)

    def back0_feature(base, lane):
        g = get9(r.res0_bar, channels, base, lane)
        e = get9(r.env0, channels, base, lane)
        more = terms_sum([((2, g), (1, e))], 0)
        have = get9(r.emb0_bar, channels, base, lane)
        put9(r.emb0_bar, channels, base, lane, [a + b for a, b in zip(have, more)])

    r.need(r.env0)
    planes(channels, edges, back0_feature)
    r.send(r.emb0_bar)
    collect(r.w0, r.emb0_bar, r.w0_bar)
    w_pair0 = split(r.w0_bar[...])

    @pl.loop(0, 2)
    def _(t):
        rows = pl.ds(pl.multiple_of(t * 512, 512), 512)
        r.lat0_bar[rows, :] += three_pass(pair(r.env0w_t, rows), w_pair0)

    def out0_bar(rows, total):
        value = r.lat0_bar[rows, :] + RES * r.lat1_bar[rows, :]
        r.lat0_bar[rows, :] = value
        put(r.out0_bar, rows, env() * value)
        return (total + fold(value * r.out0[rows, :]),)

    r.need(r.out0)
    (env_bar0,) = each(out0_bar, (nothing,))
    r.send(r.lat0_bar, r.out0_bar)
    stream.product(r.out0_bar, r.hid_bar)

    def pre0_bar(rows):
        put(r.pre0_bar, rows, r.hid_bar[rows, :] * silu_parts(r.pre0[rows, :])[1])
        return ()

    r.send(r.hid_bar)
    r.need(r.pre0)
    each(pre0_bar)
    r.send(r.pre0_bar)
    r.bessel_bar[...] = three_pass(pair(r.in_w), pair(r.pre0_bar))
    down = lambda v: jnp.sum(v, axis=0, keepdims=True)
    env_bar = (
        RES * factor() * (r.per[0:1, :] + 2.0 * env() * r.per[1:2, :])
        + RES * down(env_bar1)
        + down(env_bar0)
    )
    row = lambda ref, k: ref[k : k + 1, :]
    unit = [row(r.geo, k) for k in range(3)]
    dist_bar = env_bar * row(r.geo, 4) + down(r.bessel_bar[0:NB, :] * r.dbessel[0:NB, :])
    unit_bar = harmonics_back_rows(unit, [row(r.shape_bar, k) for k in range(9)])
    along = sum(u * b for u, b in zip(unit, unit_bar))
    r.vec_bar[...] = jnp.zeros_like(r.vec_bar)
    for k in range(3):
        r.vec_bar[k : k + 1, :] = dist_bar * unit[k] + (unit_bar[k] - unit[k] * along) * row(r.geo, 3)
    r.force_part[...] = exact(r.vec_bar[...], r.ends[...])


def tangent_up(r, channels, edges, scale):
    rows9 = 9 * channels
    env, factor, env_dot = (
        lambda: r.rows[0:1, :],
        lambda: r.rows[1:2, :],
        lambda: r.env_row[0:1, :],
    )
    lead = lambda: RES * env() * env() * factor()
    lead_dot = lambda: 2.0 * RES * env() * factor() * env_dot()
    stream = Stream(
        r,
        [
            (r.out_t, None),
            (r.mt, 0),
            (r.mt, 1),
            (r.mt, 2),
        ],
    )
    r.fetch(r.pre0, r.out0)
    clear_tail(r, rows9)
    nothing = jnp.zeros((8, edges), jnp.float32)
    row = lambda ref, k: ref[k : k + 1, :]
    residual = [row(r.force, k) - row(r.label, k) for k in range(3)]
    r.loss_part[...] = row(r.label, 3) * sum(v * v for v in residual)
    r.cot[...] = jnp.zeros_like(r.cot)
    for k in range(3):
        r.cot[k : k + 1, :] = row(r.label, 4) * residual[k]
    vec_dot = exact(r.cot[...], r.ends[...], NT)
    vec_dot = [vec_dot[k : k + 1, :] for k in range(3)]
    unit = [row(r.geo, k) for k in range(3)]
    dist_dot = sum(u * v for u, v in zip(unit, vec_dot))
    unit_dot = [(v - u * dist_dot) * row(r.geo, 3) for u, v in zip(unit, vec_dot)]
    r.env_row[...] = jnp.broadcast_to(row(r.geo, 4) * dist_dot, r.env_row.shape)
    r.bessel_dot[...] = r.dbessel[...] * dist_dot
    r.shape_dot[...] = jnp.zeros_like(r.shape_dot)
    for k, value in enumerate(harmonics_dot_rows(unit, unit_dot)):
        r.shape_dot[k : k + 1, :] = value
    bessel = split(r.bessel_dot[...])

    @pl.loop(0, 2)
    def _(t):
        rows = pl.ds(pl.multiple_of(t * 512, 512), 512)
        r.pre0_dot[rows, :] = three_pass(pair(r.in_t, rows), bessel)

    def hidden(rows):
        put(r.hid_dot, rows, r.pre0_dot[rows, :] * silu_parts(r.pre0[rows, :])[1])
        return ()

    r.send(r.pre0_dot)
    r.need(r.pre0)
    each(hidden)
    r.send(r.hid_dot)
    r.fetch(r.env0)
    stream.product(r.hid_dot, r.tmp)

    def lat0(rows):
        value = env_dot() * r.out0[rows, :] + env() * r.tmp[rows, :]
        r.keep[rows, :] = value
        put(r.lat0_dot, rows, value)
        return ()

    r.need(r.out0)
    each(lat0)
    r.send(r.lat0_dot)
    r.fetch(r.pre1, r.out1)
    stream.product(r.lat0_dot, r.pre1_dot, beside=(r.env0w, r.w0_dot))

    def embed_dot(w_ref, w_dot_ref, base, lane):
        w, wd = w_ref[pl.ds(base, 16), lane], w_dot_ref[pl.ds(base, 16), lane]
        return [
            yd * w + y * wd for y, yd in zip(row9(r.shape, lane), row9(r.shape_dot, lane))
        ]

    def embed0(base, lane):
        put9_split(r, channels, base, lane, embed_dot(r.w0, r.w0_dot, base, lane))

    planes(channels, edges, embed0)
    same_atom(r, scale, r.env0_dot, rows9)
    r.send(r.env0_dot)
    r.need(r.env0)

    def multiply(base, lane):
        w = r.w0[pl.ds(base, 16), lane]
        emb = [y * w for y in row9(r.shape, lane)]
        emb_dot = embed_dot(r.w0, r.w0_dot, base, lane)
        e, ed = get9(r.env0, channels, base, lane), get9(r.env0_dot, channels, base, lane)
        put9(
            r.res0_dot,
            channels,
            base,
            lane,
            terms_sum([((0, emb_dot), (1, e)), ((0, emb), (1, ed))], 2),
        )

    planes(channels, edges, multiply)
    r.send(r.res0_dot)
    r.fetch(r.lat1, r.mix)
    add_small(r.pre1_dot, r.sc0_t, split(r.res0_dot[0:channels, :]))

    def act1(rows):
        put(r.act1_dot, rows, r.pre1_dot[rows, :] * silu_parts(r.pre1[rows, :])[1])
        return ()

    r.send(r.pre1_dot)
    r.need(r.pre1)
    each(act1)
    r.send(r.act1_dot)
    r.fetch(r.feat1, r.env1, r.pre2)
    stream.product(r.act1_dot, r.tmp)

    def lat1(rows, per):
        value = RES * (
            r.keep[rows, :] + env_dot() * r.out1[rows, :] + env() * r.tmp[rows, :]
        )
        put(r.lat1_dot, rows, value)
        lat = r.lat1[0][rows, :].astype(jnp.float32) + r.lat1[1][rows, :].astype(jnp.float32)
        part = factor() * (env_dot() * lat + env() * value)
        r.head_part[rows, :] = sum(part[:, s : s + 128] for s in range(0, edges, 128))
        return (per + fold(value * r.head[rows, :]),)

    r.need(r.out1, r.lat1)
    (per1,) = each(lat1, (nothing,))
    r.send(r.lat1_dot)
    stream.product(r.lat1_dot, r.tmp, beside=(r.env1w, r.w1_dot))

    def embed1(base, lane):
        put9_split(r, channels, base, lane, embed_dot(r.w1, r.w1_dot, base, lane))

    planes(channels, edges, embed1)
    same_atom(r, scale, r.env1_dot, rows9)
    r.send(r.env1_dot)
    r.need(r.mix)

    def take(base, lane):
        put9_split(r, channels, base, lane, get9(r.res0_dot, channels, base, lane))

    planes(channels, edges, take)
    mixed(r, r.mix, r.feat1_dot, rows9)
    r.send(r.feat1_dot)
    r.need(r.feat1, r.env1)

    def scalar(base, lane):
        f, fd = get9(r.feat1, channels, base, lane), get9(r.feat1_dot, channels, base, lane)
        e, ed = get9(r.env1, channels, base, lane), get9(r.env1_dot, channels, base, lane)
        total = sum(fd[k] * e[k] + f[k] * ed[k] for k in range(9))
        r.res1_dot[pl.ds(base, 16), lane] = total * (1.0 / 3.0)

    planes(channels, edges, scalar)
    add_small(r.tmp, r.sc1_t, split(r.res1_dot[...]))

    def act2(rows, per):
        v, vd, top = r.pre2[rows, :], r.tmp[rows, :], r.top[rows, :]
        s = sig(v)
        t = 1.0 - s
        slope, curve = s * (1.0 + v * t), s * t * (2.0 + v * (t - s))
        act_dot = slope * vd
        part = lead_dot() * (v * s) + lead() * act_dot
        r.last_part[rows, :] = sum(part[:, k : k + 128] for k in range(0, edges, 128))
        put(r.pre2_hat, rows, top * (lead_dot() * slope + lead() * curve * vd))
        return (per + fold(act_dot * top),)

    r.need(r.pre2)
    (per2,) = each(act2, (nothing,))
    r.send(r.pre2_hat)
    r.per_dot[...] = jnp.zeros_like(r.per_dot)
    r.per_dot[0:1, :] = jnp.sum(per1, axis=0, keepdims=True)
    r.per_dot[1:2, :] = jnp.sum(per2, axis=0, keepdims=True)


def tangent_down(r, channels, edges, scale):
    rows9 = 9 * channels
    env, factor, env_dot = (
        lambda: r.rows[0:1, :],
        lambda: r.rows[1:2, :],
        lambda: r.env_row[0:1, :],
    )
    stream = Stream(
        r,
        [
            (r.m, 2),
            (r.m, 1),
            (r.m, 0),
            (r.out, None),
        ],
    )
    r.fetch(r.feat1, r.feat1_dot, r.env1, r.env1_dot)
    clear_tail(r, rows9)
    stream.product(r.pre2_hat, r.hat1, beside=(r.sc1, r.small))
    r.fetch(r.emb1_bar, r.lat1_bar)
    r.need(r.feat1, r.feat1_dot, r.env1, r.env1_dot)

    def back1(base, lane):
        gh = r.small[pl.ds(base, 16), lane] * (1.0 / 3.0)
        g = r.res1_bar[pl.ds(base, 16), lane] * (1.0 / 3.0)
        f, fd = get9(r.feat1, channels, base, lane), get9(r.feat1_dot, channels, base, lane)
        e, ed = get9(r.env1, channels, base, lane), get9(r.env1_dot, channels, base, lane)
        put9_split(r, channels, base, lane, [gh * f[k] + g * fd[k] for k in range(9)])
        put9(r.feat1_hat, channels, base, lane, [gh * e[k] + g * ed[k] for k in range(9)])

    planes(channels, edges, back1)
    r.send(r.feat1_hat)
    r.fetch(r.mix_t, r.pre1, r.act1_bar, r.pre1_dot)
    same_atom(r, scale, r.plane, rows9)

    def collect(bar_ref, out_ref):
        def run(base, lane):
            bar = get9(bar_ref, channels, base, lane)
            hat = get9(r.plane, channels, base, lane)
            y, yd = row9(r.shape, lane), row9(r.shape_dot, lane)
            out_ref[pl.ds(base, 16), lane] = sum(
                yd[k] * bar[k] + y[k] * hat[k] for k in range(9)
            )

        planes(channels, edges, run)

    r.need(r.emb1_bar)
    collect(r.emb1_bar, r.w1_hat)
    w_pair = split(r.w1_hat[...])

    @pl.loop(0, 2)
    def _(t):
        rows = pl.ds(pl.multiple_of(t * 512, 512), 512)
        r.hat1[rows, :] += three_pass(pair(r.env1w_t, rows), w_pair)

    def out1(rows):
        value = r.hat1[rows, :] + (RES * factor() * env_dot()) * r.head[rows, :]
        r.hat1[rows, :] = value
        put(r.out1_hat, rows, RES * (env_dot() * r.lat1_bar[rows, :] + env() * value))
        return ()

    r.need(r.lat1_bar)
    each(out1)
    r.send(r.out1_hat)
    r.fetch(r.res0_bar, r.env0, r.env0_dot)
    stream.product(r.out1_hat, r.tmp)
    r.need(r.mix_t)

    def take(base, lane):
        put9_split(r, channels, base, lane, get9(r.feat1_hat, channels, base, lane))

    planes(channels, edges, take)
    mixed(r, r.mix_t, r.res0_hat, rows9)

    def pre1(rows):
        slope, curve = silu_slopes(r.pre1[rows, :])
        put(
            r.pre1_hat,
            rows,
            r.tmp[rows, :] * slope + r.act1_bar[rows, :] * curve * r.pre1_dot[rows, :],
        )
        return ()

    r.need(r.pre1, r.act1_bar, r.pre1_dot)
    each(pre1)
    r.send(r.pre1_hat)
    r.fetch(r.emb0_bar, r.lat0_bar)
    stream.product(r.pre1_hat, r.tmp, beside=(r.sc0, r.small))
    r.res0_hat[0:channels, :] += r.small[...]

    def embed_pair(base, lane):
        w, wd = r.w0[pl.ds(base, 16), lane], r.w0_dot[pl.ds(base, 16), lane]
        y, yd = row9(r.shape, lane), row9(r.shape_dot, lane)
        emb = [a * w for a in y]
        emb_dot = [b * w + a * wd for a, b in zip(y, yd)]
        return emb, emb_dot

    def back0(base, lane):
        emb, emb_dot = embed_pair(base, lane)
        gh, g = get9(r.res0_hat, channels, base, lane), get9(r.res0_bar, channels, base, lane)
        put9_split(
            r, channels, base, lane, terms_sum([((2, gh), (0, emb)), ((2, g), (0, emb_dot))], 1)
        )

    r.need(r.res0_bar)
    planes(channels, edges, back0)
    r.fetch(r.pre0, r.hid_bar, r.pre0_dot)
    same_atom(r, scale, r.plane, rows9)

    def back0_feature(base, lane):
        gh, g = get9(r.res0_hat, channels, base, lane), get9(r.res0_bar, channels, base, lane)
        e, ed = get9(r.env0, channels, base, lane), get9(r.env0_dot, channels, base, lane)
        more = terms_sum([((2, gh), (1, e)), ((2, g), (1, ed))], 0)
        have = get9(r.plane, channels, base, lane)
        put9(r.plane, channels, base, lane, [a + b for a, b in zip(have, more)])

    r.need(r.env0, r.env0_dot)
    planes(channels, edges, back0_feature)
    r.need(r.emb0_bar)
    collect(r.emb0_bar, r.w0_hat)
    w_pair0 = split(r.w0_hat[...])

    @pl.loop(0, 2)
    def _(t):
        rows = pl.ds(pl.multiple_of(t * 512, 512), 512)
        r.tmp[rows, :] += three_pass(pair(r.env0w_t, rows), w_pair0)

    def out0(rows):
        value = r.tmp[rows, :] + RES * r.hat1[rows, :]
        put(r.out0_hat, rows, env_dot() * r.lat0_bar[rows, :] + env() * value)
        return ()

    r.need(r.lat0_bar)
    each(out0)
    r.send(r.out0_hat)
    stream.product(r.out0_hat, r.tmp)

    def pre0(rows):
        slope, curve = silu_slopes(r.pre0[rows, :])
        put(
            r.pre0_hat,
            rows,
            r.tmp[rows, :] * slope + r.hid_bar[rows, :] * curve * r.pre0_dot[rows, :],
        )
        return ()

    r.need(r.pre0, r.hid_bar, r.pre0_dot)
    each(pre0)
    r.send(r.pre0_hat)


def small_gradients(r, channels, edges):
    r.fetch(r.hid, r.out0_hat, r.pre0_bar, r.pre0_hat)
    tiles = [pl.ds(t * HALF, HALF) for t in range(2)]
    for rows in tiles:
        r.out_grad[rows, :] = three_pass(pair(r.hid_dot, rows), pair(r.out0_bar), NT)
    r.need(r.hid, r.out0_hat)
    for rows in tiles:
        r.out_grad[rows, :] += three_pass(pair(r.hid, rows), pair(r.out0_hat), NT)
    r.send(r.out_grad)
    r.need(r.pre0_bar, r.pre0_hat)
    r.fetch(r.feat1_bar, r.res0_dot, r.feat1_hat, r.res0)
    r.in_grad[...] = three_pass(split(r.bessel_dot[...]), pair(r.pre0_bar), NT) + three_pass(
        split(r.feat[...]), pair(r.pre0_hat), NT
    )
    r.fetch(r.lat0_dot, r.lat0, r.pre1_bar, r.pre1_hat)

    def twice(first, second, third, fourth):
        return three_pass(split(first), pair(second), NT) + three_pass(split(third), pair(fourth), NT)

    r.need(r.feat1_bar, r.res0_dot, r.feat1_hat, r.res0)
    r.fetch(r.lat1_dot, r.lat1, r.pre2_bar, r.pre2_hat)
    r.need(r.lat0_dot, r.lat0, r.pre1_bar, r.pre1_hat)
    r.env_grad[0] = twice(r.w0_bar[...], r.lat0_dot, r.w0_hat[...], r.lat0)
    r.sc_grad[0] = twice(r.res0_dot[0:channels, :], r.pre1_bar, r.res0[0:channels, :], r.pre1_hat)
    r.need(r.lat1_dot, r.lat1, r.pre2_bar, r.pre2_hat)
    r.env_grad[1] = twice(r.w1_bar[...], r.lat1_dot, r.w1_hat[...], r.lat1)
    r.sc_grad[1] = twice(r.res1_dot[...], r.pre2_bar, r.res1[...], r.pre2_hat)
    for order, (start, stop) in enumerate(((0, 1), (1, 4), (4, 9))):
        total = None
        for k in range(start, stop):
            part = slice(k * channels, (k + 1) * channels)
            term = three_pass(split(r.feat1_bar[part, :]), split(r.res0_dot[part, :]), NT)
            term = term + three_pass(split(r.feat1_hat[part, :]), split(r.res0[part, :]), NT)
            total = term if total is None else total + term
        r.mix_grad[order] = total


def load_blocks(r):
    depth = 3

    def incoming(step):
        slot = lax.rem(step, depth)
        return [
            pltpu.make_async_copy(
                r.piece.at[r.where[step * SIDE + j]], r.blocks.at[slot, j], r.sem.at[slot, j]
            )
            for j in range(SIDE)
        ]

    def outgoing(step):
        slot, m, i = step % 2, step // SIDE, step % SIDE
        rows = pl.ds(pl.multiple_of(i * BS, BS), BS)
        plain = [
            pltpu.make_async_copy(
                r.flat.at[slot, part], r.m[part].at[m, rows, :], r.out_sem.at[slot, part]
            )
            for part in range(2)
        ]
        turned = [
            pltpu.make_async_copy(
                r.turned.at[slot, part], r.mt[part].at[m, :, rows], r.out_sem.at[slot, 2 + part]
            )
            for part in range(2)
        ]
        return plain + turned

    steps = 3 * SIDE
    for step in range(depth - 1):
        for copy in incoming(step):
            copy.start()
    eye = (
        lax.broadcasted_iota(jnp.int32, (BS, BS), 0) == lax.broadcasted_iota(jnp.int32, (BS, BS), 1)
    ).astype(jnp.bfloat16)

    @pl.loop(0, steps)
    def _(step):
        @pl.when(step + depth - 1 < steps)
        def _():
            for copy in incoming(step + depth - 1):
                copy.start()

        for copy in incoming(step):
            copy.wait()

        @pl.when(step >= 2)
        def _():
            for copy in outgoing(step - 2):
                copy.wait()

        slot, source = step % 2, lax.rem(step, depth)
        for j in range(SIDE):
            part = slice(j * BS, (j + 1) * BS)
            high, low = split(r.blocks[source, j])
            r.flat[slot, 0, :, part] = high
            r.flat[slot, 1, :, part] = low
            r.turned[slot, 0, part, :] = one_pass(eye, high, NT).astype(jnp.bfloat16)
            r.turned[slot, 1, part, :] = low.T
        for copy in outgoing(step):
            copy.start()

    def last(i):
        return [
            pltpu.make_async_copy(
                r.piece.at[r.where[(3 * SIDE + i) * SIDE + j]],
                r.last.at[pl.ds(i * BS, BS), pl.ds(j * BS, BS)],
                r.last_sem.at[i, j],
            )
            for j in range(SIDE)
        ]

    for i in range(SIDE):
        for copy in last(i):
            copy.start()
    for step in (steps - 2, steps - 1):
        for copy in outgoing(step):
            copy.wait()
    head = r.head[...]
    for i in range(SIDE):
        for copy in last(i):
            copy.wait()

    def top(rows):
        r.top[rows, :] = jnp.sum(r.last[rows, :] * head, axis=1, keepdims=True)
        return ()

    each(top)


def block_gradients(r, channels, edges, targets):
    names = [(r.lat0_dot, r.lat0, r.pre1_bar, r.pre1_hat)]
    names.append((r.act1_dot, r.act1, r.out1_bar, r.out1_hat))
    names.append((r.lat1_dot, r.lat1, r.pre2_bar, r.pre2_hat))
    tile = HALF
    count = tile // BS * SIDE

    def incoming(m):
        return [
            pltpu.make_async_copy(ref, r.held.at[m % 2, a, part], r.arrived.at[m % 2, a, part])
            for a, refs in enumerate(names[m])
            for part, ref in enumerate(refs)
        ]

    for copy in incoming(0):
        copy.start()

    def spot(q):
        rows = pl.ds(pl.multiple_of((q // SIDE) * BS, BS), BS)
        return rows, pl.ds(pl.multiple_of((q % SIDE) * BS, BS), BS)

    def wait_tile(slot):
        whole = r.out[0].at[pl.ds(0, count)]
        pltpu.make_async_copy(whole, whole, r.sent_sem.at[slot]).wait()

    def send_tile(first, slot):
        def one(q, state):
            which, where = r.which[first + q], r.where[first + q]
            for n in range(targets):

                @pl.when(which == n)
                def _(n=n):
                    pltpu.make_async_copy(
                        r.stage.at[slot, *spot(q)], r.out[n].at[where], r.sent_sem.at[slot]
                    ).start()

            return state

        lax.fori_loop(0, count, one, 0)

    for m in (3, 0, 1, 2):
        if m < 3:
            if m + 1 < 3:
                for copy in incoming(m + 1):
                    copy.start()
            for copy in incoming(m):
                copy.wait()
            held = lambda a, which=slice(None): (
                r.held[m % 2, a, 0, which, :],
                r.held[m % 2, a, 1, which, :],
            )
        for t in range(2):
            if m != 3:
                wait_tile(t)
            rows = pl.ds(t * tile, tile)
            if m < 3:
                r.stage[t] = three_pass(held(0, rows), held(2), NT) + three_pass(
                    held(1, rows), held(3), NT
                )
            else:
                r.stage[t] = r.lead[rows, :] * r.head[...]
            send_tile((m * SIDE + t * (tile // BS)) * SIDE, t)
    wait_tile(0)
    wait_tile(1)


def soap_kernel(count, *refs):
    grad, weight, first, second, left, right, lstat, rstat, average = refs[:9]
    outs = refs[9:]
    tn_dims = ((0,), (0,))

    def mm(a, b, dims=((1,), (0,))):
        return [three_pass(split(x), split(y), dims) for x, y in zip(a, b)]

    load = lambda ref: [ref[s] for s in range(count)]
    g, l, rr = load(grad), load(left), load(right)
    rotated = mm(mm(l, g, tn_dims), rr)
    first_new = [0.9 * first[s] + 0.1 * rotated[s] for s in range(count)]
    second_new = [0.99 * second[s] + 0.01 * rotated[s] * rotated[s] for s in range(count)]
    normal = [
        a * (1.0 / (1.0 - 0.9**ADAM_STEP)) / (jnp.sqrt(b * (1.0 / (1.0 - 0.99**ADAM_STEP))) + 1e-08)
        for a, b in zip(first_new, second_new)
    ]
    step = mm(mm(l, normal), rr, NT)
    for s in range(count):
        new = weight[s] - 0.01 * (step[s] + 0.01 * weight[s])
        outs[0][s] = new
        outs[7][s] = 0.99 * average[s] + 0.01 * new
        outs[2][s] = second_new[s]
    plain = mm(mm(l, first_new), rr, NT)
    ls = [0.95 * lstat[s] + 0.05 * v for s, v in enumerate(mm(g, g, NT))]
    rs = [0.95 * rstat[s] + 0.05 * v for s, v in enumerate(mm(g, g, tn_dims))]
    for s in range(count):
        outs[5][s] = ls[s]
        outs[6][s] = rs[s]
    x = mm(ls, l) + mm(rs, rr)
    x = [v / jnp.sqrt(jnp.sum(v * v)) for v in x]
    for _ in range(NS_STEPS):
        x = [1.5 * a - 0.5 * b for a, b in zip(x, mm(mm(x, x, NT), x))]
    ln, rn = x[:count], x[count:]
    out = mm(mm(ln, plain, tn_dims), rn)
    for s in range(count):
        outs[3][s] = ln[s]
        outs[4][s] = rn[s]
        outs[1][s] = out[s]


def soap_update(arrays):
    slots = arrays[0].shape[0]
    count = 4 if slots % 4 == 0 else 1
    spec = pl.BlockSpec((count, BS, BS), lambda s: (s, 0, 0))
    return pl.pallas_call(
        partial(soap_kernel, count),
        grid=(slots // count,),
        out_shape=[f32(slots, BS, BS)] * 8,
        in_specs=[spec] * 9,
        out_specs=[spec] * 8,
        compiler_params=pltpu.CompilerParams(vmem_limit_bytes=40 * 2**20),
    )(*arrays)


def adamw(weight, first, second, grad):
    first_new = 0.9 * first + 0.1 * grad
    second_new = 0.99 * second + 0.01 * grad * grad
    normal = (
        first_new
        / (1.0 - 0.9**ADAM_STEP)
        / (jnp.sqrt(second_new / (1.0 - 0.99**ADAM_STEP)) + 1e-08)
    )
    return (weight - 0.01 * (normal + 0.01 * weight), first_new, second_new)


def to_matrices(blocks):
    return (
        blocks.reshape(2 * LAYERS, SIDE, SIDE, BS, BS).transpose(0, 1, 3, 2, 4).reshape(2 * LAYERS, D, D)
    )


def to_blocks(matrices):
    return (
        matrices.reshape(2 * LAYERS, SIDE, BS, SIDE, BS)
        .transpose(0, 1, 3, 2, 4)
        .reshape(2 * LAYERS * SIDE * SIDE, BS, BS)
    )


def tables(block_owner, slots, sizes):
    ids = jnp.arange(block_owner.shape[0], dtype=jnp.int32)
    inverse = jnp.sum(jnp.where(block_owner[None] == ids[:, None], ids[None], 0), axis=1)
    if not is_cube(sizes):
        return jnp.zeros_like(inverse), inverse, inverse
    y, x, z, core = place()
    device, slot = inverse // slots, inverse % slots
    rank = jnp.sum(
        jnp.where(
            jnp.asarray(Z_ORDER)[z][:, None] == (device // 2 % 4)[None],
            jnp.arange(4, dtype=jnp.int32)[:, None],
            0,
        ),
        axis=0,
    )
    which = ((device % 2) ^ core) * 4 + rank
    where = (((device // 8 % 2) ^ x) * 2 + ((device // 16) ^ y)) * slots + slot
    return which, where, inverse


def sum_pieces(pieces, sizes, slots):
    if not is_cube(sizes):
        total = lax.psum_scatter(pieces[0], AX, scatter_dimension=0, tiled=True)
        return total, total
    chunks = [pieces[p] + hop(pieces[4 + p], HOP_CORE) for p in range(4)]
    return reduce_chips([c.reshape(2, 2, slots, BS, BS) for c in chunks])


def block_diagonal(mixing, depth):
    channels = mixing.shape[-1]
    rows = []
    for k in range(9):
        block = mixing[0 if k == 0 else 1 if k < 4 else 2]
        rows.append(jnp.pad(block, ((0, 0), (k * channels, depth - (k + 1) * channels))))
    return jnp.concatenate(rows, axis=0)


def fast_chain(weights, every, inverse, targets, which, where, scale, add_up, label, ends, vec, live, src, ss, st):
    pair_in, pair_out, env_weight, scalar_weight, mix_weight, energy_head = weights
    channels, edges = env_weight.shape[1], vec.shape[1]
    rows9 = 9 * channels
    depth = -(-rows9 // 128) * 128
    head = energy_head[:D]
    factor = jnp.sum(energy_head[D:, None] * ss, axis=0)
    inv, unit, env, denv, bessel, dbessel = geometry(vec, live)
    pad_rows = lambda v, n: jnp.pad(v, ((0, n - v.shape[0]), (0, 0)))
    shape = pad_rows(harmonics(unit), 16)
    feat = jnp.concatenate([bessel, ss, st], axis=0)
    rows = pad_rows(jnp.stack([env, factor]), 8)
    geo = pad_rows(jnp.concatenate([unit, inv[None], denv[None]], axis=0), 8)
    dbessel_rows = pad_rows(dbessel, 2 * NB)
    same = (src[:, None] == src[None]).astype(jnp.bfloat16)
    cut = split_outside
    in_t, in_w, out_t, out_w = cut(pair_in.T), cut(pair_in), cut(pair_out.T), cut(pair_out)
    env_w, env_t = cut(env_weight), cut(env_weight.transpose(0, 2, 1))
    sc_w, sc_t = cut(scalar_weight), cut(scalar_weight.transpose(0, 2, 1))
    layer = lambda parts, l: tuple(v[l] for v in parts)
    mix_w = cut(block_diagonal(mix_weight, depth))
    mix_t = cut(block_diagonal(mix_weight.transpose(0, 2, 1), depth))
    wide, plane, narrow = (D, edges), (rows9, edges), (channels, edges)
    unit_flops = 6 * D * D * edges
    temps = dict(**stream_scratch(), **plane_scratch(rows9, edges))
    args = (channels, edges, scale)

    one = kernel_call(
        lambda r: first_layer(r, *args),
        dict(shape=shape, rows=rows, same=same, feat=feat, in_t=in_t, env0w=layer(env_w, 0)),
        dict(w0=f32(*narrow)),
        temps,
        sent=dict(
            pre0=f32(*wide),
            out0=f32(*wide),
            hid=pair_of(*wide),
            lat0=pair_of(*wide),
            env0=f32(*plane),
            res0=f32(*plane),
        ),
        hbm=dict(out_t=out_t),
        flops=unit_flops,
    )
    loaded = kernel_call(
        load_blocks,
        dict(head=head[None]),
        dict(last=f32(D, D), top=f32(D, 1)),
        dict(
            blocks=pltpu.VMEM((3, SIDE, BS, BS), jnp.float32),
            flat=pltpu.VMEM((2, 2, BS, D), jnp.bfloat16),
            turned=pltpu.VMEM((2, 2, D, BS), jnp.bfloat16),
            sem=pltpu.SemaphoreType.DMA((3, SIDE)),
            out_sem=pltpu.SemaphoreType.DMA((2, 4)),
            last_sem=pltpu.SemaphoreType.DMA((SIDE, SIDE)),
        ),
        hbm=dict(piece=every),
        hbm_out=dict(m=pair_of(3, D, D), mt=pair_of(3, D, D)),
        smem=dict(where=inverse),
    )
    head_col = head[:, None]
    up = kernel_call(
        lambda r: energy_up(r, *args),
        dict(
            shape=shape,
            rows=rows,
            same=same,
            head=head_col,
            top=loaded.top,
            lat0=one.lat0,
            res0=one.res0,
            sc0_t=layer(sc_t, 0),
            sc1_t=layer(sc_t, 1),
            env1w=layer(env_w, 1),
        ),
        dict(w1=f32(*narrow), res1=f32(*narrow), per=f32(8, edges)),
        temps,
        late=dict(out0=one.out0, mix=mix_w),
        sent=dict(
            pre1=f32(*wide),
            out1=f32(*wide),
            pre2=f32(*wide),
            act1=pair_of(*wide),
            lat1=pair_of(*wide),
            pre2_bar=pair_of(*wide),
            env1=f32(*plane),
            feat1=f32(*plane),
        ),
        hbm=dict(mt=loaded.mt),
        flops=3 * unit_flops,
    )
    down = kernel_call(
        lambda r: energy_down(r, *args),
        dict(
            shape=shape,
            rows=rows,
            same=same,
            head=head_col,
            geo=geo,
            dbessel=dbessel_rows,
            ends=ends,
            w0=one.w0,
            w1=up.w1,
            per=up.per,
            pre2_bar=up.pre2_bar,
            sc0=layer(sc_w, 0),
            sc1=layer(sc_w, 1),
            env0w_t=layer(env_t, 0),
            env1w_t=layer(env_t, 1),
            in_w=in_w,
        ),
        dict(
            res1_bar=f32(*narrow),
            w1_bar=f32(*narrow),
            w0_bar=f32(*narrow),
            shape_bar=f32(16, edges),
            force_part=f32(8, ends.shape[1]),
            bessel_bar=f32(16, edges),
        ),
        dict(**temps, vec_bar=pltpu.VMEM((8, edges), jnp.float32)),
        late=dict(
            pre0=one.pre0,
            out0=one.out0,
            env0=one.env0,
            pre1=up.pre1,
            out1=up.out1,
            env1=up.env1,
            feat1=up.feat1,
            mix_t=mix_t,
        ),
        sent=dict(
            lat1_bar=f32(*wide),
            act1_bar=f32(*wide),
            lat0_bar=f32(*wide),
            hid_bar=f32(*wide),
            out1_bar=pair_of(*wide),
            pre1_bar=pair_of(*wide),
            out0_bar=pair_of(*wide),
            pre0_bar=pair_of(*wide),
            feat1_bar=f32(*plane),
            emb1_bar=f32(*plane),
            res0_bar=f32(*plane),
            emb0_bar=f32(*plane),
        ),
        hbm=dict(m=loaded.m, out=out_w),
        flops=4 * unit_flops,
    )
    force = add_up(down.force_part)
    tan = kernel_call(
        lambda r: tangent_up(r, *args),
        dict(
            shape=shape,
            rows=rows,
            same=same,
            geo=geo,
            dbessel=dbessel_rows,
            ends=ends,
            force=force,
            label=label,
            head=head_col,
            top=loaded.top,
            w0=one.w0,
            w1=up.w1,
            in_t=in_t,
            sc0_t=layer(sc_t, 0),
            sc1_t=layer(sc_t, 1),
            env0w=layer(env_w, 0),
            env1w=layer(env_w, 1),
        ),
        dict(
            w0_dot=f32(*narrow),
            w1_dot=f32(*narrow),
            res1_dot=f32(*narrow),
            head_part=f32(D, 128),
            last_part=f32(D, 128),
            per_dot=f32(8, edges),
            env_row=f32(8, edges),
            shape_dot=f32(16, edges),
            bessel_dot=f32(2 * NB, edges),
            loss_part=f32(1, ends.shape[1]),
        ),
        dict(
            **temps,
            cot=pltpu.VMEM((8, ends.shape[1]), jnp.float32),
            tmp=pltpu.VMEM(wide, jnp.float32),
            keep=pltpu.VMEM(wide, jnp.float32),
        ),
        late=dict(
            pre0=one.pre0,
            out0=one.out0,
            env0=one.env0,
            pre1=up.pre1,
            out1=up.out1,
            pre2=up.pre2,
            env1=up.env1,
            feat1=up.feat1,
            lat1=up.lat1,
            mix=mix_w,
        ),
        sent=dict(
            pre0_dot=f32(*wide),
            pre1_dot=f32(*wide),
            hid_dot=pair_of(*wide),
            lat0_dot=pair_of(*wide),
            act1_dot=pair_of(*wide),
            lat1_dot=pair_of(*wide),
            pre2_hat=pair_of(*wide),
            env0_dot=f32(*plane),
            res0_dot=f32(*plane),
            env1_dot=f32(*plane),
            feat1_dot=f32(*plane),
        ),
        hbm=dict(out_t=out_t, mt=loaded.mt),
        flops=4 * unit_flops,
    )
    hat = kernel_call(
        lambda r: tangent_down(r, *args),
        dict(
            shape=shape,
            rows=rows,
            same=same,
            shape_dot=tan.shape_dot,
            env_row=tan.env_row,
            head=head_col,
            pre2_hat=tan.pre2_hat,
            w0=one.w0,
            w0_dot=tan.w0_dot,
            res1_bar=down.res1_bar,
            sc0=layer(sc_w, 0),
            sc1=layer(sc_w, 1),
            env0w_t=layer(env_t, 0),
            env1w_t=layer(env_t, 1),
        ),
        dict(w1_hat=f32(*narrow), w0_hat=f32(*narrow)),
        dict(
            **temps,
            hat1=pltpu.VMEM(wide, jnp.float32),
            tmp=pltpu.VMEM(wide, jnp.float32),
            small=pltpu.VMEM(narrow, jnp.float32),
            plane=pltpu.VMEM(plane, jnp.float32),
            res0_hat=pltpu.VMEM(plane, jnp.float32),
        ),
        late=dict(
            pre0=one.pre0,
            env0=one.env0,
            pre1=up.pre1,
            env1=up.env1,
            feat1=up.feat1,
            lat1_bar=down.lat1_bar,
            act1_bar=down.act1_bar,
            lat0_bar=down.lat0_bar,
            hid_bar=down.hid_bar,
            emb1_bar=down.emb1_bar,
            emb0_bar=down.emb0_bar,
            res0_bar=down.res0_bar,
            pre0_dot=tan.pre0_dot,
            pre1_dot=tan.pre1_dot,
            env1_dot=tan.env1_dot,
            feat1_dot=tan.feat1_dot,
            env0_dot=tan.env0_dot,
            mix_t=mix_t,
        ),
        sent=dict(
            out1_hat=pair_of(*wide),
            pre1_hat=pair_of(*wide),
            out0_hat=pair_of(*wide),
            pre0_hat=pair_of(*wide),
            feat1_hat=f32(*plane),
        ),
        hbm=dict(m=loaded.m, out=out_w),
        flops=4 * unit_flops,
    )
    env_dot = tan.env_row[0]
    loss = jnp.sum(tan.loss_part)
    lead_sum = jnp.sum(tan.last_part, axis=1)
    head_grad = RES * jnp.sum(tan.head_part, axis=1) + jnp.sum(
        lead_sum[:, None] * loaded.last, axis=0
    )
    per1, per2 = up.per[0], up.per[1]
    energy_dot = env_dot * RES * (per1 + env * per2) + env * RES * (
        tan.per_dot[0] + env_dot * per2 + env * tan.per_dot[1]
    )
    head_grad = jnp.concatenate([head_grad, jnp.sum(ss * energy_dot[None], axis=1)])
    made = kernel_call(
        lambda r: block_gradients(r, channels, edges, targets),
        dict(
            lead=lead_sum[:, None],
            head=head[None],
        ),
        {},
        dict(
            held=pltpu.VMEM((2, 4, 2, D, edges), jnp.bfloat16),
            arrived=pltpu.SemaphoreType.DMA((2, 4, 2)),
            stage=pltpu.VMEM((2, HALF, D), jnp.float32),
            sent_sem=pltpu.SemaphoreType.DMA((2,)),
        ),
        hbm=dict(
            lat0_dot=tan.lat0_dot,
            act1_dot=tan.act1_dot,
            lat1_dot=tan.lat1_dot,
            pre2_hat=tan.pre2_hat,
            lat0=one.lat0,
            act1=up.act1,
            lat1=up.lat1,
            pre2_bar=up.pre2_bar,
            pre1_bar=down.pre1_bar,
            out1_bar=down.out1_bar,
            pre1_hat=hat.pre1_hat,
            out1_hat=hat.out1_hat,
        ),
        hbm_out=dict(out=[f32(every.shape[0] // targets, BS, BS) for _ in range(targets)]),
        smem=dict(which=which, where=where),
        flops=6 * unit_flops,
    )

    feat = lax.optimization_barrier((feat, made.out[0]))[0]
    small = kernel_call(
        lambda r: small_gradients(r, channels, edges),
        dict(
            feat=feat,
            bessel_dot=tan.bessel_dot,
            hid_dot=tan.hid_dot,
            out0_bar=down.out0_bar,
            w0_bar=down.w0_bar,
            w1_bar=down.w1_bar,
            w0_hat=hat.w0_hat,
            w1_hat=hat.w1_hat,
            res1=up.res1,
            res1_dot=tan.res1_dot,
        ),
        dict(
            in_grad=f32(2 * NB, D),
            mix_grad=f32(3, channels, channels),
            env_grad=f32(2, channels, D),
            sc_grad=f32(2, channels, D),
        ),
        {},
        late=dict(
            hid=one.hid,
            out0_hat=hat.out0_hat,
            pre0_bar=down.pre0_bar,
            pre0_hat=hat.pre0_hat,
            feat1_bar=down.feat1_bar,
            res0_dot=tan.res0_dot,
            feat1_hat=hat.feat1_hat,
            res0=one.res0,
            lat0_dot=tan.lat0_dot,
            lat0=one.lat0,
            pre1_bar=down.pre1_bar,
            pre1_hat=hat.pre1_hat,
            lat1_dot=tan.lat1_dot,
            lat1=up.lat1,
            pre2_bar=up.pre2_bar,
            pre2_hat=tan.pre2_hat,
        ),
        sent=dict(out_grad=f32(D, D)),
        flops=2 * unit_flops,
    )

    return small, head_grad, loss, made


def local(
    sizes,
    edge_vec,
    edge_live,
    source,
    target,
    species,
    force_label,
    force_mask,
    block_owner,
    pair_in_weight,
    pair_in_first,
    pair_in_second,
    pair_out_weight,
    pair_out_first,
    pair_out_second,
    env_weight,
    env_first,
    env_second,
    scalar_weight,
    scalar_first,
    scalar_second,
    mix_weight,
    mix_first,
    mix_second,
    energy_head,
    head_first,
    head_second,
    soap_weight,
    soap_first,
    soap_second,
    soap_left,
    soap_right,
    soap_lstat,
    soap_rstat,
    soap_average,
):
    devices = sizes[0] * sizes[1]
    edges = edge_vec.shape[1]
    per_atoms = force_label.shape[1]
    atoms = per_atoms * devices
    me = lax.axis_index("irrep") * sizes[1] + lax.axis_index("edge")
    scale = math.sqrt(per_atoms / edges)
    as_float = lambda v: v.astype(jnp.float32)

    labels = jnp.concatenate([force_label, as_float(force_mask)[None]], axis=0).reshape(-1)
    packed = jnp.concatenate(
        [
            edge_vec,
            as_float(source)[None],
            as_float(target)[None],
            as_float(edge_live)[None],
            jnp.pad(labels, (0, edges - labels.shape[0]))[None],
        ],
        axis=0,
    )
    every = gather_small(packed, sizes)
    label_all = every[:, 6, : 4 * per_atoms].reshape(devices, 4, per_atoms)
    label_all = label_all.transpose(1, 0, 2).reshape(4, atoms)
    label_mask = label_all[3]
    label_total = jnp.sum(label_mask)
    payload = every[:, :5].transpose(0, 2, 1).reshape(devices * edges, 5)
    all_source = every[:, 3].reshape(-1).astype(jnp.int32)
    all_live = every[:, 5].reshape(-1)

    low = (all_source[:, None] % 32 == jnp.arange(32)[None]).astype(jnp.bfloat16)
    high = (all_source[None] // 32 == jnp.arange(-(-atoms // 32))[:, None]) & (all_live[None] > 0)
    counts = jnp.dot(
        high.astype(jnp.bfloat16), low, preferred_element_type=jnp.float32
    ).reshape(-1)[:atoms]
    atom_ids = jnp.arange(atoms)
    before = jnp.dot(
        (atom_ids[:, None] > atom_ids[None]).astype(jnp.float32), counts, precision=FULL
    )
    middle = (2.0 * before + counts).astype(jnp.int32)
    total = jnp.sum(counts).astype(jnp.int32)
    owner = jnp.minimum((middle * devices) // (2 * total), devices - 1)
    loads = jnp.sum(
        jnp.where(owner[None] == jnp.arange(devices)[:, None], counts[None], 0.0), axis=1
    )
    fits = jnp.max(loads) <= edges
    first_atom = jnp.sum(owner < me)
    last_atom = jnp.sum(owner <= me)
    mine = (all_live > 0) & (all_source >= first_atom) & (all_source < last_atom)
    flags = as_float(mine).reshape(-1, 128)
    tri = jnp.arange(128)
    inside = jnp.dot(flags, as_float(tri[:, None] <= tri[None]))
    row_ids = jnp.arange(flags.shape[0])
    row_sum = jnp.sum(flags, axis=1)
    offset = jnp.sum(
        jnp.where(row_ids[None] < row_ids[:, None], row_sum[None], 0.0), axis=1
    )
    rank = (inside + offset[:, None]).reshape(-1)
    slot_ids = jnp.arange(edges).astype(jnp.float32)
    index = jnp.sum((rank[None] <= slot_ids[:, None]).astype(jnp.float32), axis=1).astype(jnp.int32)
    valid = slot_ids < rank[-1]
    chosen = payload[jnp.minimum(index, devices * edges - 1)].T
    safe = jnp.asarray([1.5, 0.0, 0.0], jnp.float32)[:, None]
    my_vec = jnp.where(valid[None], chosen[:3], safe)
    my_source = jnp.where(valid, chosen[3], -1.0).astype(jnp.int32)
    my_target = jnp.where(valid, chosen[4], -1.0).astype(jnp.int32)
    my_live = as_float(valid)

    weights = (pair_in_weight, pair_out_weight, env_weight, scalar_weight, mix_weight[0], energy_head)
    slots = soap_weight.shape[0]
    kinds = jnp.arange(SPECIES, dtype=jnp.int32)[:, None]
    every_block = lax.all_gather(soap_weight, AX, axis=0, tiled=True)
    targets = 8 if is_cube(sizes) else 1
    which, where, inverse = tables(block_owner, slots, sizes)

    def views(src, tgt):
        from_atom = (src[:, None] == atom_ids[None]).astype(jnp.float32)
        to_atom = (tgt[:, None] == atom_ids[None]).astype(jnp.float32)
        spec = (species[None] == kinds).astype(jnp.float32)
        species_source = dot(spec, from_atom, ((1,), (1,)), None)
        species_target = dot(spec, to_atom, ((1,), (1,)), None)
        ends = from_atom - to_atom

        def force_to_tangent(vec_bar):
            force = sum_small(dot(vec_bar, ends, ((1,), (0,)), FULL), sizes)
            residual = force - label_all[:3]
            loss = jnp.sum(label_mask[None] * residual * residual)
            cot = 2.0 * label_mask[None] * residual / label_total
            return dot(cot, ends, ((1,), (1,)), FULL), loss

        return from_atom, species_source, species_target, force_to_tangent

    def general():
        from_atom, ss, st, force_to_tangent = views(source, target)
        blocks = every_block[inverse]

        def environ(tensor):
            sums = lax.psum(nn(tensor.reshape(-1, edges), from_atom), AX)
            return scale * nt(sums, from_atom).reshape(tensor.shape)

        matrices = to_matrices(blocks)
        out = chain(
            weights,
            lambda after: matrices,
            environ,
            force_to_tangent,
            edge_vec,
            as_float(edge_live),
            ss,
            st,
        )
        flat = to_blocks(jnp.stack(out[6]))
        per = inverse.shape[0] // targets
        place_of = which * per + where
        order = jnp.zeros_like(place_of).at[place_of].set(jnp.arange(place_of.shape[0]))
        laid = flat[order].reshape(targets, per, BS, BS)
        return out[:6] + (tuple(laid[n] for n in range(targets)), out[7])

    def pack_first(in_grad, out_grad, mix_grad, head_grad):
        rest = jnp.concatenate([mix_grad.reshape(-1), head_grad])
        rest = jnp.pad(rest, (0, -rest.shape[0] % (8 * D))).reshape(-1, D)
        return jnp.concatenate([in_grad, rest], axis=0), out_grad

    flat_rows = lambda env_grad, sc_grad: (env_grad.reshape(-1, D), sc_grad.reshape(-1, D))
    def replace(state):
        out = general()
        parts = pack_first(out[0], out[1], out[4], out[5]) + flat_rows(out[2], out[3])
        own, _ = sum_pieces(out[6], sizes, slots)
        return (jnp.asarray(False), own, lax.psum(parts, AX), out[7])

    rest_rows = 8 * (-(-(mix_weight.size + energy_head.shape[0]) // (8 * D))) + 2 * NB
    zeros = lambda n: jnp.zeros((n, D), jnp.float32)
    wide_rows = env_weight.shape[0] * env_weight.shape[1]
    _, general_own, general_shared, general_loss = lax.while_loop(
        lambda state: state[0],
        replace,
        (
            jnp.logical_not(fits),
            jnp.zeros_like(soap_weight),
            (zeros(rest_rows), zeros(D), zeros(wide_rows), zeros(wide_rows)),
            jnp.zeros((), jnp.float32),
        ),
    )
    every_block, general_loss = lax.optimization_barrier((every_block, general_loss))
    _, my_ss, my_st, _ = views(my_source, my_target)
    my_ends = (my_source[:, None] == atom_ids[None]).astype(jnp.bfloat16)
    my_ends = my_ends - (my_target[:, None] == atom_ids[None]).astype(jnp.bfloat16)
    labels_all = jnp.concatenate([label_all, 2.0 * label_mask[None] / label_total], axis=0)
    labels_all = jnp.pad(labels_all, ((0, 8 - labels_all.shape[0]), (0, 0)))
    add_up = lambda part: sum_small(part, sizes)
    fast = fast_chain(
        weights, every_block, inverse, targets, which, where, scale, add_up, labels_all, my_ends, my_vec, my_live, my_source, my_ss, my_st
    )

    small, head_part, fast_loss, made = fast
    local_sums = pack_first(small.in_grad, small.out_grad, small.mix_grad, head_part)
    local_sums = local_sums + flat_rows(small.env_grad, small.sc_grad)
    summed = lax.psum(local_sums, AX)
    loss_sum = jnp.where(fits, fast_loss, general_loss)

    own_grads, nearly = sum_pieces(tuple(made.out), sizes, slots)
    own_grads = jnp.where(fits, own_grads, general_own)
    soap = soap_update(
        (
            own_grads,
            soap_weight,
            soap_first,
            soap_second,
            soap_left,
            soap_right,
            soap_lstat,
            soap_rstat,
            soap_average,
        )
    )
    (summed, general_shared), soap = lax.optimization_barrier(((summed, general_shared), tuple(soap)))
    misc, pair_out_grad, env_grad, scalar_grad = jax.tree.map(
        lambda a, b: jnp.where(fits, a, b), summed, general_shared
    )
    pair_in_grad = misc[: 2 * NB]
    rest = misc[2 * NB :].reshape(-1)
    mix_grad = rest[: mix_weight.size].reshape(mix_weight.shape[1:])
    head_grad = rest[mix_weight.size : mix_weight.size + energy_head.shape[0]]
    env_grad = env_grad.reshape(env_weight.shape)
    scalar_grad = scalar_grad.reshape(scalar_weight.shape)
    new_pair_in = adamw(pair_in_weight, pair_in_first, pair_in_second, pair_in_grad)
    new_pair_out = adamw(pair_out_weight, pair_out_first, pair_out_second, pair_out_grad)
    new_env = adamw(env_weight, env_first, env_second, env_grad)
    new_scalar = adamw(scalar_weight, scalar_first, scalar_second, scalar_grad)
    new_mix = adamw(mix_weight, mix_first, mix_second, mix_grad[None])
    new_head = adamw(energy_head, head_first, head_second, head_grad)
    return (
        (loss_sum, label_total)
        + new_pair_in
        + new_pair_out
        + new_env
        + new_scalar
        + new_mix
        + new_head
        + tuple(soap)
    )


def solution(mesh):
    shared, split = P(), P(AX)
    column = P(None, AX)
    blocks = P(AX, None, None)
    placed = (
        (column, split, split, split, shared, column, split, shared) + (shared,) * 18 + (blocks,) * 8
    )
    return jax.shard_map(
        partial(local, (mesh.shape["irrep"], mesh.shape["edge"])),
        mesh=mesh,
        in_specs=placed,
        out_specs=(shared,) * 20 + (blocks,) * 8,
        check_vma=False,
    )
```

```python
from functools import partial
import math
from types import SimpleNamespace

import jax
import jax.numpy as jnp
import numpy as np
from jax import lax
from jax.experimental import pallas as pl
from jax.experimental.pallas import tpu as pltpu
from jax.sharding import PartitionSpec as P

D = 1024
NB = 8
SPECIES = 4
LAYERS = 2
BS = 128
NS_STEPS = 4
ADAM_STEP = 10
SIDE = D // BS
AX = ("irrep", "edge")

HIGH = lax.Precision.HIGH
FULL = lax.Precision.HIGHEST
CUTOFF = 5.0
ROOT_TWO = math.sqrt(2.0)
ROOT_THREE = math.sqrt(3.0)
ROOT_SIX = math.sqrt(6.0)
HARMONIC = math.sqrt(7.5)
RES = 1.0 / math.sqrt(2.0)


def shape_basis():
    return [
        np.array([[0.0, 1, 0], [1, 0, 0], [0, 0, 0]]) / ROOT_TWO,
        np.array([[0.0, 0, 0], [0, 0, 1], [0, 1, 0]]) / ROOT_TWO,
        np.array([[0.0, 0, 1], [0, 0, 0], [1, 0, 0]]) / ROOT_TWO,
        np.array([[1.0, 0, 0], [0, -1, 0], [0, 0, 0]]) / ROOT_TWO,
        np.array([[-1.0, 0, 0], [0, -1, 0], [0, 0, 2]]) / ROOT_SIX,
    ]


def cross_three(left_vec, right_vec):
    return np.array(
        [
            left_vec[1] * right_vec[2] - left_vec[2] * right_vec[1],
            left_vec[2] * right_vec[0] - left_vec[0] * right_vec[2],
            left_vec[0] * right_vec[1] - left_vec[1] * right_vec[0],
        ]
    )


def product_table():
    tensors = shape_basis()
    table = np.zeros((9, 9, 9))
    unit_rows = np.eye(9)
    for first in range(9):
        for second in range(9):
            left = unit_rows[first]
            right = unit_rows[second]
            left_mat = sum((left[4 + slot] * tensors[slot] for slot in range(5)))
            right_mat = sum((right[4 + slot] * tensors[slot] for slot in range(5)))
            left_vec = left[1:4]
            right_vec = right[1:4]
            scalar = left[0] * right[0] + left_vec @ right_vec + np.sum(left_mat * right_mat.T)
            vector = (
                left[0] * right_vec
                + right[0] * left_vec
                + cross_three(left_vec, right_vec)
                + left_mat @ right_vec
                + right_mat @ left_vec
            )
            matrix = (
                left[0] * right_mat
                + right[0] * left_mat
                + (np.outer(left_vec, right_vec) + np.outer(right_vec, left_vec)) / 2
                + (left_mat @ right_mat + right_mat @ left_mat) / 2
            )
            table[first, second, 0] = scalar
            table[first, second, 1:4] = vector
            for slot in range(5):
                table[first, second, 4 + slot] = np.sum(tensors[slot] * matrix)
    return (table / 3.0).astype(np.float32)


TABLE = product_table()
TERMS = [
    (a, b, k, float(TABLE[a, b, k]))
    for a in range(9)
    for b in range(9)
    for k in range(9)
    if abs(TABLE[a, b, k]) > 1e-7
]


def dot(left, right, dims, precision=HIGH):
    return lax.dot_general(left, right, ((dims[0], dims[1]), ((), ())), precision=precision)


def nn(left, right):
    return dot(left, right, ((1,), (0,)))


def tn(left, right):
    return dot(left, right, ((0,), (0,)))


def nt(left, right):
    return dot(left, right, ((1,), (1,)))


def device_of(y, x, z, core):
    return (y * 2 + x) * 8 + z * 2 + core


CUBE = [(y, x, z, c) for y in range(2) for x in range(2) for z in range(4) for c in range(2)]
HOP_X = [(device_of(y, x, z, c), device_of(y, 1 - x, z, c)) for y, x, z, c in CUBE]
HOP_Y = [(device_of(y, x, z, c), device_of(1 - y, x, z, c)) for y, x, z, c in CUBE]
HOP_XY = [(device_of(y, x, z, c), device_of(1 - y, 1 - x, z, c)) for y, x, z, c in CUBE]
HOP_CORE = [(device_of(y, x, z, c), device_of(y, x, z, 1 - c)) for y, x, z, c in CUBE]


def along_z(pairs):
    return [
        (device_of(y, x, s, c), device_of(y, x, t, c))
        for s, t in pairs
        for y in range(2)
        for x in range(2)
        for c in range(2)
    ]


HOP_IN = along_z([(0, 1), (3, 2)])
HOP_MID = along_z([(1, 2), (2, 1)])
HOP_OUT = along_z([(1, 0), (2, 3)])
HOP_Z = [along_z([(s, s ^ k) for s in range(4)]) for k in range(1, 4)]


def hop(value, pairs):
    return lax.ppermute(value, AX, pairs)


def place():
    irrep = lax.axis_index("irrep")
    edge = lax.axis_index("edge")
    return irrep // 2, irrep % 2, edge // 2, edge % 2


Z_ORDER = np.array([[3, 2, 1, 0], [3, 2, 0, 1], [0, 1, 3, 2], [0, 1, 2, 3]], np.int32)


def relative_devices():
    y, x, z, core = place()
    zs = jnp.asarray(Z_ORDER)[z]
    two = jnp.arange(2, dtype=jnp.int32)
    irrep = (two[None, :] ^ y) * 2 + (two[:, None] ^ x)
    return (
        irrep[None, :, :, None] * 8 + zs[:, None, None, None] * 2 + (two ^ core)[None, None, None, :]
    )


def reduce_chips(chunks):
    first, planes_done = [], []

    def second(p):
        (a0, a1), (b0, b1) = first[p]
        planes_done.append(
            jnp.concatenate([a0 + hop(a1, HOP_Y), b0 + hop(b1, HOP_X)], axis=0)
        )

    for p in range(4):
        block = chunks[p]
        if p >= 2:
            block, first[p - 2] = lax.optimization_barrier((block, first[p - 2]))
            second(p - 2)
        half = block.shape[2] // 2
        upper, lower = block[:, :, :half], block[:, :, half:]
        a = upper[0] + hop(upper[1], HOP_X)
        b = lower[:, 0] + hop(lower[:, 1], HOP_Y)
        first.append(((a[0], a[1]), (b[0], b[1])))
    second(2)
    second(3)
    q0, q1, q2, q3 = planes_done
    p0 = q0 + hop(q0, HOP_IN)
    p1 = q1 + hop(q1, HOP_IN)
    p2 = q2 + hop(p0, HOP_MID)
    return q3 + hop(q2, HOP_IN) + hop(p1, HOP_MID) + hop(p2, HOP_OUT), p2


def is_cube(sizes):
    return sizes == (4, 8)


def gather_small(value, sizes):
    if not is_cube(sizes):
        return lax.all_gather(value, AX, axis=0, tiled=False)
    y, x, z, core = place()
    plane = jnp.stack([value, hop(value, HOP_X), hop(value, HOP_Y), hop(value, HOP_XY)])
    column = jnp.stack([plane] + [hop(plane, pairs) for pairs in HOP_Z])
    every = jnp.stack([column, hop(column, HOP_CORE)])
    flat = every.reshape((32,) + value.shape)
    ids = np.arange(32, dtype=np.int32)
    core_of, z_of, x_of, y_of = ids % 2, ids // 2 % 4, ids // 8 % 2, ids // 16
    index = (core_of ^ core) * 16 + (z_of ^ z) * 4 + (y_of ^ y) * 2 + (x_of ^ x)
    return flat[index]


def sum_small(value, sizes):
    if not is_cube(sizes):
        return lax.psum(value, AX)
    total = value + hop(value, HOP_CORE)
    plane = total + hop(total, HOP_X) + (hop(total, HOP_Y) + hop(total, HOP_XY))
    one, two, three = [hop(plane, pairs) for pairs in HOP_Z]
    return (plane + one) + (two + three)


def geometry(vec, live):
    dist = jnp.sqrt(jnp.sum(vec * vec, axis=0))
    inv = 1.0 / dist
    unit = vec * inv[None]
    ratio = dist / CUTOFF
    r5 = ratio**5
    env = (1.0 - r5 * ratio * (28.0 - 48.0 * ratio + 21.0 * ratio * ratio)) * live
    denv = -(168.0 / CUTOFF) * r5 * (1.0 - ratio) * (1.0 - ratio) * live
    order = jnp.arange(1, NB + 1).astype(jnp.float32)[:, None] * (math.pi / CUTOFF)
    angle = order * dist[None]
    norm = math.sqrt(2.0 / CUTOFF)
    bessel = norm * jnp.sin(angle) * inv[None]
    dbessel = norm * order * jnp.cos(angle) * inv[None] - bessel * inv[None]
    return inv, unit, env, denv, bessel, dbessel


def harmonics(unit):
    x, y, z = unit
    h = HARMONIC
    return jnp.stack(
        [
            jnp.ones_like(x),
            ROOT_THREE * x,
            ROOT_THREE * y,
            ROOT_THREE * z,
            h * ROOT_TWO * x * y,
            h * ROOT_TWO * y * z,
            h * ROOT_TWO * x * z,
            h * (x * x - y * y) / ROOT_TWO,
            h * (2.0 * z * z - x * x - y * y) / ROOT_SIX,
        ]
    )


def harmonics_dot_rows(unit, dunit):
    x, y, z = unit
    dx, dy, dz = dunit
    h = HARMONIC
    return (
        [
            jnp.zeros_like(x),
            ROOT_THREE * dx,
            ROOT_THREE * dy,
            ROOT_THREE * dz,
            h * ROOT_TWO * (dx * y + x * dy),
            h * ROOT_TWO * (dy * z + y * dz),
            h * ROOT_TWO * (dx * z + x * dz),
            h * ROOT_TWO * (x * dx - y * dy),
            (2.0 * h / ROOT_SIX) * (2.0 * z * dz - x * dx - y * dy),
        ]
    )


def harmonics_back_rows(unit, bar):
    x, y, z = unit
    a, b = HARMONIC * ROOT_TWO, 2.0 * HARMONIC / ROOT_SIX
    return (
        [
            ROOT_THREE * bar[1] + a * (y * bar[4] + z * bar[6] + x * bar[7]) - b * x * bar[8],
            ROOT_THREE * bar[2] + a * (x * bar[4] + z * bar[5] - y * bar[7]) - b * y * bar[8],
            ROOT_THREE * bar[3] + a * (y * bar[5] + x * bar[6]) + 2.0 * b * z * bar[8],
        ]
    )


def harmonics_dot(unit, dunit):
    return jnp.stack(harmonics_dot_rows(unit, dunit))


def harmonics_back(unit, bar):
    return jnp.stack(harmonics_back_rows(unit, bar))


def silu(v):
    return v * jax.nn.sigmoid(v)


def silu_one(v):
    s = jax.nn.sigmoid(v)
    return s * (1.0 + v * (1.0 - s))


def silu_two(v):
    s = jax.nn.sigmoid(v)
    return s * (1.0 - s) * (2.0 + v * (1.0 - 2.0 * s))


def bilinear(sets, out, size):
    total = [None] * size
    for index in TERMS:
        a, b, k, value = index
        slot = index[out]
        for (li, left), (ri, right) in sets:
            term = left[index[li]] * right[index[ri]]
            term = value * term
            total[slot] = term if total[slot] is None else total[slot] + term
    return jnp.stack(total)


def product(feature, environ):
    return bilinear([((0, feature), (1, environ))], 2, 9)


def mix(mixing, tensor, transposed):
    op = tn if transposed else nn
    out = []
    for order, (start, stop) in enumerate(((0, 1), (1, 4), (4, 9))):
        for k in range(start, stop):
            out.append(op(mixing[order], tensor[k]))
    return jnp.stack(out)


def mix_gradient(left, right):
    out = []
    for start, stop in ((0, 1), (1, 4), (4, 9)):
        out.append(sum(nt(left[k], right[k]) for k in range(start, stop)))
    return out


def chain(weights, load_matrices, environ, force_to_tangent, vec, live, species_source, species_target):
    pair_in, pair_out, env_weight, scalar_weight, mix_weight, energy_head = weights
    head = energy_head[:D]
    factor = jnp.sum(
        energy_head[D:, None] * species_source, axis=0
    )
    inv, unit, env, denv, bessel, dbessel = geometry(vec, live)
    shape = harmonics(unit)
    feat = jnp.concatenate([bessel, species_source, species_target], axis=0)
    col = lambda v: v[:, None]
    pre0 = tn(feat, pair_in)
    hid = silu(pre0)
    out0 = nn(hid, pair_out)
    lat0 = col(env) * out0
    w0 = nt(env_weight[0], lat0)
    emb0 = shape[:, None] * w0[None]
    env0 = environ(emb0)
    res0 = product(emb0, env0)
    matrices = load_matrices(res0)
    pre1 = nn(lat0, matrices[0]) + tn(res0[0], scalar_weight[0])
    act1 = silu(pre1)
    out1 = nn(act1, matrices[1])
    lat1 = (lat0 + col(env) * out1) * RES
    w1 = nt(env_weight[1], lat1)
    emb1 = shape[:, None] * w1[None]
    env1 = environ(emb1)
    feat1 = mix(mix_weight, res0, False)
    res1 = jnp.sum(feat1 * env1, axis=0) / 3.0
    pre2 = nn(lat1, matrices[2]) + tn(res1, scalar_weight[1])
    act2 = silu(pre2)
    top = dot(matrices[3], head, ((1,), (0,)))
    slope = env * factor
    per1 = jnp.sum(lat1 * head[None], axis=1)
    per2 = jnp.sum(act2 * top[None], axis=1)
    env_bar = RES * factor * (per1 + 2.0 * env * per2)
    alpha = RES * slope
    lead = alpha * env
    slope2 = silu_one(pre2)
    pre2_bar = col(lead) * top[None] * slope2
    lat1_bar = col(alpha) * head[None] + nt(pre2_bar, matrices[2])
    res1_bar = nt(scalar_weight[1], pre2_bar)
    feat1_bar = res1_bar[None] * env1 / 3.0
    emb1_bar = environ(res1_bar[None] * feat1 / 3.0)
    shape_bar = jnp.sum(emb1_bar * w1[None], axis=1)
    w1_bar = jnp.sum(shape[:, None] * emb1_bar, axis=0)
    lat1_bar = lat1_bar + tn(w1_bar, env_weight[1])
    res0_bar = mix(mix_weight, feat1_bar, True)
    env_bar = env_bar + RES * jnp.sum(lat1_bar * out1, axis=1)
    out1_bar = RES * col(env) * lat1_bar
    act1_bar = nt(out1_bar, matrices[1])
    slope1 = silu_one(pre1)
    pre1_bar = act1_bar * slope1
    lat0_bar = RES * lat1_bar + nt(pre1_bar, matrices[0])
    res0_bar = res0_bar.at[0].add(nt(scalar_weight[0], pre1_bar))
    emb0_bar = bilinear([((2, res0_bar), (1, env0))], 0, 9) + environ(
        bilinear([((2, res0_bar), (0, emb0))], 1, 9)
    )
    shape_bar = shape_bar + jnp.sum(emb0_bar * w0[None], axis=1)
    w0_bar = jnp.sum(shape[:, None] * emb0_bar, axis=0)
    lat0_bar = lat0_bar + tn(w0_bar, env_weight[0])
    env_bar = env_bar + jnp.sum(lat0_bar * out0, axis=1)
    out0_bar = col(env) * lat0_bar
    hid_bar = nt(out0_bar, pair_out)
    slope0 = silu_one(pre0)
    pre0_bar = hid_bar * slope0
    bessel_bar = nt(pair_in[:NB], pre0_bar)
    dist_bar = env_bar * denv + jnp.sum(bessel_bar * dbessel, axis=0)
    unit_bar = harmonics_back(unit, shape_bar)
    along = jnp.sum(unit * unit_bar, axis=0)
    vec_bar = dist_bar[None] * unit + (unit_bar - unit * along[None]) * inv[None]
    vec_dot, loss_parts = force_to_tangent(vec_bar)
    dist_dot = jnp.sum(unit * vec_dot, axis=0)
    unit_dot = (vec_dot - unit * dist_dot[None]) * inv[None]
    env_dot = denv * dist_dot
    bessel_dot = dbessel * dist_dot[None]
    shape_dot = harmonics_dot(unit, unit_dot)
    pre0_dot = tn(bessel_dot, pair_in[:NB])
    hid_dot = slope0 * pre0_dot
    lat0_dot = col(env_dot) * out0 + col(env) * nn(hid_dot, pair_out)
    w0_dot = nt(env_weight[0], lat0_dot)
    emb0_dot = shape_dot[:, None] * w0[None] + shape[:, None] * w0_dot[None]
    env0_dot = environ(emb0_dot)
    res0_dot = bilinear(
        [((0, emb0_dot), (1, env0)), ((0, emb0), (1, env0_dot))], 2, 9
    )
    pre1_dot = nn(lat0_dot, matrices[0]) + tn(res0_dot[0], scalar_weight[0])
    act1_dot = slope1 * pre1_dot
    lat1_dot = (lat0_dot + col(env_dot) * out1 + col(env) * nn(act1_dot, matrices[1])) * RES
    w1_dot = nt(env_weight[1], lat1_dot)
    emb1_dot = shape_dot[:, None] * w1[None] + shape[:, None] * w1_dot[None]
    env1_dot = environ(emb1_dot)
    feat1_dot = mix(mix_weight, res0_dot, False)
    res1_dot = jnp.sum(feat1_dot * env1 + feat1 * env1_dot, axis=0) / 3.0
    pre2_dot = nn(lat1_dot, matrices[2]) + tn(res1_dot, scalar_weight[1])
    act2_dot = slope2 * pre2_dot
    lead_dot = 2.0 * RES * slope * env_dot
    last = jnp.sum(col(lead_dot) * act2 + col(lead) * act2_dot, axis=0)
    head_grad = RES * jnp.sum(
        col(factor * env_dot) * lat1 + col(slope) * lat1_dot, axis=0
    ) + jnp.sum(last[:, None] * matrices[3], axis=0)
    per1_dot = jnp.sum(lat1_dot * head[None], axis=1)
    per2_dot = jnp.sum(act2_dot * top[None], axis=1)
    energy_dot = env_dot * RES * (per1 + env * per2) + env * RES * (
        per1_dot + env_dot * per2 + env * per2_dot
    )
    scale_grad = jnp.sum(species_source * energy_dot[None], axis=1)
    head_grad = jnp.concatenate([head_grad, scale_grad])
    pre2_hat = top[None] * (col(lead_dot) * slope2 + col(lead) * silu_two(pre2) * pre2_dot)
    lat1_hat = col(RES * factor * env_dot) * head[None] + nt(pre2_hat, matrices[2])
    res1_hat = nt(scalar_weight[1], pre2_hat)
    feat1_hat = (res1_hat[None] * env1 + res1_bar[None] * env1_dot) / 3.0
    emb1_hat = environ((res1_hat[None] * feat1 + res1_bar[None] * feat1_dot) / 3.0)
    w1_hat = jnp.sum(shape_dot[:, None] * emb1_bar + shape[:, None] * emb1_hat, axis=0)
    lat1_hat = lat1_hat + tn(w1_hat, env_weight[1])
    res0_hat = mix(mix_weight, feat1_hat, True)
    out1_hat = RES * (col(env_dot) * lat1_bar + col(env) * lat1_hat)
    act1_hat = nt(out1_hat, matrices[1])
    pre1_hat = act1_hat * slope1 + act1_bar * silu_two(pre1) * pre1_dot
    lat0_hat = RES * lat1_hat + nt(pre1_hat, matrices[0])
    res0_hat = res0_hat.at[0].add(nt(scalar_weight[0], pre1_hat))
    emb0_hat = bilinear(
        [((2, res0_hat), (1, env0)), ((2, res0_bar), (1, env0_dot))], 0, 9
    ) + environ(bilinear([((2, res0_hat), (0, emb0)), ((2, res0_bar), (0, emb0_dot))], 1, 9))
    w0_hat = jnp.sum(shape_dot[:, None] * emb0_bar + shape[:, None] * emb0_hat, axis=0)
    lat0_hat = lat0_hat + tn(w0_hat, env_weight[0])
    out0_hat = col(env_dot) * lat0_bar + col(env) * lat0_hat
    pre0_hat = nt(out0_hat, pair_out) * slope0 + hid_bar * silu_two(pre0) * pre0_dot
    both = lambda first, second: jnp.concatenate([first, second], axis=0)
    pair_in_grad = nn(feat, pre0_hat)
    pair_in_grad = pair_in_grad.at[:NB].add(nn(bessel_dot, pre0_bar))
    mix_grad = jnp.stack(
        [
            first + second
            for first, second in zip(
                mix_gradient(feat1_bar, res0_dot), mix_gradient(feat1_hat, res0)
            )
        ]
    )
    env_grad = jnp.stack(
        [nn(w0_bar, lat0_dot) + nn(w0_hat, lat0), nn(w1_bar, lat1_dot) + nn(w1_hat, lat1)]
    )
    scalar_grad = jnp.stack(
        [
            nn(res0_dot[0], pre1_bar) + nn(res0[0], pre1_hat),
            nn(res1_dot, pre2_bar) + nn(res1, pre2_hat),
        ]
    )
    pair_out_grad = tn(both(hid_dot, hid), both(out0_bar, out0_hat))
    matrix_grad = [
        tn(both(lat0_dot, lat0), both(pre1_bar, pre1_hat)),
        tn(both(act1_dot, act1), both(out1_bar, out1_hat)),
        tn(both(lat1_dot, lat1), both(pre2_bar, pre2_hat)),
        last[:, None] * head[None],
    ]
    return (
        pair_in_grad,
        pair_out_grad,
        env_grad,
        scalar_grad,
        mix_grad,
        head_grad,
        matrix_grad,
        loss_parts,
    )


def split(v):
    high = v.astype(jnp.bfloat16)
    return high, (v - high.astype(jnp.float32)).astype(jnp.bfloat16)


def split_outside(v):
    high = lax.reduce_precision(v, exponent_bits=8, mantissa_bits=7)
    return high.astype(jnp.bfloat16), (v - high).astype(jnp.bfloat16)


def one_pass(left, right, dims=((1,), (0,))):
    return lax.dot_general(left, right, (dims, ((), ())), preferred_element_type=jnp.float32)


def three_pass(left, right, dims=((1,), (0,))):
    lh, ll = left
    rh, rl = right
    return one_pass(lh, rh, dims) + (one_pass(lh, rl, dims) + one_pass(ll, rh, dims))


NT = ((1,), (1,))


def exact(left, ends, dims=((1,), (0,))):
    high, low = split(left)
    rest = left - high.astype(jnp.float32) - low.astype(jnp.float32)
    return (
        one_pass(high, ends, dims)
        + one_pass(low, ends, dims)
        + one_pass(rest.astype(jnp.bfloat16), ends, dims)
    )


def kernel_call(
    body,
    ins,
    outs,
    scratch,
    late=None,
    sent=None,
    hbm=None,
    smem=None,
    hbm_out=None,
    flops=0,
    limit=60,
):
    late, sent, hbm, smem, hbm_out = late or {}, sent or {}, hbm or {}, smem or {}, hbm_out or {}
    leaves, tree = jax.tree.flatten((ins, smem, hbm, late))
    out_leaves, out_tree = jax.tree.flatten((outs, hbm_out, sent))
    buffers = jax.tree.map(lambda v: pltpu.VMEM(v.shape, v.dtype), (late, sent))
    late_count, sent_count = len(jax.tree.leaves(late)), len(jax.tree.leaves(sent))
    own = (scratch, buffers)
    own_leaves, own_tree = jax.tree.flatten(own)

    def kernel(*refs):
        n, m = len(leaves), len(leaves) + len(out_leaves)
        given = jax.tree.unflatten(tree, refs[:n])
        made = jax.tree.unflatten(out_tree, refs[n:m])
        temps, (landed, leaving) = jax.tree.unflatten(own_tree, refs[m : m + len(own_leaves)])
        sems = refs[m + len(own_leaves) :]
        r = SimpleNamespace(
            **given[0], **given[1], **given[2], **made[0], **made[1], **temps, **landed, **leaving
        )
        coming, going, started = {}, {}, []
        index = 0
        for name in sorted(late):
            sources, targets = jax.tree.leaves(given[3][name]), jax.tree.leaves(landed[name])
            coming[id(landed[name])] = []
            for source, target in zip(sources, targets):
                coming[id(landed[name])].append(
                    pltpu.make_async_copy(source, target, sems[0].at[index])
                )
                index += 1
        index = 0
        for name in sorted(sent):
            sources, targets = jax.tree.leaves(leaving[name]), jax.tree.leaves(made[2][name])
            going[id(leaving[name])] = []
            for source, target in zip(sources, targets):
                going[id(leaving[name])].append(
                    pltpu.make_async_copy(source, target, sems[1].at[index])
                )
                index += 1

        def fetch(*items):
            for item in items:
                for copy in coming[id(item)]:
                    copy.start()

        def need(*items):
            for item in items:
                for copy in coming[id(item)]:
                    copy.wait()

        def send(*items):
            for item in items:
                for copy in going[id(item)]:
                    copy.start()
                    started.append(copy)

        r.fetch, r.need, r.send = fetch, need, send
        body(r)
        for copy in started:
            copy.wait()
        assert len(started) == sent_count

    vmem, hbm_spec = pl.BlockSpec(memory_space=pltpu.VMEM), pl.BlockSpec(memory_space=pl.ANY)
    count = lambda v: len(jax.tree.leaves(v))
    in_specs = [vmem] * count(ins) + [pl.BlockSpec(memory_space=pltpu.SMEM)] * count(smem)
    in_specs += [hbm_spec] * (count(hbm) + count(late))
    out_specs = [vmem] * count(outs) + [hbm_spec] * (count(hbm_out) + count(sent))
    size = sum(v.size * v.dtype.itemsize for v in leaves + out_leaves)
    result = pl.pallas_call(
        kernel,
        out_shape=out_leaves,
        in_specs=in_specs,
        out_specs=out_specs,
        scratch_shapes=own_leaves
        + [pltpu.SemaphoreType.DMA((max(late_count, 1),)), pltpu.SemaphoreType.DMA((max(sent_count, 1),))],
        compiler_params=pltpu.CompilerParams(vmem_limit_bytes=limit * 2**20),
        cost_estimate=pl.CostEstimate(flops=flops, bytes_accessed=size, transcendentals=0),
    )(*leaves)
    made = jax.tree.unflatten(out_tree, result)
    return SimpleNamespace(**made[0], **made[1], **made[2])


def f32(*shape):
    return jax.ShapeDtypeStruct(shape, jnp.float32)


def b16(*shape):
    return jax.ShapeDtypeStruct(shape, jnp.bfloat16)


def pair_of(*shape):
    return (b16(*shape), b16(*shape))


def pair(refs, rows=None):
    high, low = refs
    return (high[...], low[...]) if rows is None else (high[rows, :], low[rows, :])


def put(refs, rows, value):
    high, low = split(value)
    refs[0][rows, :] = high
    refs[1][rows, :] = low


HALF = D // 2


class Stream:
    def __init__(self, r, sources):
        self.r, self.sources, self.step = r, sources, 0
        self.copies(0, True)

    def copies(self, step, start):
        rows = pl.ds((step % 2) * HALF, HALF)
        refs, index = self.sources[step // 2]
        for part, ref in enumerate(refs):
            view = ref.at[rows, :] if index is None else ref.at[index, rows, :]
            copy = pltpu.make_async_copy(
                view, self.r.held.at[step % 2, part, pl.ds(0, HALF)], self.r.arrived.at[step % 2, part]
            )
            copy.start() if start else copy.wait()

    def product(self, right, store, extra=None, beside=None):
        held = self.r.held
        if beside is not None:
            (weight, target), tail = beside, HALF + beside[0][0].shape[0]
            for part in range(2):
                held[1, part, HALF:tail, :] = weight[part][...]
        for half in range(2):
            step = self.step
            self.step += 1
            if step + 1 < 2 * len(self.sources):
                self.copies(step + 1, True)
            self.copies(step, False)
            rows = pl.ds(half * HALF, HALF)
            end = tail if half and beside is not None else HALF
            acc = three_pass((held[half, 0, 0:end, :], held[half, 1, 0:end, :]), pair(right))
            if end > HALF:
                target[...] = acc[HALF:, :]
                acc = acc[:HALF, :]
            if extra is not None:
                acc = acc + three_pass(pair(extra[0], rows), extra[1])
            store[rows, :] = acc


def add_small(store, weight, right):
    for half in range(2):
        rows = pl.ds(half * HALF, HALF)
        store[rows, :] += three_pass(pair(weight, rows), right)


def stream_scratch():
    return dict(
        held=pltpu.VMEM((2, 2, HALF + BS, D), jnp.bfloat16),
        arrived=pltpu.SemaphoreType.DMA((2, 2)),
    )


def each(body, carry=(), step=128, count=D):
    def run(i, state):
        return body(pl.ds(pl.multiple_of(i * step, step), step), *state)

    return lax.fori_loop(0, count // step, run, carry)


def fold(v):
    return jnp.sum(v.reshape(v.shape[0] // 8, 8, v.shape[1]), axis=0)


def planes(channels, edges, body):
    lanes = edges // 128

    def run(i, state):
        base = pl.multiple_of((i // lanes) * 16, 16)
        lane = pl.ds(pl.multiple_of((i % lanes) * 128, 128), 128)
        body(base, lane)
        return state

    lax.fori_loop(0, (channels // 16) * lanes, run, 0)


def get9(ref, channels, base, lane):
    return [ref[pl.ds(k * channels + base, 16), lane] for k in range(9)]


def put9(ref, channels, base, lane, values):
    for k, v in enumerate(values):
        ref[pl.ds(k * channels + base, 16), lane] = v


def put9_split(r, channels, base, lane, values):
    for k, v in enumerate(values):
        high, low = split(v)
        r.t_h[pl.ds(k * channels + base, 16), lane] = high
        r.t_l[pl.ds(k * channels + base, 16), lane] = low


def row9(ref, lane):
    return [ref[k : k + 1, lane] for k in range(9)]


def terms_sum(sets, out):
    total = [None] * 9
    pairs = {}
    for index in TERMS:
        for n, ((li, left), (ri, right)) in enumerate(sets):
            key = (n, index[li], index[ri])
            if key not in pairs:
                pairs[key] = left[index[li]] * right[index[ri]]
    for index in TERMS:
        for n, ((li, left), (ri, right)) in enumerate(sets):
            term = index[3] * pairs[(n, index[li], index[ri])]
            slot = index[out]
            total[slot] = term if total[slot] is None else total[slot] + term
    return total


TILE9 = 192


def same_atom(r, scale, store, rows9):
    @pl.loop(0, rows9 // TILE9)
    def _(t):
        rows = pl.ds(pl.multiple_of(t * TILE9, TILE9), TILE9)
        store[rows, :] = scale * (
            one_pass(r.t_h[rows, :], r.same[...]) + one_pass(r.t_l[rows, :], r.same[...])
        )


def mixed(r, mixing, store, rows9):
    @pl.loop(0, rows9 // TILE9)
    def _(t):
        rows = pl.ds(pl.multiple_of(t * TILE9, TILE9), TILE9)
        store[rows, :] = three_pass(pair(mixing, rows), (r.t_h[...], r.t_l[...]))


def clear_tail(r, rows9):
    tail = r.t_h.shape[0] - rows9
    r.t_h[rows9:, :] = jnp.zeros((tail, r.t_h.shape[1]), jnp.bfloat16)
    r.t_l[rows9:, :] = jnp.zeros((tail, r.t_l.shape[1]), jnp.bfloat16)


def plane_scratch(rows9, edges):
    depth = -(-rows9 // 128) * 128
    return dict(
        t_h=pltpu.VMEM((depth, edges), jnp.bfloat16), t_l=pltpu.VMEM((depth, edges), jnp.bfloat16)
    )


def sig(v):
    return 1.0 / (1.0 + jnp.exp(-v))


def silu_parts(v):
    s = sig(v)
    return v * s, s * (1.0 + v * (1.0 - s))


def silu_slopes(v):
    s = sig(v)
    t = 1.0 - s
    return s * (1.0 + v * t), s * t * (2.0 + v * (t - s))


def first_layer(r, channels, edges, scale):
    rows9 = 9 * channels
    stream = Stream(r, [(r.out_t, None)])
    for ref in r.blank:
        ref[...] = jnp.zeros_like(ref)
    r.send(r.blank)
    feat = split(r.feat[...])

    @pl.loop(0, 2)
    def _(t):
        rows = pl.ds(pl.multiple_of(t * 512, 512), 512)
        r.pre0[rows, :] = three_pass(pair(r.in_t, rows), feat)

    def hidden(rows):
        put(r.hid, rows, silu_parts(r.pre0[rows, :])[0])
        return ()

    r.send(r.pre0)
    each(hidden)
    r.send(r.hid)
    stream.product(r.hid, r.out0)

    def latent(rows):
        put(r.lat0, rows, r.rows[0:1, :] * r.out0[rows, :])
        return ()

    r.send(r.out0)
    each(latent)
    r.send(r.lat0)
    r.w0[...] = three_pass(pair(r.env0w), pair(r.lat0))

    def embed(base, lane):
        w = r.w0[pl.ds(base, 16), lane]
        put9_split(r, channels, base, lane, [y * w for y in row9(r.shape, lane)])

    planes(channels, edges, embed)
    same_atom(r, scale, r.env0, rows9)
    r.send(r.env0)

    def multiply(base, lane):
        w = r.w0[pl.ds(base, 16), lane]
        emb = [y * w for y in row9(r.shape, lane)]
        env = get9(r.env0, channels, base, lane)
        put9(r.res0, channels, base, lane, terms_sum([((0, emb), (1, env))], 2))

    planes(channels, edges, multiply)
    r.send(r.res0)


def energy_up(r, channels, edges, scale):
    rows9 = 9 * channels
    env, factor = lambda: r.rows[0:1, :], lambda: r.rows[1:2, :]
    alpha = lambda: RES * r.rows[0:1, :] * r.rows[1:2, :]
    stream = Stream(
        r,
        [
            (r.mt, 0),
            (r.mt, 1),
            (r.mt, 2),
        ],
    )
    r.fetch(r.out0, r.mix)
    clear_tail(r, rows9)
    nothing = jnp.zeros((8, edges), jnp.float32)
    stream.product(r.lat0, r.pre1, (r.sc0_t, split(r.res0[0:channels, :])))

    def act1(rows):
        put(r.act1, rows, silu_parts(r.pre1[rows, :])[0])
        return ()

    r.send(r.pre1)
    each(act1)
    r.send(r.act1)
    stream.product(r.act1, r.out1)

    def lat1(rows, per):
        value = RES * env() * (r.out0[rows, :] + r.out1[rows, :])
        put(r.lat1, rows, value)
        return (per + fold(value * r.head[rows, :]),)

    r.send(r.out1)
    r.need(r.out0)
    (per1,) = each(lat1, (nothing,))
    r.send(r.lat1)
    stream.product(r.lat1, r.pre2, beside=(r.env1w, r.w1))

    def embed(base, lane):
        w = r.w1[pl.ds(base, 16), lane]
        put9_split(r, channels, base, lane, [y * w for y in row9(r.shape, lane)])

    planes(channels, edges, embed)
    same_atom(r, scale, r.env1, rows9)
    r.send(r.env1)

    def take(base, lane):
        put9_split(r, channels, base, lane, get9(r.res0, channels, base, lane))

    planes(channels, edges, take)
    r.need(r.mix)
    mixed(r, r.mix, r.feat1, rows9)
    r.send(r.feat1)

    def scalar(base, lane):
        f, e = get9(r.feat1, channels, base, lane), get9(r.env1, channels, base, lane)
        r.res1[pl.ds(base, 16), lane] = sum(a * b for a, b in zip(f, e)) * (1.0 / 3.0)

    planes(channels, edges, scalar)
    add_small(r.pre2, r.sc1_t, split(r.res1[...]))

    def act2(rows, per):
        act, slope = silu_parts(r.pre2[rows, :])
        put(r.pre2_bar, rows, (alpha() * env()) * r.top[rows, :] * slope)
        return (per + fold(act * r.top[rows, :]),)

    r.send(r.pre2)
    (per2,) = each(act2, (nothing,))
    r.send(r.pre2_bar)
    per1 = jnp.sum(per1, axis=0, keepdims=True)
    per2 = jnp.sum(per2, axis=0, keepdims=True)
    r.per[...] = jnp.zeros_like(r.per)
    r.per[0:1, :] = per1
    r.per[1:2, :] = per2


def energy_down(r, channels, edges, scale):
    rows9 = 9 * channels
    env, factor = lambda: r.rows[0:1, :], lambda: r.rows[1:2, :]
    alpha = lambda: RES * r.rows[0:1, :] * r.rows[1:2, :]
    stream = Stream(r, [(r.m, 2), (r.m, 1), (r.m, 0), (r.out, None)])
    r.fetch(r.feat1, r.env1)
    clear_tail(r, rows9)
    nothing = jnp.zeros((8, edges), jnp.float32)
    stream.product(r.pre2_bar, r.lat1_bar, beside=(r.sc1, r.res1_bar))
    r.fetch(r.out1, r.mix_t, r.pre1)
    r.need(r.feat1, r.env1)

    def back1(base, lane):
        g = r.res1_bar[pl.ds(base, 16), lane] * (1.0 / 3.0)
        put9_split(r, channels, base, lane, [g * f for f in get9(r.feat1, channels, base, lane)])
        put9(r.feat1_bar, channels, base, lane, [g * e for e in get9(r.env1, channels, base, lane)])

    planes(channels, edges, back1)
    r.send(r.feat1_bar)
    same_atom(r, scale, r.emb1_bar, rows9)
    r.send(r.emb1_bar)
    r.shape_bar[...] = jnp.zeros_like(r.shape_bar)

    def collect(w_ref, emb_ref, out_ref):
        def run(base, lane):
            w = w_ref[pl.ds(base, 16), lane]
            emb = get9(emb_ref, channels, base, lane)
            out_ref[pl.ds(base, 16), lane] = sum(y * v for y, v in zip(row9(r.shape, lane), emb))
            for k in range(9):
                r.shape_bar[k : k + 1, lane] += jnp.sum(emb[k] * w, axis=0, keepdims=True)

        planes(channels, edges, run)

    collect(r.w1, r.emb1_bar, r.w1_bar)
    w_pair = split(r.w1_bar[...])

    @pl.loop(0, 2)
    def _(t):
        rows = pl.ds(pl.multiple_of(t * 512, 512), 512)
        r.lat1_bar[rows, :] += three_pass(pair(r.env1w_t, rows), w_pair)

    def out1_bar(rows, total):
        value = r.lat1_bar[rows, :] + alpha() * r.head[rows, :]
        r.lat1_bar[rows, :] = value
        put(r.out1_bar, rows, (RES * env()) * value)
        return (total + fold(value * r.out1[rows, :]),)

    r.need(r.out1)
    (env_bar1,) = each(out1_bar, (nothing,))
    r.send(r.lat1_bar, r.out1_bar)
    r.fetch(r.env0, r.out0)
    stream.product(r.out1_bar, r.act1_bar)
    r.send(r.act1_bar)
    r.need(r.mix_t)

    def take_bar(base, lane):
        put9_split(r, channels, base, lane, get9(r.feat1_bar, channels, base, lane))

    planes(channels, edges, take_bar)
    mixed(r, r.mix_t, r.res0_bar, rows9)

    def pre1_bar(rows):
        put(r.pre1_bar, rows, r.act1_bar[rows, :] * silu_parts(r.pre1[rows, :])[1])
        return ()

    r.need(r.pre1)
    each(pre1_bar)
    r.send(r.pre1_bar)
    stream.product(r.pre1_bar, r.lat0_bar, beside=(r.sc0, r.w0_bar))
    r.res0_bar[0:channels, :] += r.w0_bar[...]
    r.send(r.res0_bar)
    r.fetch(r.pre0)

    def back0(base, lane):
        w = r.w0[pl.ds(base, 16), lane]
        emb = [y * w for y in row9(r.shape, lane)]
        g = get9(r.res0_bar, channels, base, lane)
        put9_split(r, channels, base, lane, terms_sum([((2, g), (0, emb))], 1))

    planes(channels, edges, back0)
    same_atom(r, scale, r.emb0_bar, rows9)

    def back0_feature(base, lane):
        g = get9(r.res0_bar, channels, base, lane)
        e = get9(r.env0, channels, base, lane)
        more = terms_sum([((2, g), (1, e))], 0)
        have = get9(r.emb0_bar, channels, base, lane)
        put9(r.emb0_bar, channels, base, lane, [a + b for a, b in zip(have, more)])

    r.need(r.env0)
    planes(channels, edges, back0_feature)
    r.send(r.emb0_bar)
    collect(r.w0, r.emb0_bar, r.w0_bar)
    w_pair0 = split(r.w0_bar[...])

    @pl.loop(0, 2)
    def _(t):
        rows = pl.ds(pl.multiple_of(t * 512, 512), 512)
        r.lat0_bar[rows, :] += three_pass(pair(r.env0w_t, rows), w_pair0)

    def out0_bar(rows, total):
        value = r.lat0_bar[rows, :] + RES * r.lat1_bar[rows, :]
        r.lat0_bar[rows, :] = value
        put(r.out0_bar, rows, env() * value)
        return (total + fold(value * r.out0[rows, :]),)

    r.need(r.out0)
    (env_bar0,) = each(out0_bar, (nothing,))
    r.send(r.lat0_bar, r.out0_bar)
    stream.product(r.out0_bar, r.hid_bar)

    def pre0_bar(rows):
        put(r.pre0_bar, rows, r.hid_bar[rows, :] * silu_parts(r.pre0[rows, :])[1])
        return ()

    r.send(r.hid_bar)
    r.need(r.pre0)
    each(pre0_bar)
    r.send(r.pre0_bar)
    r.bessel_bar[...] = three_pass(pair(r.in_w), pair(r.pre0_bar))
    down = lambda v: jnp.sum(v, axis=0, keepdims=True)
    env_bar = (
        RES * factor() * (r.per[0:1, :] + 2.0 * env() * r.per[1:2, :])
        + RES * down(env_bar1)
        + down(env_bar0)
    )
    row = lambda ref, k: ref[k : k + 1, :]
    unit = [row(r.geo, k) for k in range(3)]
    dist_bar = env_bar * row(r.geo, 4) + down(r.bessel_bar[0:NB, :] * r.dbessel[0:NB, :])
    unit_bar = harmonics_back_rows(unit, [row(r.shape_bar, k) for k in range(9)])
    along = sum(u * b for u, b in zip(unit, unit_bar))
    r.vec_bar[...] = jnp.zeros_like(r.vec_bar)
    for k in range(3):
        r.vec_bar[k : k + 1, :] = dist_bar * unit[k] + (unit_bar[k] - unit[k] * along) * row(r.geo, 3)
    r.force_part[...] = exact(r.vec_bar[...], r.ends[...])


def tangent_up(r, channels, edges, scale):
    rows9 = 9 * channels
    env, factor, env_dot = (
        lambda: r.rows[0:1, :],
        lambda: r.rows[1:2, :],
        lambda: r.env_row[0:1, :],
    )
    lead = lambda: RES * env() * env() * factor()
    lead_dot = lambda: 2.0 * RES * env() * factor() * env_dot()
    stream = Stream(
        r,
        [
            (r.out_t, None),
            (r.mt, 0),
            (r.mt, 1),
            (r.mt, 2),
        ],
    )
    r.fetch(r.pre0, r.out0)
    clear_tail(r, rows9)
    nothing = jnp.zeros((8, edges), jnp.float32)
    row = lambda ref, k: ref[k : k + 1, :]
    residual = [row(r.force, k) - row(r.label, k) for k in range(3)]
    r.loss_part[...] = row(r.label, 3) * sum(v * v for v in residual)
    r.cot[...] = jnp.zeros_like(r.cot)
    for k in range(3):
        r.cot[k : k + 1, :] = row(r.label, 4) * residual[k]
    vec_dot = exact(r.cot[...], r.ends[...], NT)
    vec_dot = [vec_dot[k : k + 1, :] for k in range(3)]
    unit = [row(r.geo, k) for k in range(3)]
    dist_dot = sum(u * v for u, v in zip(unit, vec_dot))
    unit_dot = [(v - u * dist_dot) * row(r.geo, 3) for u, v in zip(unit, vec_dot)]
    r.env_row[...] = jnp.broadcast_to(row(r.geo, 4) * dist_dot, r.env_row.shape)
    r.bessel_dot[...] = r.dbessel[...] * dist_dot
    r.shape_dot[...] = jnp.zeros_like(r.shape_dot)
    for k, value in enumerate(harmonics_dot_rows(unit, unit_dot)):
        r.shape_dot[k : k + 1, :] = value
    bessel = split(r.bessel_dot[...])

    @pl.loop(0, 2)
    def _(t):
        rows = pl.ds(pl.multiple_of(t * 512, 512), 512)
        r.pre0_dot[rows, :] = three_pass(pair(r.in_t, rows), bessel)

    def hidden(rows):
        put(r.hid_dot, rows, r.pre0_dot[rows, :] * silu_parts(r.pre0[rows, :])[1])
        return ()

    r.send(r.pre0_dot)
    r.need(r.pre0)
    each(hidden)
    r.send(r.hid_dot)
    r.fetch(r.env0)
    stream.product(r.hid_dot, r.tmp)

    def lat0(rows):
        value = env_dot() * r.out0[rows, :] + env() * r.tmp[rows, :]
        r.keep[rows, :] = value
        put(r.lat0_dot, rows, value)
        return ()

    r.need(r.out0)
    each(lat0)
    r.send(r.lat0_dot)
    r.fetch(r.pre1, r.out1)
    stream.product(r.lat0_dot, r.pre1_dot, beside=(r.env0w, r.w0_dot))

    def embed_dot(w_ref, w_dot_ref, base, lane):
        w, wd = w_ref[pl.ds(base, 16), lane], w_dot_ref[pl.ds(base, 16), lane]
        return [
            yd * w + y * wd for y, yd in zip(row9(r.shape, lane), row9(r.shape_dot, lane))
        ]

    def embed0(base, lane):
        put9_split(r, channels, base, lane, embed_dot(r.w0, r.w0_dot, base, lane))

    planes(channels, edges, embed0)
    same_atom(r, scale, r.env0_dot, rows9)
    r.send(r.env0_dot)
    r.need(r.env0)

    def multiply(base, lane):
        w = r.w0[pl.ds(base, 16), lane]
        emb = [y * w for y in row9(r.shape, lane)]
        emb_dot = embed_dot(r.w0, r.w0_dot, base, lane)
        e, ed = get9(r.env0, channels, base, lane), get9(r.env0_dot, channels, base, lane)
        put9(
            r.res0_dot,
            channels,
            base,
            lane,
            terms_sum([((0, emb_dot), (1, e)), ((0, emb), (1, ed))], 2),
        )

    planes(channels, edges, multiply)
    r.send(r.res0_dot)
    r.fetch(r.lat1, r.mix)
    add_small(r.pre1_dot, r.sc0_t, split(r.res0_dot[0:channels, :]))

    def act1(rows):
        put(r.act1_dot, rows, r.pre1_dot[rows, :] * silu_parts(r.pre1[rows, :])[1])
        return ()

    r.send(r.pre1_dot)
    r.need(r.pre1)
    each(act1)
    r.send(r.act1_dot)
    r.fetch(r.feat1, r.env1, r.pre2)
    stream.product(r.act1_dot, r.tmp)

    def lat1(rows, per):
        value = RES * (
            r.keep[rows, :] + env_dot() * r.out1[rows, :] + env() * r.tmp[rows, :]
        )
        put(r.lat1_dot, rows, value)
        lat = r.lat1[0][rows, :].astype(jnp.float32) + r.lat1[1][rows, :].astype(jnp.float32)
        part = factor() * (env_dot() * lat + env() * value)
        r.head_part[rows, :] = sum(part[:, s : s + 128] for s in range(0, edges, 128))
        return (per + fold(value * r.head[rows, :]),)

    r.need(r.out1, r.lat1)
    (per1,) = each(lat1, (nothing,))
    r.send(r.lat1_dot)
    stream.product(r.lat1_dot, r.tmp, beside=(r.env1w, r.w1_dot))

    def embed1(base, lane):
        put9_split(r, channels, base, lane, embed_dot(r.w1, r.w1_dot, base, lane))

    planes(channels, edges, embed1)
    same_atom(r, scale, r.env1_dot, rows9)
    r.send(r.env1_dot)
    r.need(r.mix)

    def take(base, lane):
        put9_split(r, channels, base, lane, get9(r.res0_dot, channels, base, lane))

    planes(channels, edges, take)
    mixed(r, r.mix, r.feat1_dot, rows9)
    r.send(r.feat1_dot)
    r.need(r.feat1, r.env1)

    def scalar(base, lane):
        f, fd = get9(r.feat1, channels, base, lane), get9(r.feat1_dot, channels, base, lane)
        e, ed = get9(r.env1, channels, base, lane), get9(r.env1_dot, channels, base, lane)
        total = sum(fd[k] * e[k] + f[k] * ed[k] for k in range(9))
        r.res1_dot[pl.ds(base, 16), lane] = total * (1.0 / 3.0)

    planes(channels, edges, scalar)
    add_small(r.tmp, r.sc1_t, split(r.res1_dot[...]))

    def act2(rows, per):
        v, vd, top = r.pre2[rows, :], r.tmp[rows, :], r.top[rows, :]
        s = sig(v)
        t = 1.0 - s
        slope, curve = s * (1.0 + v * t), s * t * (2.0 + v * (t - s))
        act_dot = slope * vd
        part = lead_dot() * (v * s) + lead() * act_dot
        r.last_part[rows, :] = sum(part[:, k : k + 128] for k in range(0, edges, 128))
        put(r.pre2_hat, rows, top * (lead_dot() * slope + lead() * curve * vd))
        return (per + fold(act_dot * top),)

    r.need(r.pre2)
    (per2,) = each(act2, (nothing,))
    r.send(r.pre2_hat)
    r.per_dot[...] = jnp.zeros_like(r.per_dot)
    r.per_dot[0:1, :] = jnp.sum(per1, axis=0, keepdims=True)
    r.per_dot[1:2, :] = jnp.sum(per2, axis=0, keepdims=True)


def tangent_down(r, channels, edges, scale):
    rows9 = 9 * channels
    env, factor, env_dot = (
        lambda: r.rows[0:1, :],
        lambda: r.rows[1:2, :],
        lambda: r.env_row[0:1, :],
    )
    stream = Stream(
        r,
        [
            (r.m, 2),
            (r.m, 1),
            (r.m, 0),
            (r.out, None),
        ],
    )
    r.fetch(r.feat1, r.feat1_dot, r.env1, r.env1_dot)
    clear_tail(r, rows9)
    stream.product(r.pre2_hat, r.hat1, beside=(r.sc1, r.small))
    r.fetch(r.emb1_bar, r.lat1_bar)
    r.need(r.feat1, r.feat1_dot, r.env1, r.env1_dot)

    def back1(base, lane):
        gh = r.small[pl.ds(base, 16), lane] * (1.0 / 3.0)
        g = r.res1_bar[pl.ds(base, 16), lane] * (1.0 / 3.0)
        f, fd = get9(r.feat1, channels, base, lane), get9(r.feat1_dot, channels, base, lane)
        e, ed = get9(r.env1, channels, base, lane), get9(r.env1_dot, channels, base, lane)
        put9_split(r, channels, base, lane, [gh * f[k] + g * fd[k] for k in range(9)])
        put9(r.feat1_hat, channels, base, lane, [gh * e[k] + g * ed[k] for k in range(9)])

    planes(channels, edges, back1)
    r.send(r.feat1_hat)
    r.fetch(r.mix_t, r.pre1, r.act1_bar, r.pre1_dot)
    same_atom(r, scale, r.plane, rows9)

    def collect(bar_ref, out_ref):
        def run(base, lane):
            bar = get9(bar_ref, channels, base, lane)
            hat = get9(r.plane, channels, base, lane)
            y, yd = row9(r.shape, lane), row9(r.shape_dot, lane)
            out_ref[pl.ds(base, 16), lane] = sum(
                yd[k] * bar[k] + y[k] * hat[k] for k in range(9)
            )

        planes(channels, edges, run)

    r.need(r.emb1_bar)
    collect(r.emb1_bar, r.w1_hat)
    w_pair = split(r.w1_hat[...])

    @pl.loop(0, 2)
    def _(t):
        rows = pl.ds(pl.multiple_of(t * 512, 512), 512)
        r.hat1[rows, :] += three_pass(pair(r.env1w_t, rows), w_pair)

    def out1(rows):
        value = r.hat1[rows, :] + (RES * factor() * env_dot()) * r.head[rows, :]
        r.hat1[rows, :] = value
        put(r.out1_hat, rows, RES * (env_dot() * r.lat1_bar[rows, :] + env() * value))
        return ()

    r.need(r.lat1_bar)
    each(out1)
    r.send(r.out1_hat)
    r.fetch(r.res0_bar, r.env0, r.env0_dot)
    stream.product(r.out1_hat, r.tmp)
    r.need(r.mix_t)

    def take(base, lane):
        put9_split(r, channels, base, lane, get9(r.feat1_hat, channels, base, lane))

    planes(channels, edges, take)
    mixed(r, r.mix_t, r.res0_hat, rows9)

    def pre1(rows):
        slope, curve = silu_slopes(r.pre1[rows, :])
        put(
            r.pre1_hat,
            rows,
            r.tmp[rows, :] * slope + r.act1_bar[rows, :] * curve * r.pre1_dot[rows, :],
        )
        return ()

    r.need(r.pre1, r.act1_bar, r.pre1_dot)
    each(pre1)
    r.send(r.pre1_hat)
    r.fetch(r.emb0_bar, r.lat0_bar)
    stream.product(r.pre1_hat, r.tmp, beside=(r.sc0, r.small))
    r.res0_hat[0:channels, :] += r.small[...]

    def embed_pair(base, lane):
        w, wd = r.w0[pl.ds(base, 16), lane], r.w0_dot[pl.ds(base, 16), lane]
        y, yd = row9(r.shape, lane), row9(r.shape_dot, lane)
        emb = [a * w for a in y]
        emb_dot = [b * w + a * wd for a, b in zip(y, yd)]
        return emb, emb_dot

    def back0(base, lane):
        emb, emb_dot = embed_pair(base, lane)
        gh, g = get9(r.res0_hat, channels, base, lane), get9(r.res0_bar, channels, base, lane)
        put9_split(
            r, channels, base, lane, terms_sum([((2, gh), (0, emb)), ((2, g), (0, emb_dot))], 1)
        )

    r.need(r.res0_bar)
    planes(channels, edges, back0)
    r.fetch(r.pre0, r.hid_bar, r.pre0_dot)
    same_atom(r, scale, r.plane, rows9)

    def back0_feature(base, lane):
        gh, g = get9(r.res0_hat, channels, base, lane), get9(r.res0_bar, channels, base, lane)
        e, ed = get9(r.env0, channels, base, lane), get9(r.env0_dot, channels, base, lane)
        more = terms_sum([((2, gh), (1, e)), ((2, g), (1, ed))], 0)
        have = get9(r.plane, channels, base, lane)
        put9(r.plane, channels, base, lane, [a + b for a, b in zip(have, more)])

    r.need(r.env0, r.env0_dot)
    planes(channels, edges, back0_feature)
    r.need(r.emb0_bar)
    collect(r.emb0_bar, r.w0_hat)
    w_pair0 = split(r.w0_hat[...])

    @pl.loop(0, 2)
    def _(t):
        rows = pl.ds(pl.multiple_of(t * 512, 512), 512)
        r.tmp[rows, :] += three_pass(pair(r.env0w_t, rows), w_pair0)

    def out0(rows):
        value = r.tmp[rows, :] + RES * r.hat1[rows, :]
        put(r.out0_hat, rows, env_dot() * r.lat0_bar[rows, :] + env() * value)
        return ()

    r.need(r.lat0_bar)
    each(out0)
    r.send(r.out0_hat)
    stream.product(r.out0_hat, r.tmp)

    def pre0(rows):
        slope, curve = silu_slopes(r.pre0[rows, :])
        put(
            r.pre0_hat,
            rows,
            r.tmp[rows, :] * slope + r.hid_bar[rows, :] * curve * r.pre0_dot[rows, :],
        )
        return ()

    r.need(r.pre0, r.hid_bar, r.pre0_dot)
    each(pre0)
    r.send(r.pre0_hat)


def small_gradients(r, channels, edges):
    r.fetch(r.hid, r.out0_hat, r.pre0_bar, r.pre0_hat)
    tiles = [pl.ds(t * HALF, HALF) for t in range(2)]
    for rows in tiles:
        r.out_grad[rows, :] = three_pass(pair(r.hid_dot, rows), pair(r.out0_bar), NT)
    r.need(r.hid, r.out0_hat)
    for rows in tiles:
        r.out_grad[rows, :] += three_pass(pair(r.hid, rows), pair(r.out0_hat), NT)
    r.send(r.out_grad)
    r.need(r.pre0_bar, r.pre0_hat)
    r.fetch(r.feat1_bar, r.res0_dot, r.feat1_hat, r.res0)
    r.in_grad[...] = three_pass(split(r.bessel_dot[...]), pair(r.pre0_bar), NT) + three_pass(
        split(r.feat[...]), pair(r.pre0_hat), NT
    )
    r.fetch(r.lat0_dot, r.lat0, r.pre1_bar, r.pre1_hat)

    def twice(first, second, third, fourth):
        return three_pass(split(first), pair(second), NT) + three_pass(split(third), pair(fourth), NT)

    r.need(r.feat1_bar, r.res0_dot, r.feat1_hat, r.res0)
    r.fetch(r.lat1_dot, r.lat1, r.pre2_bar, r.pre2_hat)
    r.need(r.lat0_dot, r.lat0, r.pre1_bar, r.pre1_hat)
    r.env_grad[0] = twice(r.w0_bar[...], r.lat0_dot, r.w0_hat[...], r.lat0)
    r.sc_grad[0] = twice(r.res0_dot[0:channels, :], r.pre1_bar, r.res0[0:channels, :], r.pre1_hat)
    r.need(r.lat1_dot, r.lat1, r.pre2_bar, r.pre2_hat)
    r.env_grad[1] = twice(r.w1_bar[...], r.lat1_dot, r.w1_hat[...], r.lat1)
    r.sc_grad[1] = twice(r.res1_dot[...], r.pre2_bar, r.res1[...], r.pre2_hat)
    for order, (start, stop) in enumerate(((0, 1), (1, 4), (4, 9))):
        total = None
        for k in range(start, stop):
            part = slice(k * channels, (k + 1) * channels)
            term = three_pass(split(r.feat1_bar[part, :]), split(r.res0_dot[part, :]), NT)
            term = term + three_pass(split(r.feat1_hat[part, :]), split(r.res0[part, :]), NT)
            total = term if total is None else total + term
        r.mix_grad[order] = total


def load_blocks(r):
    depth = 3

    def incoming(step):
        slot = lax.rem(step, depth)
        return [
            pltpu.make_async_copy(
                r.piece.at[r.where[step * SIDE + j]], r.blocks.at[slot, j], r.sem.at[slot, j]
            )
            for j in range(SIDE)
        ]

    def outgoing(step):
        slot, m, i = step % 2, step // SIDE, step % SIDE
        rows = pl.ds(pl.multiple_of(i * BS, BS), BS)
        plain = [
            pltpu.make_async_copy(
                r.flat.at[slot, part], r.m[part].at[m, rows, :], r.out_sem.at[slot, part]
            )
            for part in range(2)
        ]
        turned = [
            pltpu.make_async_copy(
                r.turned.at[slot, part], r.mt[part].at[m, :, rows], r.out_sem.at[slot, 2 + part]
            )
            for part in range(2)
        ]
        return plain + turned

    steps = 3 * SIDE
    for step in range(depth - 1):
        for copy in incoming(step):
            copy.start()
    eye = (
        lax.broadcasted_iota(jnp.int32, (BS, BS), 0) == lax.broadcasted_iota(jnp.int32, (BS, BS), 1)
    ).astype(jnp.bfloat16)

    @pl.loop(0, steps)
    def _(step):
        @pl.when(step + depth - 1 < steps)
        def _():
            for copy in incoming(step + depth - 1):
                copy.start()

        for copy in incoming(step):
            copy.wait()

        @pl.when(step >= 2)
        def _():
            for copy in outgoing(step - 2):
                copy.wait()

        slot, source = step % 2, lax.rem(step, depth)
        for j in range(SIDE):
            part = slice(j * BS, (j + 1) * BS)
            high, low = split(r.blocks[source, j])
            r.flat[slot, 0, :, part] = high
            r.flat[slot, 1, :, part] = low
            r.turned[slot, 0, part, :] = one_pass(eye, high, NT).astype(jnp.bfloat16)
            r.turned[slot, 1, part, :] = low.T
        for copy in outgoing(step):
            copy.start()

    def last(i):
        return [
            pltpu.make_async_copy(
                r.piece.at[r.where[(3 * SIDE + i) * SIDE + j]],
                r.last.at[pl.ds(i * BS, BS), pl.ds(j * BS, BS)],
                r.last_sem.at[i, j],
            )
            for j in range(SIDE)
        ]

    for i in range(SIDE):
        for copy in last(i):
            copy.start()
    for step in (steps - 2, steps - 1):
        for copy in outgoing(step):
            copy.wait()
    head = r.head[...]
    for i in range(SIDE):
        for copy in last(i):
            copy.wait()

    def top(rows):
        r.top[rows, :] = jnp.sum(r.last[rows, :] * head, axis=1, keepdims=True)
        return ()

    each(top)


def block_gradients(r, channels, edges, targets):
    names = [(r.lat0_dot, r.lat0, r.pre1_bar, r.pre1_hat)]
    names.append((r.act1_dot, r.act1, r.out1_bar, r.out1_hat))
    names.append((r.lat1_dot, r.lat1, r.pre2_bar, r.pre2_hat))
    tile = HALF
    count = tile // BS * SIDE

    def incoming(m):
        return [
            pltpu.make_async_copy(ref, r.held.at[m % 2, a, part], r.arrived.at[m % 2, a, part])
            for a, refs in enumerate(names[m])
            for part, ref in enumerate(refs)
        ]

    for copy in incoming(0):
        copy.start()

    def spot(q):
        rows = pl.ds(pl.multiple_of((q // SIDE) * BS, BS), BS)
        return rows, pl.ds(pl.multiple_of((q % SIDE) * BS, BS), BS)

    def wait_tile(slot):
        whole = r.out[0].at[pl.ds(0, count)]
        pltpu.make_async_copy(whole, whole, r.sent_sem.at[slot]).wait()

    def send_tile(first, slot):
        def one(q, state):
            which, where = r.which[first + q], r.where[first + q]
            for n in range(targets):

                @pl.when(which == n)
                def _(n=n):
                    pltpu.make_async_copy(
                        r.stage.at[slot, *spot(q)], r.out[n].at[where], r.sent_sem.at[slot]
                    ).start()

            return state

        lax.fori_loop(0, count, one, 0)

    for m in (3, 0, 1, 2):
        if m < 3:
            if m + 1 < 3:
                for copy in incoming(m + 1):
                    copy.start()
            for copy in incoming(m):
                copy.wait()
            held = lambda a, which=slice(None): (
                r.held[m % 2, a, 0, which, :],
                r.held[m % 2, a, 1, which, :],
            )
        for t in range(2):
            if m != 3:
                wait_tile(t)
            rows = pl.ds(t * tile, tile)
            if m < 3:
                r.stage[t] = three_pass(held(0, rows), held(2), NT) + three_pass(
                    held(1, rows), held(3), NT
                )
            else:
                r.stage[t] = r.lead[rows, :] * r.head[...]
            send_tile((m * SIDE + t * (tile // BS)) * SIDE, t)
    wait_tile(0)
    wait_tile(1)


def soap_kernel(count, *refs):
    grad, weight, first, second, left, right, lstat, rstat, average = refs[:9]
    outs = refs[9:]
    tn_dims = ((0,), (0,))

    def mm(a, b, dims=((1,), (0,))):
        return [three_pass(split(x), split(y), dims) for x, y in zip(a, b)]

    load = lambda ref: [ref[s] for s in range(count)]
    g, l, rr = load(grad), load(left), load(right)
    rotated = mm(mm(l, g, tn_dims), rr)
    first_new = [0.9 * first[s] + 0.1 * rotated[s] for s in range(count)]
    second_new = [0.99 * second[s] + 0.01 * rotated[s] * rotated[s] for s in range(count)]
    normal = [
        a * (1.0 / (1.0 - 0.9**ADAM_STEP)) / (jnp.sqrt(b * (1.0 / (1.0 - 0.99**ADAM_STEP))) + 1e-08)
        for a, b in zip(first_new, second_new)
    ]
    step = mm(mm(l, normal), rr, NT)
    for s in range(count):
        new = weight[s] - 0.01 * (step[s] + 0.01 * weight[s])
        outs[0][s] = new
        outs[7][s] = 0.99 * average[s] + 0.01 * new
        outs[2][s] = second_new[s]
    plain = mm(mm(l, first_new), rr, NT)
    ls = [0.95 * lstat[s] + 0.05 * v for s, v in enumerate(mm(g, g, NT))]
    rs = [0.95 * rstat[s] + 0.05 * v for s, v in enumerate(mm(g, g, tn_dims))]
    for s in range(count):
        outs[5][s] = ls[s]
        outs[6][s] = rs[s]
    x = mm(ls, l) + mm(rs, rr)
    x = [v / jnp.sqrt(jnp.sum(v * v)) for v in x]
    for _ in range(NS_STEPS):
        x = [1.5 * a - 0.5 * b for a, b in zip(x, mm(mm(x, x, NT), x))]
    ln, rn = x[:count], x[count:]
    out = mm(mm(ln, plain, tn_dims), rn)
    for s in range(count):
        outs[3][s] = ln[s]
        outs[4][s] = rn[s]
        outs[1][s] = out[s]


def soap_update(arrays):
    slots = arrays[0].shape[0]
    count = 4 if slots % 4 == 0 else 1
    spec = pl.BlockSpec((count, BS, BS), lambda s: (s, 0, 0))
    return pl.pallas_call(
        partial(soap_kernel, count),
        grid=(slots // count,),
        out_shape=[f32(slots, BS, BS)] * 8,
        in_specs=[spec] * 9,
        out_specs=[spec] * 8,
        compiler_params=pltpu.CompilerParams(vmem_limit_bytes=40 * 2**20),
    )(*arrays)


def adamw(weight, first, second, grad):
    first_new = 0.9 * first + 0.1 * grad
    second_new = 0.99 * second + 0.01 * grad * grad
    normal = (
        first_new
        / (1.0 - 0.9**ADAM_STEP)
        / (jnp.sqrt(second_new / (1.0 - 0.99**ADAM_STEP)) + 1e-08)
    )
    return (weight - 0.01 * (normal + 0.01 * weight), first_new, second_new)


def to_matrices(blocks):
    return (
        blocks.reshape(2 * LAYERS, SIDE, SIDE, BS, BS).transpose(0, 1, 3, 2, 4).reshape(2 * LAYERS, D, D)
    )


def to_blocks(matrices):
    return (
        matrices.reshape(2 * LAYERS, SIDE, BS, SIDE, BS)
        .transpose(0, 1, 3, 2, 4)
        .reshape(2 * LAYERS * SIDE * SIDE, BS, BS)
    )


def tables(block_owner, slots, sizes):
    ids = jnp.arange(block_owner.shape[0], dtype=jnp.int32)
    inverse = jnp.sum(jnp.where(block_owner[None] == ids[:, None], ids[None], 0), axis=1)
    if not is_cube(sizes):
        return jnp.zeros_like(inverse), inverse, inverse
    y, x, z, core = place()
    device, slot = inverse // slots, inverse % slots
    rank = jnp.sum(
        jnp.where(
            jnp.asarray(Z_ORDER)[z][:, None] == (device // 2 % 4)[None],
            jnp.arange(4, dtype=jnp.int32)[:, None],
            0,
        ),
        axis=0,
    )
    which = ((device % 2) ^ core) * 4 + rank
    where = (((device // 8 % 2) ^ x) * 2 + ((device // 16) ^ y)) * slots + slot
    return which, where, inverse


def sum_pieces(pieces, sizes, slots):
    if not is_cube(sizes):
        total = lax.psum_scatter(pieces[0], AX, scatter_dimension=0, tiled=True)
        return total, total
    chunks = [pieces[p] + hop(pieces[4 + p], HOP_CORE) for p in range(4)]
    return reduce_chips([c.reshape(2, 2, slots, BS, BS) for c in chunks])


def block_diagonal(mixing, depth):
    channels = mixing.shape[-1]
    rows = []
    for k in range(9):
        block = mixing[0 if k == 0 else 1 if k < 4 else 2]
        rows.append(jnp.pad(block, ((0, 0), (k * channels, depth - (k + 1) * channels))))
    return jnp.concatenate(rows, axis=0)


def fast_chain(weights, every, inverse, targets, which, where, scale, add_up, after_first, blank, label, ends, vec, live, src, ss, st):
    pair_in, pair_out, env_weight, scalar_weight, mix_weight, energy_head = weights
    channels, edges = env_weight.shape[1], vec.shape[1]
    rows9 = 9 * channels
    depth = -(-rows9 // 128) * 128
    head = energy_head[:D]
    factor = jnp.sum(energy_head[D:, None] * ss, axis=0)
    inv, unit, env, denv, bessel, dbessel = geometry(vec, live)
    pad_rows = lambda v, n: jnp.pad(v, ((0, n - v.shape[0]), (0, 0)))
    shape = pad_rows(harmonics(unit), 16)
    feat = jnp.concatenate([bessel, ss, st], axis=0)
    rows = pad_rows(jnp.stack([env, factor]), 8)
    geo = pad_rows(jnp.concatenate([unit, inv[None], denv[None]], axis=0), 8)
    dbessel_rows = pad_rows(dbessel, 2 * NB)
    same = (src[:, None] == src[None]).astype(jnp.bfloat16)
    cut = split_outside
    in_t, in_w, out_t, out_w = cut(pair_in.T), cut(pair_in), cut(pair_out.T), cut(pair_out)
    env_w, env_t = cut(env_weight), cut(env_weight.transpose(0, 2, 1))
    sc_w, sc_t = cut(scalar_weight), cut(scalar_weight.transpose(0, 2, 1))
    layer = lambda parts, l: tuple(v[l] for v in parts)
    mix_w = cut(block_diagonal(mix_weight, depth))
    mix_t = cut(block_diagonal(mix_weight.transpose(0, 2, 1), depth))
    wide, plane, narrow = (D, edges), (rows9, edges), (channels, edges)
    unit_flops = 6 * D * D * edges
    temps = dict(**stream_scratch(), **plane_scratch(rows9, edges))
    args = (channels, edges, scale)

    one = kernel_call(
        lambda r: first_layer(r, *args),
        dict(shape=shape, rows=rows, same=same, feat=feat, in_t=in_t, env0w=layer(env_w, 0)),
        dict(w0=f32(*narrow)),
        temps,
        sent=dict(
            pre0=f32(*wide),
            out0=f32(*wide),
            hid=pair_of(*wide),
            lat0=pair_of(*wide),
            env0=f32(*plane),
            res0=f32(*plane),
            blank=tuple(f32(*shape) for shape in blank),
        ),
        hbm=dict(out_t=out_t),
        flops=unit_flops,
    )
    every = after_first(one.blank, every)
    loaded = kernel_call(
        load_blocks,
        dict(head=head[None]),
        dict(last=f32(D, D), top=f32(D, 1)),
        dict(
            blocks=pltpu.VMEM((3, SIDE, BS, BS), jnp.float32),
            flat=pltpu.VMEM((2, 2, BS, D), jnp.bfloat16),
            turned=pltpu.VMEM((2, 2, D, BS), jnp.bfloat16),
            sem=pltpu.SemaphoreType.DMA((3, SIDE)),
            out_sem=pltpu.SemaphoreType.DMA((2, 4)),
            last_sem=pltpu.SemaphoreType.DMA((SIDE, SIDE)),
        ),
        hbm=dict(piece=every),
        hbm_out=dict(m=pair_of(3, D, D), mt=pair_of(3, D, D)),
        smem=dict(where=inverse),
    )
    head_col = head[:, None]
    up = kernel_call(
        lambda r: energy_up(r, *args),
        dict(
            shape=shape,
            rows=rows,
            same=same,
            head=head_col,
            top=loaded.top,
            lat0=one.lat0,
            res0=one.res0,
            sc0_t=layer(sc_t, 0),
            sc1_t=layer(sc_t, 1),
            env1w=layer(env_w, 1),
        ),
        dict(w1=f32(*narrow), res1=f32(*narrow), per=f32(8, edges)),
        temps,
        late=dict(out0=one.out0, mix=mix_w),
        sent=dict(
            pre1=f32(*wide),
            out1=f32(*wide),
            pre2=f32(*wide),
            act1=pair_of(*wide),
            lat1=pair_of(*wide),
            pre2_bar=pair_of(*wide),
            env1=f32(*plane),
            feat1=f32(*plane),
        ),
        hbm=dict(mt=loaded.mt),
        flops=3 * unit_flops,
    )
    down = kernel_call(
        lambda r: energy_down(r, *args),
        dict(
            shape=shape,
            rows=rows,
            same=same,
            head=head_col,
            geo=geo,
            dbessel=dbessel_rows,
            ends=ends,
            w0=one.w0,
            w1=up.w1,
            per=up.per,
            pre2_bar=up.pre2_bar,
            sc0=layer(sc_w, 0),
            sc1=layer(sc_w, 1),
            env0w_t=layer(env_t, 0),
            env1w_t=layer(env_t, 1),
            in_w=in_w,
        ),
        dict(
            res1_bar=f32(*narrow),
            w1_bar=f32(*narrow),
            w0_bar=f32(*narrow),
            shape_bar=f32(16, edges),
            force_part=f32(8, ends.shape[1]),
            bessel_bar=f32(16, edges),
        ),
        dict(**temps, vec_bar=pltpu.VMEM((8, edges), jnp.float32)),
        late=dict(
            pre0=one.pre0,
            out0=one.out0,
            env0=one.env0,
            pre1=up.pre1,
            out1=up.out1,
            env1=up.env1,
            feat1=up.feat1,
            mix_t=mix_t,
        ),
        sent=dict(
            lat1_bar=f32(*wide),
            act1_bar=f32(*wide),
            lat0_bar=f32(*wide),
            hid_bar=f32(*wide),
            out1_bar=pair_of(*wide),
            pre1_bar=pair_of(*wide),
            out0_bar=pair_of(*wide),
            pre0_bar=pair_of(*wide),
            feat1_bar=f32(*plane),
            emb1_bar=f32(*plane),
            res0_bar=f32(*plane),
            emb0_bar=f32(*plane),
        ),
        hbm=dict(m=loaded.m, out=out_w),
        flops=4 * unit_flops,
    )
    force = add_up(down.force_part)
    tan = kernel_call(
        lambda r: tangent_up(r, *args),
        dict(
            shape=shape,
            rows=rows,
            same=same,
            geo=geo,
            dbessel=dbessel_rows,
            ends=ends,
            force=force,
            label=label,
            head=head_col,
            top=loaded.top,
            w0=one.w0,
            w1=up.w1,
            in_t=in_t,
            sc0_t=layer(sc_t, 0),
            sc1_t=layer(sc_t, 1),
            env0w=layer(env_w, 0),
            env1w=layer(env_w, 1),
        ),
        dict(
            w0_dot=f32(*narrow),
            w1_dot=f32(*narrow),
            res1_dot=f32(*narrow),
            head_part=f32(D, 128),
            last_part=f32(D, 128),
            per_dot=f32(8, edges),
            env_row=f32(8, edges),
            shape_dot=f32(16, edges),
            bessel_dot=f32(2 * NB, edges),
            loss_part=f32(1, ends.shape[1]),
        ),
        dict(
            **temps,
            cot=pltpu.VMEM((8, ends.shape[1]), jnp.float32),
            tmp=pltpu.VMEM(wide, jnp.float32),
            keep=pltpu.VMEM(wide, jnp.float32),
        ),
        late=dict(
            pre0=one.pre0,
            out0=one.out0,
            env0=one.env0,
            pre1=up.pre1,
            out1=up.out1,
            pre2=up.pre2,
            env1=up.env1,
            feat1=up.feat1,
            lat1=up.lat1,
            mix=mix_w,
        ),
        sent=dict(
            pre0_dot=f32(*wide),
            pre1_dot=f32(*wide),
            hid_dot=pair_of(*wide),
            lat0_dot=pair_of(*wide),
            act1_dot=pair_of(*wide),
            lat1_dot=pair_of(*wide),
            pre2_hat=pair_of(*wide),
            env0_dot=f32(*plane),
            res0_dot=f32(*plane),
            env1_dot=f32(*plane),
            feat1_dot=f32(*plane),
        ),
        hbm=dict(out_t=out_t, mt=loaded.mt),
        flops=4 * unit_flops,
    )
    hat = kernel_call(
        lambda r: tangent_down(r, *args),
        dict(
            shape=shape,
            rows=rows,
            same=same,
            shape_dot=tan.shape_dot,
            env_row=tan.env_row,
            head=head_col,
            pre2_hat=tan.pre2_hat,
            w0=one.w0,
            w0_dot=tan.w0_dot,
            res1_bar=down.res1_bar,
            sc0=layer(sc_w, 0),
            sc1=layer(sc_w, 1),
            env0w_t=layer(env_t, 0),
            env1w_t=layer(env_t, 1),
        ),
        dict(w1_hat=f32(*narrow), w0_hat=f32(*narrow)),
        dict(
            **temps,
            hat1=pltpu.VMEM(wide, jnp.float32),
            tmp=pltpu.VMEM(wide, jnp.float32),
            small=pltpu.VMEM(narrow, jnp.float32),
            plane=pltpu.VMEM(plane, jnp.float32),
            res0_hat=pltpu.VMEM(plane, jnp.float32),
        ),
        late=dict(
            pre0=one.pre0,
            env0=one.env0,
            pre1=up.pre1,
            env1=up.env1,
            feat1=up.feat1,
            lat1_bar=down.lat1_bar,
            act1_bar=down.act1_bar,
            lat0_bar=down.lat0_bar,
            hid_bar=down.hid_bar,
            emb1_bar=down.emb1_bar,
            emb0_bar=down.emb0_bar,
            res0_bar=down.res0_bar,
            pre0_dot=tan.pre0_dot,
            pre1_dot=tan.pre1_dot,
            env1_dot=tan.env1_dot,
            feat1_dot=tan.feat1_dot,
            env0_dot=tan.env0_dot,
            mix_t=mix_t,
        ),
        sent=dict(
            out1_hat=pair_of(*wide),
            pre1_hat=pair_of(*wide),
            out0_hat=pair_of(*wide),
            pre0_hat=pair_of(*wide),
            feat1_hat=f32(*plane),
        ),
        hbm=dict(m=loaded.m, out=out_w),
        flops=4 * unit_flops,
    )
    env_dot = tan.env_row[0]
    loss = jnp.sum(tan.loss_part)
    lead_sum = jnp.sum(tan.last_part, axis=1)
    head_grad = RES * jnp.sum(tan.head_part, axis=1) + jnp.sum(
        lead_sum[:, None] * loaded.last, axis=0
    )
    per1, per2 = up.per[0], up.per[1]
    energy_dot = env_dot * RES * (per1 + env * per2) + env * RES * (
        tan.per_dot[0] + env_dot * per2 + env * tan.per_dot[1]
    )
    head_grad = jnp.concatenate([head_grad, jnp.sum(ss * energy_dot[None], axis=1)])
    made = kernel_call(
        lambda r: block_gradients(r, channels, edges, targets),
        dict(
            lead=lead_sum[:, None],
            head=head[None],
        ),
        {},
        dict(
            held=pltpu.VMEM((2, 4, 2, D, edges), jnp.bfloat16),
            arrived=pltpu.SemaphoreType.DMA((2, 4, 2)),
            stage=pltpu.VMEM((2, HALF, D), jnp.float32),
            sent_sem=pltpu.SemaphoreType.DMA((2,)),
        ),
        hbm=dict(
            lat0_dot=tan.lat0_dot,
            act1_dot=tan.act1_dot,
            lat1_dot=tan.lat1_dot,
            pre2_hat=tan.pre2_hat,
            lat0=one.lat0,
            act1=up.act1,
            lat1=up.lat1,
            pre2_bar=up.pre2_bar,
            pre1_bar=down.pre1_bar,
            out1_bar=down.out1_bar,
            pre1_hat=hat.pre1_hat,
            out1_hat=hat.out1_hat,
        ),
        hbm_out=dict(out=[f32(every.shape[0] // targets, BS, BS) for _ in range(targets)]),
        smem=dict(which=which, where=where),
        flops=6 * unit_flops,
    )

    feat = lax.optimization_barrier((feat, made.out[0]))[0]
    small = kernel_call(
        lambda r: small_gradients(r, channels, edges),
        dict(
            feat=feat,
            bessel_dot=tan.bessel_dot,
            hid_dot=tan.hid_dot,
            out0_bar=down.out0_bar,
            w0_bar=down.w0_bar,
            w1_bar=down.w1_bar,
            w0_hat=hat.w0_hat,
            w1_hat=hat.w1_hat,
            res1=up.res1,
            res1_dot=tan.res1_dot,
        ),
        dict(
            in_grad=f32(2 * NB, D),
            mix_grad=f32(3, channels, channels),
            env_grad=f32(2, channels, D),
            sc_grad=f32(2, channels, D),
        ),
        {},
        late=dict(
            hid=one.hid,
            out0_hat=hat.out0_hat,
            pre0_bar=down.pre0_bar,
            pre0_hat=hat.pre0_hat,
            feat1_bar=down.feat1_bar,
            res0_dot=tan.res0_dot,
            feat1_hat=hat.feat1_hat,
            res0=one.res0,
            lat0_dot=tan.lat0_dot,
            lat0=one.lat0,
            pre1_bar=down.pre1_bar,
            pre1_hat=hat.pre1_hat,
            lat1_dot=tan.lat1_dot,
            lat1=up.lat1,
            pre2_bar=up.pre2_bar,
            pre2_hat=tan.pre2_hat,
        ),
        sent=dict(out_grad=f32(D, D)),
        flops=2 * unit_flops,
    )

    return small, head_grad, loss, made


def local(
    sizes,
    edge_vec,
    edge_live,
    source,
    target,
    species,
    force_label,
    force_mask,
    block_owner,
    pair_in_weight,
    pair_in_first,
    pair_in_second,
    pair_out_weight,
    pair_out_first,
    pair_out_second,
    env_weight,
    env_first,
    env_second,
    scalar_weight,
    scalar_first,
    scalar_second,
    mix_weight,
    mix_first,
    mix_second,
    energy_head,
    head_first,
    head_second,
    soap_weight,
    soap_first,
    soap_second,
    soap_left,
    soap_right,
    soap_lstat,
    soap_rstat,
    soap_average,
):
    devices = sizes[0] * sizes[1]
    edges = edge_vec.shape[1]
    per_atoms = force_label.shape[1]
    atoms = per_atoms * devices
    me = lax.axis_index("irrep") * sizes[1] + lax.axis_index("edge")
    scale = math.sqrt(per_atoms / edges)
    as_float = lambda v: v.astype(jnp.float32)

    labels = jnp.concatenate([force_label, as_float(force_mask)[None]], axis=0).reshape(-1)
    packed = jnp.concatenate(
        [
            edge_vec,
            as_float(source)[None],
            as_float(target)[None],
            as_float(edge_live)[None],
            jnp.pad(labels, (0, edges - labels.shape[0]))[None],
        ],
        axis=0,
    )
    every = gather_small(packed, sizes)
    label_all = every[:, 6, : 4 * per_atoms].reshape(devices, 4, per_atoms)
    label_all = label_all.transpose(1, 0, 2).reshape(4, atoms)
    label_mask = label_all[3]
    label_total = jnp.sum(label_mask)
    payload = every[:, :5].transpose(0, 2, 1).reshape(devices * edges, 5)
    all_source = every[:, 3].reshape(-1).astype(jnp.int32)
    all_live = every[:, 5].reshape(-1)

    low = (all_source[:, None] % 32 == jnp.arange(32)[None]).astype(jnp.bfloat16)
    high = (all_source[None] // 32 == jnp.arange(-(-atoms // 32))[:, None]) & (all_live[None] > 0)
    counts = jnp.dot(
        high.astype(jnp.bfloat16), low, preferred_element_type=jnp.float32
    ).reshape(-1)[:atoms]
    atom_ids = jnp.arange(atoms)
    before = jnp.dot(
        (atom_ids[:, None] > atom_ids[None]).astype(jnp.float32), counts, precision=FULL
    )
    middle = (2.0 * before + counts).astype(jnp.int32)
    total = jnp.sum(counts).astype(jnp.int32)
    owner = jnp.minimum((middle * devices) // (2 * total), devices - 1)
    loads = jnp.sum(
        jnp.where(owner[None] == jnp.arange(devices)[:, None], counts[None], 0.0), axis=1
    )
    fits = jnp.max(loads) <= edges
    first_atom = jnp.sum(owner < me)
    last_atom = jnp.sum(owner <= me)
    mine = (all_live > 0) & (all_source >= first_atom) & (all_source < last_atom)
    flags = as_float(mine).reshape(-1, 128)
    tri = jnp.arange(128)
    inside = jnp.dot(flags, as_float(tri[:, None] <= tri[None]))
    row_ids = jnp.arange(flags.shape[0])
    row_sum = jnp.sum(flags, axis=1)
    offset = jnp.sum(
        jnp.where(row_ids[None] < row_ids[:, None], row_sum[None], 0.0), axis=1
    )
    rank = (inside + offset[:, None]).reshape(-1)
    slot_ids = jnp.arange(edges).astype(jnp.float32)
    index = jnp.sum((rank[None] <= slot_ids[:, None]).astype(jnp.float32), axis=1).astype(jnp.int32)
    valid = slot_ids < rank[-1]
    chosen = payload[jnp.minimum(index, devices * edges - 1)].T
    safe = jnp.asarray([1.5, 0.0, 0.0], jnp.float32)[:, None]
    my_vec = jnp.where(valid[None], chosen[:3], safe)
    my_source = jnp.where(valid, chosen[3], -1.0).astype(jnp.int32)
    my_target = jnp.where(valid, chosen[4], -1.0).astype(jnp.int32)
    my_live = as_float(valid)

    weights = (pair_in_weight, pair_out_weight, env_weight, scalar_weight, mix_weight[0], energy_head)
    slots = soap_weight.shape[0]
    kinds = jnp.arange(SPECIES, dtype=jnp.int32)[:, None]
    every_block = lax.all_gather(soap_weight, AX, axis=0, tiled=True)
    targets = 8 if is_cube(sizes) else 1
    which, where, inverse = tables(block_owner, slots, sizes)

    def views(src, tgt):
        from_atom = (src[:, None] == atom_ids[None]).astype(jnp.float32)
        to_atom = (tgt[:, None] == atom_ids[None]).astype(jnp.float32)
        spec = (species[None] == kinds).astype(jnp.float32)
        species_source = dot(spec, from_atom, ((1,), (1,)), None)
        species_target = dot(spec, to_atom, ((1,), (1,)), None)
        ends = from_atom - to_atom

        def force_to_tangent(vec_bar):
            force = sum_small(dot(vec_bar, ends, ((1,), (0,)), FULL), sizes)
            residual = force - label_all[:3]
            loss = jnp.sum(label_mask[None] * residual * residual)
            cot = 2.0 * label_mask[None] * residual / label_total
            return dot(cot, ends, ((1,), (1,)), FULL), loss

        return from_atom, species_source, species_target, force_to_tangent

    def general():
        from_atom, ss, st, force_to_tangent = views(source, target)
        blocks = every_block[inverse]

        def environ(tensor):
            sums = lax.psum(nn(tensor.reshape(-1, edges), from_atom), AX)
            return scale * nt(sums, from_atom).reshape(tensor.shape)

        matrices = to_matrices(blocks)
        out = chain(
            weights,
            lambda after: matrices,
            environ,
            force_to_tangent,
            edge_vec,
            as_float(edge_live),
            ss,
            st,
        )
        flat = to_blocks(jnp.stack(out[6]))
        per = inverse.shape[0] // targets
        place_of = which * per + where
        order = jnp.zeros_like(place_of).at[place_of].set(jnp.arange(place_of.shape[0]))
        laid = flat[order].reshape(targets, per, BS, BS)
        return out[:6] + (tuple(laid[n] for n in range(targets)), out[7])

    def pack_first(in_grad, out_grad, mix_grad, head_grad):
        rest = jnp.concatenate([mix_grad.reshape(-1), head_grad])
        rest = jnp.pad(rest, (0, -rest.shape[0] % (8 * D))).reshape(-1, D)
        return jnp.concatenate([in_grad, rest], axis=0), out_grad

    flat_rows = lambda env_grad, sc_grad: (env_grad.reshape(-1, D), sc_grad.reshape(-1, D))
    def replace(state):
        out = general()
        parts = pack_first(out[0], out[1], out[4], out[5]) + flat_rows(out[2], out[3])
        own, _ = sum_pieces(out[6], sizes, slots)
        return (jnp.asarray(False), own, lax.psum(parts, AX), out[7])

    rest_rows = 8 * (-(-(mix_weight.size + energy_head.shape[0]) // (8 * D))) + 2 * NB
    wide_rows = env_weight.shape[0] * env_weight.shape[1]
    blank = (soap_weight.shape, (rest_rows, D), (D, D), (wide_rows, D), (wide_rows, D))
    general_out = []

    def after_first(empty, every):
        state = (jnp.logical_not(fits), empty[0], tuple(empty[1:]), jnp.zeros((), jnp.float32))
        _, own, shared, loss = lax.while_loop(lambda state: state[0], replace, state)
        every, loss = lax.optimization_barrier((every, loss))
        general_out.extend((own, shared, loss))
        return every

    _, my_ss, my_st, _ = views(my_source, my_target)
    my_ends = (my_source[:, None] == atom_ids[None]).astype(jnp.bfloat16)
    my_ends = my_ends - (my_target[:, None] == atom_ids[None]).astype(jnp.bfloat16)
    labels_all = jnp.concatenate([label_all, 2.0 * label_mask[None] / label_total], axis=0)
    labels_all = jnp.pad(labels_all, ((0, 8 - labels_all.shape[0]), (0, 0)))
    add_up = lambda part: sum_small(part, sizes)
    fast = fast_chain(
        weights, every_block, inverse, targets, which, where, scale, add_up, after_first, blank, labels_all, my_ends, my_vec, my_live, my_source, my_ss, my_st
    )

    small, head_part, fast_loss, made = fast
    general_own, general_shared, general_loss = general_out
    local_sums = pack_first(small.in_grad, small.out_grad, small.mix_grad, head_part)
    local_sums = local_sums + flat_rows(small.env_grad, small.sc_grad)
    summed = lax.psum(local_sums, AX)
    loss_sum = jnp.where(fits, fast_loss, general_loss)

    own_grads, nearly = sum_pieces(tuple(made.out), sizes, slots)
    own_grads = jnp.where(fits, own_grads, general_own)
    soap = soap_update(
        (
            own_grads,
            soap_weight,
            soap_first,
            soap_second,
            soap_left,
            soap_right,
            soap_lstat,
            soap_rstat,
            soap_average,
        )
    )
    (summed, general_shared), soap = lax.optimization_barrier(((summed, general_shared), tuple(soap)))
    misc, pair_out_grad, env_grad, scalar_grad = jax.tree.map(
        lambda a, b: jnp.where(fits, a, b), summed, general_shared
    )
    pair_in_grad = misc[: 2 * NB]
    rest = misc[2 * NB :].reshape(-1)
    mix_grad = rest[: mix_weight.size].reshape(mix_weight.shape[1:])
    head_grad = rest[mix_weight.size : mix_weight.size + energy_head.shape[0]]
    env_grad = env_grad.reshape(env_weight.shape)
    scalar_grad = scalar_grad.reshape(scalar_weight.shape)
    new_pair_in = adamw(pair_in_weight, pair_in_first, pair_in_second, pair_in_grad)
    new_pair_out = adamw(pair_out_weight, pair_out_first, pair_out_second, pair_out_grad)
    new_env = adamw(env_weight, env_first, env_second, env_grad)
    new_scalar = adamw(scalar_weight, scalar_first, scalar_second, scalar_grad)
    new_mix = adamw(mix_weight, mix_first, mix_second, mix_grad[None])
    new_head = adamw(energy_head, head_first, head_second, head_grad)
    return (
        (loss_sum, label_total)
        + new_pair_in
        + new_pair_out
        + new_env
        + new_scalar
        + new_mix
        + new_head
        + tuple(soap)
    )


def solution(mesh):
    shared, split = P(), P(AX)
    column = P(None, AX)
    blocks = P(AX, None, None)
    placed = (
        (column, split, split, split, shared, column, split, shared) + (shared,) * 18 + (blocks,) * 8
    )
    return jax.shard_map(
        partial(local, (mesh.shape["irrep"], mesh.shape["edge"])),
        mesh=mesh,
        in_specs=placed,
        out_specs=(shared,) * 20 + (blocks,) * 8,
        check_vma=False,
    )
```
